256 devices in a mesh: ctx: 32 (over y, x, core), tp: 8 (over z).
Axes of the slice: x: 4, y: 4, z: 8, core: 2. Of those that a mesh axis runs over, the one named last changes fastest.
Arguments:
- concepts: bfloat16 [4096, 1024], P('ctx'), may hold values from -34 to 34
- noised: bfloat16 [4096, 1024], P('ctx'), may hold values from -6 to 6
- step_ids: int32 [4096], P('ctx'), may hold values from 1 to 99
- doc_lengths: int32 [4], replicated, may hold values from 1 to 3712, 4096 in all
- context: bfloat16 [4096, 4096], P('ctx'), may hold values from -96 to 96
- time_vec: float32 [4096], P('tp'), may hold values from -6 to 6
- w_pre: bfloat16 [1024, 4096], P(None, 'tp'), may hold values from -0.1875 to 0.1875
- w_query: bfloat16 [4096, 2048], P(None, 'tp'), may hold values from -2 to 2
- w_key: bfloat16 [4096, 2048], P(None, 'tp'), may hold values from -1 to 1
- w_value: bfloat16 [4096, 2048], P(None, 'tp'), may hold values from -0.09375 to 0.09375
- w_out: bfloat16 [2048, 4096], P('tp'), may hold values from -0.125 to 0.125
- w_post: bfloat16 [4096, 1024], P('tp'), may hold values from -0.09375 to 0.09375
Outputs:
- d_context: bfloat16 [4096, 4096], P('ctx', 'tp')
- loss: float32 [], replicated
The draws below stay inside these ranges and needn't reach their ends.
Inputs may be any that keep to these rules, and one draw needn't show every extreme that they name: `doc_lengths`: they sum to 4096; the longest is exactly 3712.
All inputs are finite; a program needn't handle non-finite values.
Results may differ from the reference program's by a relative error of at most 0.04.
Values may be sent and summed in bfloat16 or wider, within the bound.
No kernel may reach another device: no remote copies, remote signals or barrier semaphores. Data moves between devices by JAX's collectives and lax.ppermute only.
A program may use at most 128 MiB of HBM per device.

```python
import math
import jax
import jax.numpy as jnp
import numpy as np
from jax import lax

D = 4096
SD = 1024
HEADS = 16
HDIM = 128
TSTEPS = 100
NDOC = 4
N = 4096
DOC_MOST = 3712


ALIGNED = 0.9


def drawn_layout(key):
    picks = jax.random.fold_in(key, 7001)
    first_key, second_key, third_key, fourth_key = jax.random.split(picks, 4)
    query_feature = jax.random.randint(first_key, (), 0, D)
    context_feature = jax.random.randint(second_key, (), 0, D)
    chosen_head = jax.random.randint(third_key, (), 0, HEADS)
    sign_vector = (2 * jax.random.randint(fourth_key, (HDIM,), 0, 2) - 1).astype(jnp.float32)
    return (query_feature, context_feature, chosen_head, sign_vector)


def planted_weight(key, feature, chosen_head, sign_vector, strength):
    drawn = jnp.clip(jax.random.normal(key, (D, HEADS * HDIM), jnp.float32), -6.0, 6.0) * D ** (-0.5)
    row_hit = (jnp.arange(D) == feature)[:, None]
    column_hit = (jnp.arange(HEADS * HDIM) // HDIM == chosen_head)[None, :]
    pattern = jnp.tile(sign_vector, HEADS)[None, :] * strength
    return jnp.where(row_hit & column_hit, drawn + pattern, drawn)


def draw_context(key, part):
    layout = drawn_layout(key)
    key = jax.random.fold_in(key, 3)
    first_key, second_key = jax.random.split(key)
    drawn = jnp.clip(jax.random.normal(first_key, (N, D), jnp.float32), -6.0, 6.0)
    wide_column = jax.random.uniform(second_key, (N, 1), jnp.float32, -0.75 * HDIM, 0.75 * HDIM)
    chosen = (jnp.arange(D) == layout[1])[None, :]
    return jnp.where(chosen, wide_column, drawn).astype(jnp.bfloat16)


def draw_w_query(key, part):
    layout = drawn_layout(key)
    key = jax.random.fold_in(key, 5)
    return planted_weight(key, layout[0], layout[2], layout[3], 1.0).astype(jnp.bfloat16)


def draw_w_key(key, part):
    layout = drawn_layout(key)
    key = jax.random.fold_in(key, 9)
    return planted_weight(key, layout[1], layout[2], layout[3], ALIGNED * HDIM ** (-0.5)).astype(jnp.bfloat16)


def draw_concepts(key, part):
    key = jax.random.fold_in(key, 11)
    first_key, second_key = jax.random.split(key)
    place = jnp.arange(N, dtype=jnp.float32)[:, None] / N
    rough = jax.random.uniform(second_key, (N, 1), jnp.float32)
    exponent = 0.5 * place + 0.25 * rough
    values = jnp.clip(jax.random.normal(first_key, (N, SD), jnp.float32), -6.0, 6.0)
    return (values * jnp.power(10.0, exponent)).astype(jnp.bfloat16)


def place_ends(drawn, stream_key, low, high):
    dims = drawn.shape
    spot = [jax.random.randint(jax.random.fold_in(stream_key, axis), (), 0, dims[axis]) for axis in range(len(dims))]
    drawn = drawn.at[tuple(spot)].set(low)
    longest = dims.index(max(dims))
    spot[longest] = (spot[longest] + 1) % dims[longest]
    return drawn.at[tuple(spot)].set(high)


def block_levels(stream_key, extent, cuts, low, largest):
    gain = 1.0
    for axis_at, parts in cuts:
        heights = jax.random.uniform(jax.random.fold_in(jax.random.fold_in(stream_key, 6), axis_at), (parts,), jnp.float32, low / len(cuts), largest / len(cuts))
        gain = gain * jnp.repeat(jnp.exp(heights), extent[axis_at] // parts).reshape((-1,) + (1,) * (len(extent) - 1 - axis_at))
    return gain


def profile(amount, total, most, lean):
    weights = [(1 << 20) // math.isqrt(rank ** lean) + 1 for rank in range(2, amount + 1)]
    spare, given = total - most - (amount - 1), [1] * (amount - 1)
    while spare > 0:
        movable = [i for i in range(amount - 1) if given[i] < most]
        whole, remaining = sum([weights[i] for i in movable]), spare
        for i in movable:
            addition = min(most - given[i], max(1, remaining * weights[i] // whole), spare)
            given[i] = given[i] + addition
            spare = spare - addition
    return np.array([most] + given)


def ragged_sizes(own_key, count, total, most, lean):
    if count == 2:
        one = jax.random.randint(own_key, (), max(1, total - most), min(most, total - 1) + 1)
        return jnp.stack([one, total - one])
    lengths = jnp.asarray(profile(count, total, most, lean), jnp.int32)
    couples = (count - 1) // 2
    giver, receiver = lengths[1:1 + 2 * couples:2], lengths[2:2 + 2 * couples:2]
    margin = jnp.minimum(giver - 1, most - receiver)
    shifted = jax.random.randint(jax.random.fold_in(own_key, 1), (couples,), 0, 1 << 20) % (margin + 1)
    lengths = lengths.at[1:1 + 2 * couples:2].set(giver - shifted).at[2:2 + 2 * couples:2].set(receiver + shifted)
    return lengths[jax.random.permutation(jax.random.fold_in(own_key, 2), count)]


def scatter_about(stream_key, shape, deviation, reach, pieces=(), kind=jnp.bfloat16):
    array = deviation * jax.random.normal(stream_key, shape, jnp.float32)
    if pieces:
        array = array * block_levels(stream_key, shape, pieces, -0.22, 0.18)
    return jnp.clip(array, -reach, reach).astype(kind)


def setup_inputs(seed: int = 0) -> dict:
    arg_keys = jax.random.split(jax.random.key(seed), 13)
    concepts = draw_concepts(jax.random.fold_in(arg_keys[12], 71), 0)
    noised = scatter_about(arg_keys[1], (N, SD), 1.0, 6.0, ((0, 32),))
    step_ids = place_ends(jax.random.randint(arg_keys[2], (N,), 1, TSTEPS), jax.random.fold_in(arg_keys[2], 1), 1, TSTEPS - 1).astype(jnp.int32)
    doc_lengths = ragged_sizes(arg_keys[3], NDOC, N, DOC_MOST, 1).astype(jnp.int32)
    context = draw_context(jax.random.fold_in(arg_keys[12], 71), 0)
    time_vec = scatter_about(arg_keys[5], (D,), 1.0, 6.0, ((0, 8),), jnp.float32)
    w_pre = scatter_about(arg_keys[6], (SD, D), SD ** -0.5, 0.1875, ((1, 8),))
    w_query = draw_w_query(jax.random.fold_in(arg_keys[12], 71), 0)
    w_key = draw_w_key(jax.random.fold_in(arg_keys[12], 71), 0)
    w_value = scatter_about(arg_keys[9], (D, HEADS * HDIM), D ** -0.5, 0.09375, ((1, 8),))
    w_out = scatter_about(arg_keys[10], (HEADS * HDIM, D), (HEADS * HDIM) ** -0.5, 0.125, ((0, 8),))
    w_post = scatter_about(arg_keys[11], (D, SD), D ** -0.5, 0.09375, ((0, 8),))
    return dict(concepts=concepts, noised=noised, step_ids=step_ids, doc_lengths=doc_lengths, context=context, time_vec=time_vec, w_pre=w_pre, w_query=w_query, w_key=w_key, w_value=w_value, w_out=w_out, w_post=w_post)


MASKED = -1e+30
EPSILON = 1e-06

def document_tables(doc_lengths):
    doc_ends = jnp.cumsum(doc_lengths).astype(jnp.int32)
    doc_starts = (doc_ends - doc_lengths).astype(jnp.int32)
    return (doc_starts, doc_ends)

def document_index(positions, doc_ends):
    return lax.optimization_barrier(jnp.sum((positions[:, None] >= doc_ends[None, :]).astype(jnp.int32), axis=1)).astype(jnp.int32)

def noise_plan(step_ids):
    angle = 0.5 * math.pi / TSTEPS * step_ids.astype(jnp.float32)
    return (jnp.cos(angle), jnp.sin(angle))

def reference(concepts, noised, step_ids, doc_lengths, context, time_vec, w_pre, w_query, w_key, w_value, w_out, w_post):
    seq_total = concepts.shape[0]
    positions = jnp.arange(seq_total, dtype=jnp.int32)
    doc_starts, doc_ends = document_tables(doc_lengths)
    doc_ids = document_index(positions, doc_ends)
    score_scale = 1.0 / math.sqrt(HDIM)
    keep_level, noise_level = noise_plan(step_ids)
    projected = jnp.dot(noised, w_pre, preferred_element_type=jnp.float32) + noise_level[:, None] * time_vec[None, :]
    input_full = projected.astype(jnp.bfloat16)
    input_wide = input_full.astype(jnp.float32)
    normed = (input_wide * lax.rsqrt(lax.optimization_barrier(jnp.mean(input_wide * input_wide, axis=1, keepdims=True)) + EPSILON)).astype(jnp.bfloat16)
    queries = jnp.dot(normed, w_query, preferred_element_type=jnp.float32).astype(jnp.bfloat16)
    key_rows = jnp.dot(context, w_key, preferred_element_type=jnp.float32).astype(jnp.bfloat16)
    value_rows = jnp.dot(context, w_value, preferred_element_type=jnp.float32).astype(jnp.bfloat16)
    allowed = (doc_ids[None, :] == doc_ids[:, None]) & (positions[None, :] <= positions[:, None])

    def split_heads(matrix):
        return matrix.reshape(seq_total, HEADS, HDIM).transpose(1, 0, 2)

    def masked_scores(query_head, key_head):
        scores = jnp.dot(query_head, key_head.T, preferred_element_type=jnp.float32) * score_scale
        return jnp.where(allowed, scores, MASKED)

    def forward_head(operands):
        query_head, key_head, value_head = operands
        scores = masked_scores(query_head, key_head)
        row_max = lax.optimization_barrier(jnp.max(scores, axis=1))
        log_total = row_max + jnp.log(lax.optimization_barrier(jnp.sum(jnp.exp(scores - row_max[:, None]), axis=1)))
        probs = jnp.exp(scores - log_total[:, None]).astype(jnp.bfloat16)
        return (jnp.dot(probs, value_head, preferred_element_type=jnp.float32).astype(jnp.bfloat16), log_total)
    query_split = split_heads(queries)
    key_split = split_heads(key_rows)
    value_split = split_heads(value_rows)
    attended_heads, log_totals = lax.map(forward_head, (query_split, key_split, value_split))
    attended = attended_heads.transpose(1, 0, 2).reshape(seq_total, HEADS * HDIM)
    mixed = input_wide + jnp.dot(attended, w_out, preferred_element_type=jnp.float32)
    inverse = lax.rsqrt(lax.optimization_barrier(jnp.mean(mixed * mixed, axis=1)) + EPSILON)
    unit = mixed * inverse[:, None]
    prediction = jnp.dot(unit.astype(jnp.bfloat16), w_post, preferred_element_type=jnp.float32)
    targets = jnp.concatenate((concepts[1:], jnp.zeros((1, concepts.shape[1]), concepts.dtype)), axis=0).astype(jnp.float32)
    valid = jnp.logical_not(jnp.any(doc_ends[None, :] == positions[:, None] + 1, axis=1))
    weights = jnp.where(valid, 1.0 + keep_level * keep_level, 0.0).astype(jnp.float32)
    missed = prediction - targets
    weighted_missed = weights[:, None] * missed
    loss = jnp.sum(weighted_missed * missed) / (seq_total * concepts.shape[1])
    pred_grad = weighted_missed.astype(jnp.bfloat16)
    unit_grad = jnp.dot(pred_grad, w_post.T, preferred_element_type=jnp.float32)
    along = lax.optimization_barrier(jnp.mean(unit_grad * unit, axis=1))
    mixed_grad = ((unit_grad - unit * along[:, None]) * inverse[:, None]).astype(jnp.bfloat16)
    attended_grad = jnp.dot(mixed_grad, w_out.T, preferred_element_type=jnp.float32).astype(jnp.bfloat16)
    grad_split = split_heads(attended_grad)
    output_dot = lax.optimization_barrier(jnp.sum(grad_split.astype(jnp.float32) * attended_heads.astype(jnp.float32), axis=2))

    def backward_head(operands):
        query_head, key_head, value_head, grad_head, log_total, dot_row = operands
        scores = masked_scores(query_head, key_head)
        probs = jnp.exp(scores - log_total[:, None])
        value_grad = jnp.dot(probs.astype(jnp.bfloat16).T, grad_head, preferred_element_type=jnp.float32)
        prob_grad = jnp.dot(grad_head, value_head.T, preferred_element_type=jnp.float32)
        score_grad = (probs * (prob_grad - dot_row[:, None]) * score_scale).astype(jnp.bfloat16)
        key_grad = jnp.dot(score_grad.T, query_head, preferred_element_type=jnp.float32)
        return (key_grad.astype(jnp.bfloat16), value_grad.astype(jnp.bfloat16))
    key_grads, value_grads = lax.map(backward_head, (query_split, key_split, value_split, grad_split, log_totals, output_dot))
    key_merged = key_grads.transpose(1, 0, 2).reshape(seq_total, HEADS * HDIM)
    value_merged = value_grads.transpose(1, 0, 2).reshape(seq_total, HEADS * HDIM)
    d_context = jnp.dot(key_merged, w_key.T, preferred_element_type=jnp.float32) + jnp.dot(value_merged, w_value.T, preferred_element_type=jnp.float32)
    return (d_context.astype(jnp.bfloat16), loss)
```

```python
import math

import jax
import jax.numpy as jnp
from jax import lax
from jax.experimental import pallas as pl
from jax.experimental.pallas import tpu as pltpu
from jax.sharding import Mesh
from jax.sharding import PartitionSpec as P

HDIM = 128
TSTEPS = 100
MASKED = -1e30
EPSILON = 1e-06
ROWS = ("y", "x", "core")
CHIPS = ("y", "x")
SCALE = 1.0 / math.sqrt(HDIM)
PAIR = 256
GROUP = 4
F32 = jnp.float32
BF16 = jnp.bfloat16


def dot(a, b, contract=((1,), (0,))):
    return lax.dot_general(a, b, (contract, ((), ())), preferred_element_type=F32)


def spread(block, axis):
    count = lax.axis_size(axis)
    stacked = jnp.broadcast_to(block[None], (count,) + block.shape)
    return lax.all_to_all(stacked, axis, 0, 0, tiled=True)


def swap(block):
    return lax.ppermute(block, "core", [(0, 1), (1, 0)])


def to_head(left, right, core):
    first = core == 0
    mine = jnp.where(first, left, right)
    got = swap(jnp.where(first, right, left))
    return jnp.concatenate((jnp.where(first, mine, got), jnp.where(first, got, mine)), axis=0)


def to_rows(block, core):
    first = core == 0
    half = block.shape[0] // 2
    top, bottom = block[:half], block[half:]
    mine = jnp.where(first, top, bottom)
    got = swap(jnp.where(first, bottom, top))
    return jnp.concatenate((jnp.where(first, mine, got), jnp.where(first, got, mine)), axis=1)


def pieces(values):
    high = lax.reduce_precision(values, 8, 7)
    rest = values - high
    middle = lax.reduce_precision(rest, 8, 7)
    low = rest - middle
    return high.astype(BF16), middle.astype(BF16), low.astype(BF16)


def start_of(ends_ref, positions):
    start = jnp.zeros_like(positions)
    for d in range(ends_ref.shape[0]):
        start = jnp.where(positions >= ends_ref[d], ends_ref[d], start)
    return start


def forward_kernel(ends_ref, chip_ref, q_ref, kv_ref, out_ref, total_ref):
    base = chip_ref[0] * PAIR
    width = GROUP * PAIR
    query_pos = base + lax.broadcasted_iota(jnp.int32, (1, PAIR), 1)
    query_start = start_of(ends_ref, query_pos)
    floor = start_of(ends_ref, base)
    q = q_ref[...]

    def body(step, carry):
        row_max, row_total, weighted = carry
        kv = kv_ref[pl.ds(step * GROUP, GROUP)].reshape(width, 2 * HDIM)
        scores = dot(kv[:, :HDIM], q, ((1,), (1,))) * SCALE
        key_pos = step * width + lax.broadcasted_iota(jnp.int32, (width, PAIR), 0)
        scores = jnp.where((key_pos >= query_start) & (key_pos <= query_pos), scores, MASKED)
        new_max = jnp.maximum(row_max, jnp.max(scores, axis=0, keepdims=True))
        probs = jnp.exp(scores - new_max)
        fading = jnp.exp(row_max - new_max)
        row_total = row_total * fading + jnp.sum(probs, axis=0, keepdims=True)
        weighted = weighted * fading + dot(kv[:, HDIM:], probs.astype(BF16), ((0,), (0,)))
        return new_max, row_total, weighted

    row_max, row_total, weighted = lax.fori_loop(
        floor // width,
        (base + PAIR - 1) // width + 1,
        body,
        (
            jnp.full((1, PAIR), MASKED, F32),
            jnp.zeros((1, PAIR), F32),
            jnp.zeros((HDIM, PAIR), F32),
        ),
    )
    out_ref[...] = (weighted / row_total).T.astype(BF16)
    total_ref[...] = row_max + jnp.log(row_total)


def backward_kernel(ends_ref, chip_ref, kv_ref, q_ref, sent_ref, out_ref):
    base = chip_ref[0] * PAIR
    width = GROUP * PAIR
    keys, values = kv_ref[:, :HDIM], kv_ref[:, HDIM:]
    last = base + PAIR - 1
    reach = q_ref.shape[0] * PAIR
    for d in reversed(range(ends_ref.shape[0])):
        reach = jnp.where(last < ends_ref[d], ends_ref[d], reach)
    key_pos = base + lax.broadcasted_iota(jnp.int32, (PAIR, width), 0)

    def body(step, carry):
        key_grad, value_grad = carry
        chips = pl.ds(step * GROUP, GROUP)
        q = q_ref[chips].reshape(width, HDIM)
        grad = sent_ref[chips, :PAIR, :].reshape(width, HDIM)
        stats = sent_ref[chips, PAIR:, :].astype(F32)

        def row(at):
            parts = [
                stats[g, at + r : at + r + 1]
                + stats[g, at + 2 + r : at + 3 + r]
                + stats[g, at + 4 + r : at + 5 + r]
                for g in range(GROUP)
                for r in range(2)
            ]
            return jnp.concatenate(parts, axis=1)

        query_pos = step * width + lax.broadcasted_iota(jnp.int32, (1, width), 1)
        query_start = start_of(ends_ref, query_pos)
        allowed = (key_pos >= query_start) & (key_pos <= query_pos)
        scores = dot(keys, q, ((1,), (1,))) * SCALE
        probs = jnp.where(allowed, jnp.exp(scores - row(0)), 0.0)
        value_grad = value_grad + dot(probs.astype(BF16), grad)
        prob_grad = dot(values, grad, ((1,), (1,)))
        score_grad = (probs * (prob_grad - row(6)) * SCALE).astype(BF16)
        key_grad = key_grad + dot(score_grad, q)
        return key_grad, value_grad

    zero = jnp.zeros((PAIR, HDIM), F32)
    key_grad, value_grad = lax.fori_loop(
        base // width, (reach + width - 1) // width, body, (zero, zero)
    )
    out_ref[:, :HDIM] = key_grad.astype(BF16)
    out_ref[:, HDIM:] = value_grad.astype(BF16)


def context_kernel(grad_ref, key_ref, value_ref, out_ref):
    key_grad = jnp.concatenate((grad_ref[:, :HDIM], grad_ref[:, 2 * HDIM : 3 * HDIM]), axis=1)
    value_grad = jnp.concatenate((grad_ref[:, HDIM : 2 * HDIM], grad_ref[:, 3 * HDIM :]), axis=1)
    total = dot(key_grad, key_ref[...], ((1,), (1,))) + dot(value_grad, value_ref[...], ((1,), (1,)))
    out_ref[0] = total.astype(BF16)


SMEM = pl.BlockSpec(memory_space=pltpu.SMEM)
VMEM = pl.BlockSpec(memory_space=pltpu.VMEM)
PARAMS = pltpu.CompilerParams(vmem_limit_bytes=40 * 1024 * 1024)


def local(
    concepts,
    noised,
    step_ids,
    doc_lengths,
    context,
    time_vec,
    w_pre,
    w_query,
    w_key,
    w_value,
    w_out,
    w_post,
):
    rows, features = concepts.shape
    parts = lax.axis_size("tp")
    chips = lax.axis_size(CHIPS)
    core = lax.axis_index("core")
    part = lax.axis_index("tp")
    seq_total = rows * lax.axis_size(ROWS)
    share = w_post.shape[0]
    width = share * parts
    own = rows // parts
    chip = lax.axis_index(CHIPS).astype(jnp.int32)
    chip_id = chip.reshape(1)
    doc_ends = jnp.cumsum(doc_lengths).astype(jnp.int32)
    positions = lax.axis_index(ROWS) * rows + jnp.arange(rows, dtype=jnp.int32)
    angle = 0.5 * math.pi / TSTEPS * step_ids.astype(F32)
    keep_level, noise_level = jnp.cos(angle), jnp.sin(angle)

    with jax.named_scope("inputs"):
        input_part = (dot(noised, w_pre) + noise_level[:, None] * time_vec[None, :]).astype(BF16)
        input_full = lax.all_gather(input_part, "tp", axis=1, tiled=True)
    with jax.named_scope("keys_values"):
        key_rows = dot(context, w_key).astype(BF16)
        value_rows = dot(context, w_value).astype(BF16)
        own_kv = to_head(
            jnp.concatenate((key_rows[:, :HDIM], value_rows[:, :HDIM]), axis=1),
            jnp.concatenate((key_rows[:, HDIM:], value_rows[:, HDIM:]), axis=1),
            core,
        )
        all_kv = spread(own_kv, CHIPS)
    with jax.named_scope("targets"):
        count = lax.axis_size(ROWS)
        following = lax.ppermute(concepts[:1], ROWS, [(i + 1, i) for i in range(count - 1)])
        targets = jnp.concatenate((concepts[1:], following), axis=0)
        targets = lax.dynamic_slice_in_dim(targets, part * own, own, 0).astype(F32)
        valid = jnp.logical_not(jnp.any(doc_ends[None, :] == positions[:, None] + 1, axis=1))
        weights = jnp.where(valid, 1.0 + keep_level * keep_level, 0.0)
        weights = lax.dynamic_slice_in_dim(weights, part * own, own, 0)
    with jax.named_scope("queries"):
        input_wide = input_full.astype(F32)
        scale = lax.rsqrt(jnp.mean(input_wide * input_wide, axis=1, keepdims=True) + EPSILON)
        normed = (input_wide * scale).astype(BF16)
        queries = dot(normed, w_query).astype(BF16)
        query_head = to_head(queries[:, :HDIM], queries[:, HDIM:], core)
        all_queries = lax.all_gather(query_head, CHIPS, axis=0, tiled=False)
    with jax.named_scope("attention"):
        attended_head, log_total = pl.pallas_call(
            forward_kernel,
            out_shape=(
                jax.ShapeDtypeStruct((PAIR, HDIM), BF16),
                jax.ShapeDtypeStruct((1, PAIR), F32),
            ),
            in_specs=[SMEM, SMEM, VMEM, VMEM],
            out_specs=(VMEM, VMEM),
            compiler_params=PARAMS,
        )(doc_ends, chip_id, query_head, all_kv)
        attended = to_rows(attended_head, core)
    with jax.named_scope("mixed"):
        head_terms = jnp.einsum(
            "rk,ktf->trf", attended, w_out.reshape(-1, parts, share), preferred_element_type=F32
        ).astype(BF16)
        arrived = lax.all_to_all(head_terms, "tp", 0, 0, tiled=True)
        mixed = input_part.astype(F32) + jnp.sum(arrived.astype(F32), axis=0)
    with jax.named_scope("prediction"):
        squares = jnp.sum(mixed * mixed, axis=1)
        raw = dot(mixed.astype(BF16), w_post).astype(BF16)
        side = jnp.stack(pieces(squares), axis=1)
        side = jnp.pad(side, ((0, 0), (0, HDIM - 3)))
        sent = jnp.concatenate((raw, side), axis=1).reshape(parts, own, features + HDIM)
        arrived = jnp.sum(lax.all_to_all(sent, "tp", 0, 0, tiled=True).astype(F32), axis=0)
        squares = jnp.sum(arrived[:, features : features + 3], axis=1)
        inverse = lax.rsqrt(squares / width + EPSILON)
        prediction = arrived[:, :features] * inverse[:, None]
    with jax.named_scope("loss"):
        missed = prediction - targets
        weighted_missed = weights[:, None] * missed
        row_loss = jnp.sum(weighted_missed * missed, axis=1)
        pred_grad = weighted_missed.astype(BF16)
        along = jnp.sum(pred_grad.astype(F32) * prediction, axis=1) / width
        side = jnp.stack(pieces(inverse) + pieces(along) + pieces(row_loss), axis=1)
        side = jnp.pad(side, ((0, 0), (0, HDIM - 9)))
        arrived = spread(jnp.concatenate((pred_grad, side), axis=1), "tp")
        arrived = arrived.reshape(rows, features + HDIM)
        side = arrived[:, features : features + 9].astype(F32)
        inverse, along, row_loss = (jnp.sum(side[:, i : i + 3], axis=1) for i in (0, 3, 6))
        loss_part = jnp.sum(row_loss)
    with jax.named_scope("mixed_grad"):
        unit_grad = dot(arrived[:, :features], w_post, ((1,), (1,)))
        unit = mixed * inverse[:, None]
        mixed_grad = ((unit_grad - unit * along[:, None]) * inverse[:, None]).astype(BF16)
        mixed_full = spread(mixed_grad, "tp")
        attended_grad = jnp.einsum(
            "trf,ktf->rk", mixed_full, w_out.reshape(-1, parts, share), preferred_element_type=F32
        ).astype(BF16)
    with jax.named_scope("sent_grads"):
        grad_head = to_head(attended_grad[:, :HDIM], attended_grad[:, HDIM:], core)
        output_dot = jnp.sum(grad_head.astype(F32) * attended_head.astype(F32), axis=1)
        stats = [p.reshape(2, HDIM) for p in pieces(log_total)]
        stats += [p.reshape(2, HDIM) for p in pieces(output_dot)]
        last = jnp.pad(jnp.stack(pieces(loss_part)), (0, HDIM - 3)).reshape(1, HDIM)
        stats = jnp.concatenate(stats + [jnp.pad(last, ((0, 3), (0, 0)))], axis=0)
        all_grads = spread(jnp.concatenate((grad_head, stats), axis=0), CHIPS)
        loss_sum = jnp.sum(all_grads[:, PAIR + 12, :3].astype(F32))
        loss = (loss_sum + swap(loss_sum)) / (seq_total * features)
    with jax.named_scope("attention_grad"):
        kv_grad = pl.pallas_call(
            backward_kernel,
            out_shape=jax.ShapeDtypeStruct((PAIR, 2 * HDIM), BF16),
            in_specs=[SMEM, SMEM, VMEM, VMEM, VMEM],
            out_specs=VMEM,
            compiler_params=PARAMS,
        )(doc_ends, chip_id, own_kv, all_queries, all_grads)
        kv_grad = to_rows(kv_grad, core)
    with jax.named_scope("d_context"):
        terms = pl.pallas_call(
            context_kernel,
            grid=(parts,),
            out_shape=jax.ShapeDtypeStruct((parts, rows, share), BF16),
            in_specs=[
                pl.BlockSpec((rows, 4 * HDIM), lambda t: (0, 0)),
                pl.BlockSpec((share, 2 * HDIM), lambda t: (t, 0)),
                pl.BlockSpec((share, 2 * HDIM), lambda t: (t, 0)),
            ],
            out_specs=pl.BlockSpec((1, rows, share), lambda t: (t, 0, 0)),
            compiler_params=PARAMS,
        )(kv_grad, w_key, w_value)
        arrived = lax.all_to_all(terms, "tp", 0, 0, tiled=True)
        d_context = jnp.sum(arrived.astype(F32), axis=0).astype(BF16)
    return d_context, loss


def solution(mesh):
    cores = 2
    count, parts = mesh.devices.shape
    side = math.isqrt(count // cores)
    split = Mesh(mesh.devices.reshape(side, side, cores, parts), ("y", "x", "core", "tp"))
    by_rows = P(ROWS, None)
    by_columns = P(None, "tp")
    return jax.shard_map(
        local,
        mesh=split,
        in_specs=(
            by_rows,
            by_rows,
            P(ROWS),
            P(),
            by_rows,
            P("tp"),
            by_columns,
            by_columns,
            by_columns,
            by_columns,
            P("tp", None),
            P("tp", None),
        ),
        out_specs=(P(ROWS, "tp"), P()),
        check_vma=False,
    )
```

```python
import functools
import math

import jax
import jax.numpy as jnp
from jax import lax
from jax.experimental import pallas as pl
from jax.experimental.pallas import tpu as pltpu
from jax.sharding import Mesh
from jax.sharding import PartitionSpec as P

HDIM = 128
TSTEPS = 100
MASKED = -1e30
EPSILON = 1e-06
ROWS = ("y", "x", "core")
CHIPS = ("y", "x")
SCALE = 1.0 / math.sqrt(HDIM)
PAIR = 256
GROUP = 4
FOLD_POST = 32
FOLD_OUT = 8
F32 = jnp.float32
BF16 = jnp.bfloat16


def dot(a, b, contract=((1,), (0,))):
    return lax.dot_general(a, b, (contract, ((), ())), preferred_element_type=F32)


def shifted(block, axis):
    count = lax.axis_size(axis)
    routes = [[(i, (i + s) % count) for i in range(count)] for s in range(1, count)]
    return [block] + [lax.ppermute(block, axis, route) for route in routes]


def spread(block, axis):
    count = lax.axis_size(axis)
    stacked = jnp.broadcast_to(block[None], (count,) + block.shape)
    return lax.all_to_all(stacked, axis, 0, 0, tiled=True)


def swap(block):
    return lax.ppermute(block, "core", [(0, 1), (1, 0)])


def to_head(left, right, core):
    first = core == 0
    mine = jnp.where(first, left, right)
    got = swap(jnp.where(first, right, left))
    return jnp.concatenate((jnp.where(first, mine, got), jnp.where(first, got, mine)), axis=0)


def to_rows(block, core):
    first = core == 0
    half = block.shape[0] // 2
    top, bottom = block[:half], block[half:]
    mine = jnp.where(first, top, bottom)
    got = swap(jnp.where(first, bottom, top))
    return jnp.concatenate((jnp.where(first, mine, got), jnp.where(first, got, mine)), axis=1)


def pieces(values):
    high = lax.reduce_precision(values, 8, 7)
    rest = values - high
    middle = lax.reduce_precision(rest, 8, 7)
    low = rest - middle
    return high.astype(BF16), middle.astype(BF16), low.astype(BF16)


def ends_of(lengths_ref):
    ends = [lengths_ref[0]]
    for d in range(1, lengths_ref.shape[0]):
        ends.append(ends[-1] + lengths_ref[d])
    return ends


def start_of(ends, positions):
    start = jnp.zeros_like(positions)
    for end in ends:
        start = jnp.where(positions >= end, end, start)
    return start


def query_kernel(place_ref, *refs):
    *blocks, w_query_ref, w_out_ref, query_ref, cross_ref = refs
    parts = len(blocks)
    rows, share = blocks[0].shape
    query = jnp.zeros(query_ref.shape, F32)
    cross = jnp.zeros(cross_ref.shape, F32)
    squares = jnp.zeros((rows, 1), F32)
    for distance, block_ref in enumerate(blocks):
        owner = lax.rem(place_ref[0] + (parts - distance), parts)
        at = pl.ds(pl.multiple_of(owner * share, share), share)
        block = block_ref[...]
        wide = block.astype(F32)
        squares = squares + jnp.sum(wide * wide, axis=1, keepdims=True)
        query = query + dot(block, w_query_ref[at, :])
        cross = cross + dot(block, w_out_ref[:, at], ((1,), (1,)))
    scale = lax.rsqrt(squares / (share * parts) + EPSILON)
    query_ref[...] = (query * scale).astype(BF16)
    cross_ref[...] = cross


def forward_kernel(lengths_ref, place_ref, q_ref, kv_ref, out_ref, total_ref):
    ends = ends_of(lengths_ref)
    base = place_ref[1] * PAIR
    width = GROUP * PAIR
    query_pos = base + lax.broadcasted_iota(jnp.int32, (1, PAIR), 1)
    query_start = start_of(ends, query_pos)
    floor = start_of(ends, base)
    q = q_ref[...]

    def body(step, carry):
        row_max, row_total, weighted = carry
        kv = kv_ref[pl.ds(step * GROUP, GROUP)].reshape(width, 2 * HDIM)
        scores = dot(kv[:, :HDIM], q, ((1,), (1,))) * SCALE
        key_pos = step * width + lax.broadcasted_iota(jnp.int32, (width, PAIR), 0)
        scores = jnp.where((key_pos >= query_start) & (key_pos <= query_pos), scores, MASKED)
        new_max = jnp.maximum(row_max, jnp.max(scores, axis=0, keepdims=True))
        probs = jnp.exp(scores - new_max)
        fading = jnp.exp(row_max - new_max)
        row_total = row_total * fading + jnp.sum(probs, axis=0, keepdims=True)
        weighted = weighted * fading + dot(kv[:, HDIM:], probs.astype(BF16), ((0,), (0,)))
        return new_max, row_total, weighted

    row_max, row_total, weighted = lax.fori_loop(
        floor // width,
        (base + PAIR - 1) // width + 1,
        body,
        (
            jnp.full((1, PAIR), MASKED, F32),
            jnp.zeros((1, PAIR), F32),
            jnp.zeros((HDIM, PAIR), F32),
        ),
    )
    out_ref[...] = (weighted / row_total).T.astype(BF16)
    total_ref[...] = row_max + jnp.log(row_total)


def both_cores(place_ref, own_ref, other_ref, count):
    own = own_ref[:, :count, :].reshape(-1, own_ref.shape[2])
    other = other_ref[:, :count, :].reshape(-1, other_ref.shape[2])
    first = place_ref[2] == 0
    return jnp.where(first, own, other), jnp.where(first, other, own)


def raw_kernel(place_ref, attended_ref, own_ref, other_ref, input_ref, out_ref):
    parts, own, _ = out_ref.shape
    attended = attended_ref[...]
    low, high = both_cores(place_ref, own_ref, other_ref, FOLD_POST)
    half = low.shape[0]
    raw_low = (dot(attended, low, ((1,), (1,))) + input_ref[:, :half]).astype(BF16)
    raw_high = (dot(attended, high, ((1,), (1,))) + input_ref[:, half:]).astype(BF16)
    packed = jnp.concatenate([attended[own * k : own * (k + 1)] for k in range(parts)], axis=1)
    for k in range(parts):
        out_ref[k, :, :half] = raw_low[own * k : own * (k + 1)]
        out_ref[k, :, half : 2 * half] = raw_high[own * k : own * (k + 1)]
        out_ref[k, :, 2 * half :] = packed


def norm_kernel(place_ref, arrived_ref, gram_ref, attended_ref, cross_ref, input_ref, back_ref, out_ref):
    parts, own, _ = arrived_ref.shape
    features = out_ref.shape[2] - HDIM
    wide = attended_ref.shape[1]
    total = arrived_ref[0, :, :features].astype(F32)
    for k in range(1, parts):
        total = total + arrived_ref[k, :, :features].astype(F32)
    cross = cross_ref[...]
    back = jnp.zeros_like(cross)
    for k in range(parts):
        theirs = jnp.concatenate(
            [
                arrived_ref[k, :, features + wide * j : features + wide * (j + 1)]
                for j in range(parts)
            ],
            axis=0,
        )
        distance = lax.rem(place_ref[0] + (parts - k), parts)
        back = back + dot(theirs, gram_ref[distance])
    back_ref[...] = cross + back
    attended = attended_ref[...].astype(F32)
    features_in = input_ref[...].astype(F32)
    squares = jnp.sum((attended * (2.0 * cross + back)).T, axis=0, keepdims=True) + jnp.sum(
        (features_in * features_in).T, axis=0, keepdims=True
    )
    high = squares.astype(BF16)
    rest = squares - high.astype(F32)
    middle = rest.astype(BF16)
    low = (rest - middle.astype(F32)).astype(BF16)
    side = jnp.concatenate((high, middle, low, jnp.zeros((own - 3, HDIM), BF16)), axis=0)
    summed = total.astype(BF16)
    for k in range(parts):
        out_ref[k, :, :features] = summed
        out_ref[k, :, features:] = side


def loss_kernel(
    width,
    place_ref,
    arrived_ref,
    target_ref,
    weight_ref,
    own_ref,
    other_ref,
    back_ref,
    hold_ref,
    grad_ref,
    loss_ref,
):
    parts, own, _ = arrived_ref.shape
    rows, features = target_ref.shape
    side = arrived_ref[:, :, features:].astype(F32)
    squares = jnp.sum(jnp.sum(side, axis=0), axis=0, keepdims=True)
    squares = jnp.broadcast_to(squares, (rows, rows)).T[:, :1]
    inverse = lax.rsqrt(jnp.maximum(squares / width, 0.0) + EPSILON)
    prediction = arrived_ref[:, :, :features].reshape(rows, features).astype(F32) * inverse
    missed = prediction - target_ref[...].astype(F32)
    weighted_missed = weight_ref[...] * missed
    loss = jnp.sum(weighted_missed * missed, axis=1, keepdims=True)
    loss_ref[...] = jnp.sum(loss, axis=0, keepdims=True)
    pred_grad = weighted_missed.astype(BF16)
    along = jnp.sum(pred_grad.astype(F32) * prediction, axis=1, keepdims=True) / width
    low, high = both_cores(place_ref, own_ref, other_ref, FOLD_POST)
    half = low.shape[0]
    direct = dot(pred_grad[:, :half], low) + dot(pred_grad[:, half:], high)
    grad_ref[...] = (inverse * (direct - along * inverse * back_ref[...])).astype(BF16)


def backward_kernel(lengths_ref, place_ref, kv_ref, q_ref, sent_ref, out_ref):
    ends = ends_of(lengths_ref)
    chip = place_ref[1]
    base = chip * PAIR
    width = GROUP * PAIR
    keys, values = kv_ref[:, :HDIM], kv_ref[:, HDIM:]
    last = base + PAIR - 1
    reach = jnp.int32(sent_ref.shape[0] * PAIR)
    for end in reversed(ends):
        reach = jnp.where(last < end, end, reach)
    key_pos = base + lax.broadcasted_iota(jnp.int32, (PAIR, width), 0)
    here_y, here_x = chip // GROUP, lax.rem(chip, GROUP)
    sides = sent_ref.shape[0] // GROUP

    def body(step, carry):
        key_grad, value_grad = carry
        chips = pl.ds(step * GROUP, GROUP)
        away_y = lax.rem(here_y + (sides - step), sides)
        q = jnp.concatenate(
            [q_ref[away_y, lax.rem(here_x + (GROUP - k), GROUP)] for k in range(GROUP)], axis=0
        )
        grad = sent_ref[chips, :PAIR, :].reshape(width, HDIM)
        stats = sent_ref[chips, PAIR:, :].astype(F32)

        def row(at):
            parts = [
                stats[g, at + r : at + r + 1]
                + stats[g, at + 2 + r : at + 3 + r]
                + stats[g, at + 4 + r : at + 5 + r]
                for g in range(GROUP)
                for r in range(2)
            ]
            return jnp.concatenate(parts, axis=1)

        query_pos = step * width + lax.broadcasted_iota(jnp.int32, (1, width), 1)
        query_start = start_of(ends, query_pos)
        allowed = (key_pos >= query_start) & (key_pos <= query_pos)
        scores = dot(keys, q, ((1,), (1,))) * SCALE
        probs = jnp.where(allowed, jnp.exp(scores - row(0)), 0.0)
        value_grad = value_grad + dot(probs.astype(BF16), grad)
        prob_grad = dot(values, grad, ((1,), (1,)))
        score_grad = (probs * (prob_grad - row(6)) * SCALE).astype(BF16)
        key_grad = key_grad + dot(score_grad, q)
        return key_grad, value_grad

    zero = jnp.zeros((PAIR, HDIM), F32)
    key_grad, value_grad = lax.fori_loop(
        base // width, (reach + width - 1) // width, body, (zero, zero)
    )
    out_ref[:, :HDIM] = key_grad.astype(BF16)
    out_ref[:, HDIM:] = value_grad.astype(BF16)


def context_kernel(grad_ref, key_ref, value_ref, out_ref):
    key_grad = jnp.concatenate((grad_ref[:, :HDIM], grad_ref[:, 2 * HDIM : 3 * HDIM]), axis=1)
    value_grad = jnp.concatenate((grad_ref[:, HDIM : 2 * HDIM], grad_ref[:, 3 * HDIM :]), axis=1)
    total = dot(key_grad, key_ref[...], ((1,), (1,))) + dot(value_grad, value_ref[...], ((1,), (1,)))
    out_ref[0] = total.astype(BF16)


SMEM = pl.BlockSpec(memory_space=pltpu.SMEM)
VMEM = pl.BlockSpec(memory_space=pltpu.VMEM)
PARAMS = pltpu.CompilerParams(vmem_limit_bytes=40 * 1024 * 1024)


def local(
    concepts,
    noised,
    step_ids,
    doc_lengths,
    context,
    time_vec,
    w_pre,
    w_query,
    w_key,
    w_value,
    w_out,
    w_post,
):
    rows, features = concepts.shape
    parts = lax.axis_size("tp")
    chips = lax.axis_size(CHIPS)
    core = lax.axis_index("core")
    part = lax.axis_index("tp")
    seq_total = rows * lax.axis_size(ROWS)
    share = w_post.shape[0]
    own = rows // parts
    chip = lax.axis_index(CHIPS).astype(jnp.int32)
    place = jnp.stack((part, chip, core)).astype(jnp.int32)
    width = share * parts

    with jax.named_scope("fold_send"):
        slot = core * chips + chip
        post_rows = lax.dynamic_slice_in_dim(w_post, slot * FOLD_POST, FOLD_POST, 1).T
        out_rows = lax.dynamic_slice_in_dim(w_out, slot * FOLD_OUT, FOLD_OUT, 0)
        fold_blocks = shifted(
            jnp.concatenate((post_rows, out_rows.reshape(-1, share)), axis=0), "tp"
        )
    with jax.named_scope("inputs"):
        angle = 0.5 * math.pi / TSTEPS * step_ids.astype(F32)
        keep_level, noise_level = jnp.cos(angle), jnp.sin(angle)
        input_part = (dot(noised, w_pre) + noise_level[:, None] * time_vec[None, :]).astype(BF16)
        input_blocks = shifted(input_part, "tp")
        input_post = dot(input_part, w_post)
    with jax.named_scope("keys_values"):
        key_rows = dot(context, w_key).astype(BF16)
        value_rows = dot(context, w_value).astype(BF16)
        own_kv = to_head(
            jnp.concatenate((key_rows[:, :HDIM], value_rows[:, :HDIM]), axis=1),
            jnp.concatenate((key_rows[:, HDIM:], value_rows[:, HDIM:]), axis=1),
            core,
        )
        all_kv = spread(own_kv, CHIPS)
    with jax.named_scope("fold"):
        turned = [fold_blocks[-k % parts][:FOLD_POST] for k in range(parts)]
        turned = lax.dynamic_slice_in_dim(jnp.stack(turned + turned), (parts - part) % parts, parts, 0)
        post_full = turned.transpose(1, 0, 2).reshape(FOLD_POST, width)
        out_full = [b[FOLD_POST:].reshape(FOLD_OUT, width) for b in fold_blocks]
        stacked = jnp.concatenate([post_full] + out_full, axis=0)
        folded = dot(stacked, w_out, ((1,), (1,))).astype(BF16)
        own_fold = spread(folded, CHIPS)
        other_fold = swap(own_fold)
        gram = [f[:, FOLD_POST:].reshape(chips, parts, FOLD_OUT, -1) for f in (own_fold, other_fold)]
        first = core == 0
        gram = jnp.stack((jnp.where(first, gram[0], gram[1]), jnp.where(first, gram[1], gram[0])))
        gram = gram.transpose(2, 0, 1, 3, 4).reshape(parts, 2 * chips * FOLD_OUT, -1)
    with jax.named_scope("targets"):
        count = lax.axis_size(ROWS)
        following = lax.ppermute(concepts[:1], ROWS, [(i + 1, i) for i in range(count - 1)])
        targets = jnp.concatenate((concepts[1:], following), axis=0)
        positions = lax.axis_index(ROWS) * rows + jnp.arange(rows, dtype=jnp.int32)
        document_end = jnp.zeros(rows, jnp.bool_)
        end = jnp.int32(0)
        for d in range(doc_lengths.shape[0]):
            end = end + doc_lengths[d]
            document_end = document_end | (end == positions + 1)
        weights = jnp.where(document_end, 0.0, 1.0 + keep_level * keep_level)[:, None]
    with jax.named_scope("queries"):
        head_width = w_query.shape[1]
        queries, cross = pl.pallas_call(
            query_kernel,
            out_shape=(
                jax.ShapeDtypeStruct((rows, head_width), BF16),
                jax.ShapeDtypeStruct((rows, head_width), F32),
            ),
            in_specs=[SMEM] + [VMEM] * (parts + 2),
            out_specs=(VMEM, VMEM),
            compiler_params=PARAMS,
        )(place, *input_blocks, w_query, w_out)
        query_head = to_head(queries[:, :HDIM], queries[:, HDIM:], core)
        along_x = jnp.stack(shifted(query_head, "x"))
        all_queries = jnp.stack(shifted(along_x, "y"))
    with jax.named_scope("attention"):
        attended_head, log_total = pl.pallas_call(
            forward_kernel,
            out_shape=(
                jax.ShapeDtypeStruct((PAIR, HDIM), BF16),
                jax.ShapeDtypeStruct((1, PAIR), F32),
            ),
            in_specs=[SMEM, SMEM, VMEM, VMEM],
            out_specs=(VMEM, VMEM),
            compiler_params=PARAMS,
        )(doc_lengths, place, query_head, all_kv)
        attended = to_rows(attended_head, core)
    with jax.named_scope("raw"):
        sent = pl.pallas_call(
            raw_kernel,
            out_shape=jax.ShapeDtypeStruct((parts, own, features + head_width * parts), BF16),
            in_specs=[SMEM, VMEM, VMEM, VMEM, VMEM],
            out_specs=VMEM,
            compiler_params=PARAMS,
        )(place, attended, own_fold, other_fold, input_post)
        arrived = lax.all_to_all(sent, "tp", 0, 0, tiled=True)
    with jax.named_scope("norm"):
        back, sent = pl.pallas_call(
            norm_kernel,
            out_shape=(
                jax.ShapeDtypeStruct((rows, head_width), F32),
                jax.ShapeDtypeStruct((parts, own, features + HDIM), BF16),
            ),
            in_specs=[SMEM] + [VMEM] * 5,
            out_specs=(VMEM, VMEM),
            compiler_params=PARAMS,
        )(place, arrived, gram, attended, cross, input_part)
        arrived = lax.all_to_all(sent, "tp", 0, 0, tiled=True)
    with jax.named_scope("loss"):
        attended_grad, loss_part = pl.pallas_call(
            functools.partial(loss_kernel, width),
            out_shape=(
                jax.ShapeDtypeStruct((rows, head_width), BF16),
                jax.ShapeDtypeStruct((1, 1), F32),
            ),
            in_specs=[SMEM] + [VMEM] * 6 + [pl.BlockSpec(memory_space=pl.ANY)],
            out_specs=(VMEM, VMEM),
            compiler_params=PARAMS,
        )(place, arrived, targets, weights, own_fold, other_fold, back, all_queries)
    with jax.named_scope("sent_grads"):
        grad_head = to_head(attended_grad[:, :HDIM], attended_grad[:, HDIM:], core)
        output_dot = jnp.sum(grad_head.astype(F32) * attended_head.astype(F32), axis=1)
        stats = [p.reshape(2, HDIM) for p in pieces(log_total)]
        stats += [p.reshape(2, HDIM) for p in pieces(output_dot)]
        last = jnp.pad(jnp.stack(pieces(loss_part[0, 0])), (0, HDIM - 3)).reshape(1, HDIM)
        stats = jnp.concatenate(stats + [jnp.pad(last, ((0, 3), (0, 0)))], axis=0)
        all_grads = spread(jnp.concatenate((grad_head, stats), axis=0), CHIPS)
        loss_sum = jnp.sum(all_grads[:, PAIR + 12, :3].astype(F32))
        loss = (loss_sum + swap(loss_sum)) / (seq_total * features)
    with jax.named_scope("attention_grad"):
        kv_grad = pl.pallas_call(
            backward_kernel,
            out_shape=jax.ShapeDtypeStruct((PAIR, 2 * HDIM), BF16),
            in_specs=[SMEM, SMEM, VMEM, VMEM, VMEM],
            out_specs=VMEM,
            compiler_params=PARAMS,
        )(doc_lengths, place, own_kv, all_queries, all_grads)
        kv_grad = to_rows(kv_grad, core)
    with jax.named_scope("d_context"):
        terms = pl.pallas_call(
            context_kernel,
            grid=(parts,),
            out_shape=jax.ShapeDtypeStruct((parts, rows, share), BF16),
            in_specs=[
                pl.BlockSpec((rows, 4 * HDIM), lambda t: (0, 0)),
                pl.BlockSpec((share, 2 * HDIM), lambda t: (t, 0)),
                pl.BlockSpec((share, 2 * HDIM), lambda t: (t, 0)),
            ],
            out_specs=pl.BlockSpec((1, rows, share), lambda t: (t, 0, 0)),
            compiler_params=PARAMS,
        )(kv_grad, w_key, w_value)
        arrived = lax.all_to_all(terms, "tp", 0, 0, tiled=True)
        d_context = jnp.sum(arrived.astype(F32), axis=0).astype(BF16)
    return d_context, loss


def solution(mesh):
    cores = 2
    count, parts = mesh.devices.shape
    side = math.isqrt(count // cores)
    split = Mesh(mesh.devices.reshape(side, side, cores, parts), ("y", "x", "core", "tp"))
    by_rows = P(ROWS, None)
    by_columns = P(None, "tp")
    return jax.shard_map(
        local,
        mesh=split,
        in_specs=(
            by_rows,
            by_rows,
            P(ROWS),
            P(),
            by_rows,
            P("tp"),
            by_columns,
            by_columns,
            by_columns,
            by_columns,
            P("tp", None),
            P("tp", None),
        ),
        out_specs=(P(ROWS, "tp"), P()),
        check_vma=False,
    )
```

```python
import functools
import math

import jax
import jax.numpy as jnp
from jax import lax
from jax.experimental import pallas as pl
from jax.experimental.pallas import tpu as pltpu
from jax.sharding import Mesh
from jax.sharding import PartitionSpec as P

HDIM = 128
TSTEPS = 100
MASKED = -1e30
EPSILON = 1e-06
ROWS = ("y", "x", "core")
CHIPS = ("y", "x")
SCALE = 1.0 / math.sqrt(HDIM)
PAIR = 256
GROUP = 4
FOLD_POST = 32
FOLD_OUT = 8
STATS = 16
F32 = jnp.float32
BF16 = jnp.bfloat16


def dot(a, b, contract=((1,), (0,))):
    return lax.dot_general(a, b, (contract, ((), ())), preferred_element_type=F32)


def shifted(block, axis):
    count = lax.axis_size(axis)
    routes = [[(i, (i + s) % count) for i in range(count)] for s in range(1, count)]
    return [block] + [lax.ppermute(block, axis, route) for route in routes]


def returned(blocks, axis):
    count = lax.axis_size(axis)
    routes = [[(i, (i - s) % count) for i in range(count)] for s in range(count)]
    return [blocks[0]] + [lax.ppermute(blocks[s], axis, routes[s]) for s in range(1, count)]


def spread(block, axis):
    count = lax.axis_size(axis)
    stacked = jnp.broadcast_to(block[None], (count,) + block.shape)
    return lax.all_to_all(stacked, axis, 0, 0, tiled=True)


def swap(block):
    return lax.ppermute(block, "core", [(0, 1), (1, 0)])


def to_head(left, right, core):
    first = core == 0
    mine = jnp.where(first, left, right)
    got = swap(jnp.where(first, right, left))
    return jnp.concatenate((jnp.where(first, mine, got), jnp.where(first, got, mine)), axis=0)


def to_rows(block, core):
    first = core == 0
    half = block.shape[0] // 2
    top, bottom = block[:half], block[half:]
    mine = jnp.where(first, top, bottom)
    got = swap(jnp.where(first, bottom, top))
    return jnp.concatenate((jnp.where(first, mine, got), jnp.where(first, got, mine)), axis=1)


def pieces(values):
    high = values.astype(BF16)
    rest = values - high.astype(F32)
    middle = rest.astype(BF16)
    return high, middle, (rest - middle.astype(F32)).astype(BF16)


def stat_rows(*rows):
    out = []
    for row in rows:
        for piece in pieces(row):
            out += [piece[:, :HDIM].astype(F32), piece[:, HDIM:].astype(F32)]
    out.append(jnp.zeros((STATS - len(out), HDIM), F32))
    return jnp.concatenate(out, axis=0).astype(BF16)


def stat_row(block, at):
    total = block[at : at + 2] + block[at + 2 : at + 4] + block[at + 4 : at + 6]
    return jnp.concatenate((total[:1], total[1:]), axis=1)


def sine(x):
    y = x * x
    total = jnp.full_like(x, 1.0 / 6227020800.0)
    for c in (-1.0 / 39916800.0, 1.0 / 362880.0, -1.0 / 5040.0, 1.0 / 120.0, -1.0 / 6.0, 1.0):
        total = total * y + c
    return total * x


def column(row):
    return jnp.broadcast_to(row, (HDIM, HDIM)).T[:, :1]


def ends_of(lengths_ref):
    ends = [lengths_ref[0]]
    for d in range(1, lengths_ref.shape[0]):
        ends.append(ends[-1] + lengths_ref[d])
    return ends


def start_of(ends, positions):
    start = jnp.zeros_like(positions)
    for end in ends:
        start = jnp.where(positions >= end, end, start)
    return start


def send_kernel(
    place_ref, steps_ref, noised_ref, pre_ref, time_ref, post_ref, out_rows_ref, sent_ref, input_ref
):
    parts = sent_ref.shape[0]
    rows, share = input_ref.shape
    slot = place_ref[2] * place_ref[3] + place_ref[1]
    angle = (0.5 * math.pi / TSTEPS) * steps_ref[...].astype(F32)
    features = dot(noised_ref[...], pre_ref[...]) + column(sine(angle)) * time_ref[...]
    features = features.astype(BF16)
    input_ref[...] = features
    post = post_ref[...].astype(F32).T
    quarter = lax.rem(slot, HDIM // FOLD_POST)
    post_rows = post[:FOLD_POST]
    for k in range(1, HDIM // FOLD_POST):
        post_rows = jnp.where(quarter == k, post[FOLD_POST * k : FOLD_POST * (k + 1)], post_rows)
    out_rows = out_rows_ref[...].astype(F32)
    out_rows = jnp.where(lax.rem(slot, 2) == 0, out_rows[:FOLD_OUT], out_rows[FOLD_OUT:])
    out_rows = [out_rows[:, share * k : share * (k + 1)] for k in range(parts)]
    rest = jnp.concatenate([post_rows] + out_rows, axis=0).astype(BF16)
    for k in range(parts):
        sent_ref[k, :rows, :] = features
        sent_ref[k, rows:, :] = rest


def fold_kernel(gathered_ref, w_out_ref, out_ref):
    parts, _, share = gathered_ref.shape
    heads = w_out_ref.shape[0]
    rows = gathered_ref.shape[1] - FOLD_POST - FOLD_OUT * parts
    middle = rows + FOLD_POST
    direct = jnp.zeros((FOLD_POST, heads), F32)
    span = FOLD_OUT * parts
    rest = gathered_ref[:, middle:, :].reshape(parts * span, share)
    gram = [jnp.zeros((FOLD_OUT, heads), F32)] * parts
    for k in range(parts):
        weight = w_out_ref[:, share * k : share * (k + 1)]
        direct = direct + dot(gathered_ref[k, rows:middle, :], weight, ((1,), (1,)))
        product = dot(rest, weight, ((1,), (1,)))
        for b in range(parts):
            at = span * b + FOLD_OUT * k
            gram[b] = gram[b] + product[at : at + FOLD_OUT]
    folded = jnp.concatenate([direct] + gram, axis=0).astype(BF16)
    for k in range(out_ref.shape[0]):
        out_ref[k] = folded


def query_kernel(gathered_ref, w_query_ref, w_out_ref, query_ref, cross_ref):
    parts, _, share = gathered_ref.shape
    rows = query_ref.shape[0]
    query = jnp.zeros(query_ref.shape, F32)
    cross = jnp.zeros(cross_ref.shape, F32)
    squares = jnp.zeros((rows, 1), F32)
    for k in range(parts):
        at = slice(share * k, share * (k + 1))
        block = gathered_ref[k, :rows, :]
        wide = block.astype(F32)
        squares = squares + jnp.sum(wide * wide, axis=1, keepdims=True)
        query = query + dot(block, w_query_ref[at, :])
        cross = cross + dot(block, w_out_ref[:, at], ((1,), (1,)))
    scale = lax.rsqrt(squares / (share * parts) + EPSILON)
    query_ref[...] = (query * scale).astype(BF16)
    cross_ref[...] = cross


def line_positions(place_ref):
    row = place_ref[1] // GROUP
    here = lax.rem(place_ref[1], GROUP)
    chips = [row * GROUP + lax.rem(here + (GROUP - k), GROUP) for k in range(GROUP)]
    lanes = lax.broadcasted_iota(jnp.int32, (1, PAIR), 1)
    return jnp.concatenate([chip * PAIR + lanes for chip in chips], axis=1)


def key_steps(place_ref, ends):
    row = place_ref[1] // GROUP
    here = lax.rem(place_ref[1], GROUP)
    floor = start_of(ends, row * (GROUP * PAIR))
    past = jnp.maximum(floor - (here * PAIR + PAIR - 1), 0)
    lowest = (past + GROUP * PAIR - 1) // (GROUP * PAIR)
    return row - lowest + 1


def allowed_pairs(place_ref, step, query_start, query_pos):
    base = (place_ref[1] - step * GROUP) * PAIR
    key_pos = base + lax.broadcasted_iota(jnp.int32, (PAIR, query_pos.shape[1]), 0)
    return (key_pos >= query_start) & (key_pos <= query_pos)


def forward_kernel(lengths_ref, place_ref, q_ref, kv_ref, out_ref):
    ends = ends_of(lengths_ref)
    width = GROUP * PAIR
    query_pos = line_positions(place_ref)
    query_start = start_of(ends, query_pos)
    q = q_ref[...].reshape(width, HDIM)

    def body(step, carry):
        row_max, row_total, weighted = carry
        scores = dot(kv_ref[step, :, :HDIM], q, ((1,), (1,))) * SCALE
        scores = jnp.where(allowed_pairs(place_ref, step, query_start, query_pos), scores, MASKED)
        new_max = jnp.maximum(row_max, jnp.max(scores, axis=0, keepdims=True))
        probs = jnp.exp(scores - new_max)
        fading = jnp.exp(row_max - new_max)
        row_total = row_total * fading + jnp.sum(probs, axis=0, keepdims=True)
        weighted = weighted * fading + dot(kv_ref[step, :, HDIM:], probs.astype(BF16), ((0,), (0,)))
        return new_max, row_total, weighted

    row_max, row_total, weighted = lax.fori_loop(
        0,
        key_steps(place_ref, ends),
        body,
        (
            jnp.full((1, width), MASKED, F32),
            jnp.zeros((1, width), F32),
            jnp.zeros((HDIM, width), F32),
        ),
    )
    out = (weighted / row_total).T.astype(BF16)
    log_total = row_max + jnp.log(row_total)
    for k in range(GROUP):
        at = slice(PAIR * k, PAIR * (k + 1))
        out_ref[k, :PAIR, :] = out[at]
        out_ref[k, PAIR:, :] = stat_rows(log_total[:, at])


def merge_kernel(*refs):
    *part_refs, out_ref, total_ref = refs
    logs = [stat_row(ref[PAIR:, :].astype(F32), 0) for ref in part_refs]
    top = functools.reduce(jnp.maximum, logs)
    log_total = top + jnp.log(functools.reduce(jnp.add, [jnp.exp(x - top) for x in logs]))
    out = jnp.zeros((PAIR, HDIM), F32)
    for x, ref in zip(logs, part_refs):
        weight = jnp.broadcast_to(jnp.exp(x - log_total), (HDIM, PAIR)).T
        out = out + weight * ref[:PAIR, :].astype(F32)
    out_ref[...] = out.astype(BF16)
    total_ref[...] = log_total


def both_cores(place_ref, own_ref, other_ref, count):
    own = own_ref[:, :count, :].reshape(-1, own_ref.shape[2])
    other = other_ref[:, :count, :].reshape(-1, other_ref.shape[2])
    first = place_ref[2] == 0
    return jnp.where(first, own, other), jnp.where(first, other, own)


def raw_kernel(place_ref, attended_ref, own_ref, other_ref, input_ref, out_ref):
    parts, own, _ = out_ref.shape
    attended = attended_ref[...]
    low, high = both_cores(place_ref, own_ref, other_ref, FOLD_POST)
    half = low.shape[0]
    raw_low = (dot(attended, low, ((1,), (1,))) + input_ref[:, :half]).astype(BF16)
    raw_high = (dot(attended, high, ((1,), (1,))) + input_ref[:, half:]).astype(BF16)
    packed = jnp.concatenate([attended[own * k : own * (k + 1)] for k in range(parts)], axis=1)
    for k in range(parts):
        out_ref[k, :, :half] = raw_low[own * k : own * (k + 1)]
        out_ref[k, :, half : 2 * half] = raw_high[own * k : own * (k + 1)]
        out_ref[k, :, 2 * half :] = packed


def norm_kernel(
    arrived_ref, gram_ref, attended_ref, cross_ref, input_ref, back_ref, out_ref
):
    parts, own, _ = arrived_ref.shape
    features = out_ref.shape[2] - HDIM
    wide = attended_ref.shape[1]
    total = arrived_ref[0, :, :features].astype(F32)
    for k in range(1, parts):
        total = total + arrived_ref[k, :, :features].astype(F32)
    cross = cross_ref[...]
    back = jnp.zeros_like(cross)
    for k in range(parts):
        theirs = jnp.concatenate(
            [
                arrived_ref[k, :, features + wide * j : features + wide * (j + 1)]
                for j in range(parts)
            ],
            axis=0,
        )
        back = back + dot(theirs, gram_ref[k])
    back_ref[...] = cross + back
    attended = attended_ref[...].astype(F32)
    features_in = input_ref[...].astype(F32)
    squares = jnp.sum((attended * (2.0 * cross + back)).T, axis=0, keepdims=True) + jnp.sum(
        (features_in * features_in).T, axis=0, keepdims=True
    )
    side = jnp.concatenate(pieces(squares) + (jnp.zeros((own - 3, HDIM), BF16),), axis=0)
    summed = total.astype(BF16)
    for k in range(parts):
        out_ref[k, :, :features] = summed
        out_ref[k, :, features:] = side


def loss_kernel(
    width,
    lengths_ref,
    place_ref,
    steps_ref,
    arrived_ref,
    target_ref,
    own_ref,
    other_ref,
    back_ref,
    grad_ref,
    loss_ref,
):
    parts, own, _ = arrived_ref.shape
    rows, features = target_ref.shape
    position = (place_ref[1] * 2 + place_ref[2]) * rows
    position = position + lax.broadcasted_iota(jnp.int32, (1, rows), 1)
    angle = (0.5 * math.pi / TSTEPS) * steps_ref[...].astype(F32)
    keep_level = sine(0.5 * math.pi - angle)
    weight = 1.0 + keep_level * keep_level
    for end in ends_of(lengths_ref):
        weight = jnp.where(position + 1 == end, 0.0, weight)
    side = arrived_ref[:, :, features:].astype(F32)
    squares = jnp.sum(jnp.sum(side, axis=0), axis=0, keepdims=True)
    inverse = column(lax.rsqrt(jnp.maximum(squares / width, 0.0) + EPSILON))
    prediction = arrived_ref[:, :, :features].reshape(rows, features).astype(F32) * inverse
    missed = prediction - target_ref[...].astype(F32)
    weighted_missed = column(weight) * missed
    loss = jnp.sum(weighted_missed * missed, axis=1, keepdims=True)
    loss_ref[...] = jnp.broadcast_to(jnp.sum(loss, axis=0, keepdims=True), (1, HDIM))
    pred_grad = weighted_missed.astype(BF16)
    along = jnp.sum(pred_grad.astype(F32) * prediction, axis=1, keepdims=True) / width
    low, high = both_cores(place_ref, own_ref, other_ref, FOLD_POST)
    half = low.shape[0]
    direct = dot(pred_grad[:, :half], low) + dot(pred_grad[:, half:], high)
    grad_ref[...] = (inverse * (direct - along * inverse * back_ref[...])).astype(BF16)


def sent_kernel(grad_ref, attended_ref, total_ref, loss_ref, out_ref):
    grad = grad_ref[...]
    product = grad.astype(F32) * attended_ref[...].astype(F32)
    output_dot = jnp.sum(product.T, axis=0, keepdims=True)
    stats = stat_rows(total_ref[...], output_dot).astype(F32)
    loss_rows = [p.astype(F32) for p in pieces(loss_ref[...])]
    stats = jnp.concatenate([stats[:12]] + loss_rows + [stats[15:]], axis=0)
    out_ref[:PAIR, :] = grad
    out_ref[PAIR:, :] = stats.astype(BF16)


def backward_kernel(lengths_ref, place_ref, kv_ref, q_ref, *refs):
    *sent_refs, out_ref = refs
    ends = ends_of(lengths_ref)
    width = GROUP * PAIR
    query_pos = line_positions(place_ref)
    query_start = start_of(ends, query_pos)
    q = q_ref[...].reshape(width, HDIM)
    grad = jnp.concatenate([ref[:PAIR, :] for ref in sent_refs], axis=0)
    stats = [ref[PAIR:, :].astype(F32) for ref in sent_refs]
    log_total = jnp.concatenate([stat_row(x, 0) for x in stats], axis=1)
    output_dot = jnp.concatenate([stat_row(x, 6) for x in stats], axis=1)
    loss = functools.reduce(jnp.add, [x[12:13] + x[13:14] + x[14:15] for x in stats])
    tail = jnp.concatenate(
        [p.astype(F32) for p in pieces(loss)] + [jnp.zeros((STATS - 3, HDIM), F32)], axis=0
    )
    tail = jnp.concatenate((tail, tail), axis=1).astype(BF16)
    steps = key_steps(place_ref, ends)
    for step in range(out_ref.shape[0]):
        out_ref[step, PAIR:, :] = tail

        @pl.when(step < steps)
        def _():
            allowed = allowed_pairs(place_ref, step, query_start, query_pos)
            scores = dot(kv_ref[step, :, :HDIM], q, ((1,), (1,))) * SCALE
            probs = jnp.where(allowed, jnp.exp(scores - log_total), 0.0)
            out_ref[step, :PAIR, HDIM:] = dot(probs.astype(BF16), grad).astype(BF16)
            prob_grad = dot(kv_ref[step, :, HDIM:], grad, ((1,), (1,)))
            score_grad = (probs * (prob_grad - output_dot) * SCALE).astype(BF16)
            out_ref[step, :PAIR, :HDIM] = dot(score_grad, q).astype(BF16)

        @pl.when(step >= steps)
        def _():
            out_ref[step, :PAIR, :] = jnp.zeros((PAIR, 2 * HDIM), BF16)


def collect_kernel(*refs):
    *part_refs, out_ref, loss_ref = refs
    total = functools.reduce(jnp.add, [ref[...].astype(F32) for ref in part_refs])
    out_ref[...] = total[:PAIR].astype(BF16)
    rows = total[PAIR : PAIR + 3, :HDIM]
    loss_ref[...] = jnp.sum(rows, axis=0, keepdims=True)


def context_kernel(grad_ref, key_ref, value_ref, out_ref):
    key_grad = jnp.concatenate((grad_ref[:, :HDIM], grad_ref[:, 2 * HDIM : 3 * HDIM]), axis=1)
    value_grad = jnp.concatenate((grad_ref[:, HDIM : 2 * HDIM], grad_ref[:, 3 * HDIM :]), axis=1)
    total = dot(key_grad, key_ref[...], ((1,), (1,))) + dot(value_grad, value_ref[...], ((1,), (1,)))
    out_ref[0] = total.astype(BF16)


SMEM = pl.BlockSpec(memory_space=pltpu.SMEM)
VMEM = pl.BlockSpec(memory_space=pltpu.VMEM)
PARAMS = pltpu.CompilerParams(vmem_limit_bytes=20 * 1024 * 1024)


def local(
    concepts,
    noised,
    step_ids,
    doc_lengths,
    context,
    time_vec,
    w_pre,
    w_query,
    w_key,
    w_value,
    w_out,
    w_post,
):
    rows, features = concepts.shape
    parts = lax.axis_size("tp")
    chips = lax.axis_size(CHIPS)
    core = lax.axis_index("core")
    part = lax.axis_index("tp")
    seq_total = rows * lax.axis_size(ROWS)
    share = w_post.shape[0]
    own = rows // parts
    chip = lax.axis_index(CHIPS)
    place = jnp.stack((part, chip, core, chips)).astype(jnp.int32)
    width = share * parts
    head_width = w_out.shape[0]
    fold_rows = FOLD_POST + FOLD_OUT * parts
    steps = step_ids.reshape(1, rows)

    with jax.named_scope("inputs"):
        sent, input_part = pl.pallas_call(
            send_kernel,
            out_shape=(
                jax.ShapeDtypeStruct((parts, rows + fold_rows, share), BF16),
                jax.ShapeDtypeStruct((rows, share), BF16),
            ),
            grid_spec=pltpu.PrefetchScalarGridSpec(
                num_scalar_prefetch=1,
                grid=(1,),
                in_specs=[
                    pl.BlockSpec((1, rows), lambda i, p: (0, 0)),
                    pl.BlockSpec((rows, features), lambda i, p: (0, 0)),
                    pl.BlockSpec((features, share), lambda i, p: (0, 0)),
                    pl.BlockSpec((1, share), lambda i, p: (0, 0)),
                    pl.BlockSpec(
                        (share, HDIM),
                        lambda i, p: (0, (p[2] * p[3] + p[1]) // (HDIM // FOLD_POST)),
                    ),
                    pl.BlockSpec((2 * FOLD_OUT, width), lambda i, p: ((p[2] * p[3] + p[1]) // 2, 0)),
                ],
                out_specs=(
                    pl.BlockSpec((parts, rows + fold_rows, share), lambda i, p: (0, 0, 0)),
                    pl.BlockSpec((rows, share), lambda i, p: (0, 0)),
                ),
            ),
            compiler_params=PARAMS,
        )(place, steps, noised, w_pre, time_vec.reshape(1, share), w_post, w_out)
        gathered = lax.all_to_all(sent, "tp", 0, 0, tiled=True)
        input_post = dot(input_part, w_post)
    with jax.named_scope("keys_values"):
        key_rows = dot(context, w_key).astype(BF16)
        value_rows = dot(context, w_value).astype(BF16)
        own_kv = to_head(
            jnp.concatenate((key_rows[:, :HDIM], value_rows[:, :HDIM]), axis=1),
            jnp.concatenate((key_rows[:, HDIM:], value_rows[:, HDIM:]), axis=1),
            core,
        )
        all_kv = jnp.stack(shifted(own_kv, "y"))
    with jax.named_scope("fold"):
        folded = pl.pallas_call(
            fold_kernel,
            out_shape=jax.ShapeDtypeStruct((chips, fold_rows, head_width), BF16),
            in_specs=[VMEM, VMEM],
            out_specs=VMEM,
            compiler_params=PARAMS,
        )(gathered, w_out)
        own_fold = lax.all_to_all(folded, CHIPS, 0, 0, tiled=True)
        other_fold = swap(own_fold)
        gram = [f[:, FOLD_POST:].reshape(chips, parts, FOLD_OUT, -1) for f in (own_fold, other_fold)]
        first = core == 0
        gram = jnp.stack((jnp.where(first, gram[0], gram[1]), jnp.where(first, gram[1], gram[0])))
        gram = gram.transpose(2, 0, 1, 3, 4).reshape(parts, 2 * chips * FOLD_OUT, -1)
    with jax.named_scope("targets"):
        count = lax.axis_size(ROWS)
        following = lax.ppermute(concepts[:1], ROWS, [(i + 1, i) for i in range(count - 1)])
        targets = jnp.concatenate((concepts[1:], following), axis=0)
    with jax.named_scope("queries"):
        queries, cross = pl.pallas_call(
            query_kernel,
            out_shape=(
                jax.ShapeDtypeStruct((rows, head_width), BF16),
                jax.ShapeDtypeStruct((rows, head_width), F32),
            ),
            in_specs=[VMEM, VMEM, VMEM],
            out_specs=(VMEM, VMEM),
            compiler_params=PARAMS,
        )(gathered, w_query, w_out)
        query_head = to_head(queries[:, :HDIM], queries[:, HDIM:], core)
        line_queries = jnp.stack(shifted(query_head, "x"))
    with jax.named_scope("attention"):
        sent = pl.pallas_call(
            forward_kernel,
            out_shape=jax.ShapeDtypeStruct((GROUP, PAIR + STATS, HDIM), BF16),
            in_specs=[SMEM, SMEM, VMEM, VMEM],
            out_specs=VMEM,
            compiler_params=PARAMS,
        )(doc_lengths, place, line_queries, all_kv)
        attended_head, log_total = pl.pallas_call(
            merge_kernel,
            out_shape=(
                jax.ShapeDtypeStruct((PAIR, HDIM), BF16),
                jax.ShapeDtypeStruct((1, PAIR), F32),
            ),
            in_specs=[VMEM] * GROUP,
            out_specs=(VMEM, VMEM),
            compiler_params=PARAMS,
        )(*returned(sent, "x"))
        attended = to_rows(attended_head, core)
    with jax.named_scope("raw"):
        sent = pl.pallas_call(
            raw_kernel,
            out_shape=jax.ShapeDtypeStruct((parts, own, features + head_width * parts), BF16),
            in_specs=[SMEM, VMEM, VMEM, VMEM, VMEM],
            out_specs=VMEM,
            compiler_params=PARAMS,
        )(place, attended, own_fold, other_fold, input_post)
        arrived = lax.all_to_all(sent, "tp", 0, 0, tiled=True)
    with jax.named_scope("norm"):
        back, sent = pl.pallas_call(
            norm_kernel,
            out_shape=(
                jax.ShapeDtypeStruct((rows, head_width), F32),
                jax.ShapeDtypeStruct((parts, own, features + HDIM), BF16),
            ),
            in_specs=[VMEM] * 5,
            out_specs=(VMEM, VMEM),
            compiler_params=PARAMS,
        )(arrived, gram, attended, cross, input_part)
        arrived = lax.all_to_all(sent, "tp", 0, 0, tiled=True)
    with jax.named_scope("loss"):
        attended_grad, loss_part = pl.pallas_call(
            functools.partial(loss_kernel, width),
            out_shape=(
                jax.ShapeDtypeStruct((rows, head_width), BF16),
                jax.ShapeDtypeStruct((1, HDIM), F32),
            ),
            in_specs=[SMEM, SMEM] + [VMEM] * 6,
            out_specs=(VMEM, VMEM),
            compiler_params=PARAMS,
        )(doc_lengths, place, steps, arrived, targets, own_fold, other_fold, back)
    with jax.named_scope("sent_grads"):
        grad_head = to_head(attended_grad[:, :HDIM], attended_grad[:, HDIM:], core)
        sent = pl.pallas_call(
            sent_kernel,
            out_shape=jax.ShapeDtypeStruct((PAIR + STATS, HDIM), BF16),
            in_specs=[VMEM] * 4,
            out_specs=VMEM,
            compiler_params=PARAMS,
        )(grad_head, attended_head, log_total, loss_part)
        line_grads = shifted(sent, "x")
    with jax.named_scope("attention_grad"):
        sent = pl.pallas_call(
            backward_kernel,
            out_shape=jax.ShapeDtypeStruct((chips // GROUP, PAIR + STATS, 2 * HDIM), BF16),
            in_specs=[SMEM, SMEM] + [VMEM] * (2 + GROUP),
            out_specs=VMEM,
            compiler_params=PARAMS,
        )(doc_lengths, place, all_kv, line_queries, *line_grads)
        kv_grad, loss_part = pl.pallas_call(
            collect_kernel,
            out_shape=(
                jax.ShapeDtypeStruct((PAIR, 2 * HDIM), BF16),
                jax.ShapeDtypeStruct((1, HDIM), F32),
            ),
            in_specs=[VMEM] * (chips // GROUP),
            out_specs=(VMEM, VMEM),
            compiler_params=PARAMS,
        )(*returned(sent, "y"))
        kv_grad = to_rows(kv_grad, core)
        loss_part = loss_part[0, 0]
        loss = (loss_part + swap(loss_part)) / (seq_total * features)
    with jax.named_scope("d_context"):
        terms = pl.pallas_call(
            context_kernel,
            grid=(parts,),
            out_shape=jax.ShapeDtypeStruct((parts, rows, share), BF16),
            in_specs=[
                pl.BlockSpec((rows, 4 * HDIM), lambda t: (0, 0)),
                pl.BlockSpec((share, 2 * HDIM), lambda t: (t, 0)),
                pl.BlockSpec((share, 2 * HDIM), lambda t: (t, 0)),
            ],
            out_specs=pl.BlockSpec((1, rows, share), lambda t: (t, 0, 0)),
            compiler_params=PARAMS,
        )(kv_grad, w_key, w_value)
        arrived = lax.all_to_all(terms, "tp", 0, 0, tiled=True)
        d_context = jnp.sum(arrived.astype(F32), axis=0).astype(BF16)
    return d_context, loss


def solution(mesh):
    cores = 2
    count, parts = mesh.devices.shape
    side = math.isqrt(count // cores)
    split = Mesh(mesh.devices.reshape(side, side, cores, parts), ("y", "x", "core", "tp"))
    by_rows = P(ROWS, None)
    by_columns = P(None, "tp")
    return jax.shard_map(
        local,
        mesh=split,
        in_specs=(
            by_rows,
            by_rows,
            P(ROWS),
            P(),
            by_rows,
            P("tp"),
            by_columns,
            by_columns,
            by_columns,
            by_columns,
            P("tp", None),
            P("tp", None),
        ),
        out_specs=(P(ROWS, "tp"), P()),
        check_vma=False,
    )
```

```python
import functools
import math

import jax
import jax.numpy as jnp
from jax import lax
from jax.experimental import pallas as pl
from jax.experimental.pallas import tpu as pltpu
from jax.sharding import Mesh
from jax.sharding import PartitionSpec as P

HDIM = 128
TSTEPS = 100
MASKED = -1e30
EPSILON = 1e-06
ROWS = ("y", "x", "core")
CHIPS = ("y", "x")
SCALE = 1.0 / math.sqrt(HDIM)
PAIR = 256
GROUP = 4
FOLD_POST = 32
FOLD_OUT = 8
STATS = 16
F32 = jnp.float32
BF16 = jnp.bfloat16


def dot(a, b, contract=((1,), (0,))):
    return lax.dot_general(a, b, (contract, ((), ())), preferred_element_type=F32)


def shifted(block, axis):
    count = lax.axis_size(axis)
    routes = [[(i, (i + s) % count) for i in range(count)] for s in range(1, count)]
    return [block] + [lax.ppermute(block, axis, route) for route in routes]


def returned(blocks, axis):
    count = lax.axis_size(axis)
    routes = [[(i, (i - s) % count) for i in range(count)] for s in range(count)]
    return [blocks[0]] + [lax.ppermute(blocks[s], axis, routes[s]) for s in range(1, count)]


def around(block, axis):
    count = lax.axis_size(axis)
    up = [(i, (i + 1) % count) for i in range(count)]
    down = [(i, (i - 1) % count) for i in range(count)]
    behind, ahead = [block], [block]
    for _ in range(count // 2 - 1):
        behind.append(lax.ppermute(behind[-1], axis, up))
        ahead.append(lax.ppermute(ahead[-1], axis, down))
    half = block.shape[0] // 2
    far = [lax.ppermute(behind[-1][:half], axis, up), lax.ppermute(ahead[-1][half:], axis, down)]
    return behind + far + ahead[:0:-1]


def gathered_blocks(refs):
    half = (len(refs) - 1) // 2
    far = jnp.concatenate((refs[half][...], refs[half + 1][...]), axis=0)
    return [r[...] for r in refs[:half]] + [far] + [r[...] for r in refs[half + 2 :]]


def owner_of(place_ref, distance, parts):
    return lax.rem(place_ref[0] + (parts - distance), parts)


def swap(block):
    return lax.ppermute(block, "core", [(0, 1), (1, 0)])


def to_head(mine, theirs, core):
    first = core == 0
    got = swap(theirs)
    return jnp.concatenate((jnp.where(first, mine, got), jnp.where(first, got, mine)), axis=0)


def to_rows(block, core):
    first = core == 0
    half = block.shape[0] // 2
    top, bottom = block[:half], block[half:]
    mine = jnp.where(first, top, bottom)
    got = swap(jnp.where(first, bottom, top))
    return jnp.concatenate((jnp.where(first, mine, got), jnp.where(first, got, mine)), axis=1)


def pieces(values):
    high = values.astype(BF16)
    rest = values - high.astype(F32)
    middle = rest.astype(BF16)
    return high, middle, (rest - middle.astype(F32)).astype(BF16)


def stat_rows(*rows):
    out = []
    for row in rows:
        for piece in pieces(row):
            out += [piece[:, :HDIM].astype(F32), piece[:, HDIM:].astype(F32)]
    out.append(jnp.zeros((STATS - len(out), HDIM), F32))
    return jnp.concatenate(out, axis=0).astype(BF16)


def stat_row(block, at):
    total = block[at : at + 2] + block[at + 2 : at + 4] + block[at + 4 : at + 6]
    return jnp.concatenate((total[:1], total[1:]), axis=1)


def sine(x):
    y = x * x
    total = jnp.full_like(x, 1.0 / 6227020800.0)
    for c in (-1.0 / 39916800.0, 1.0 / 362880.0, -1.0 / 5040.0, 1.0 / 120.0, -1.0 / 6.0, 1.0):
        total = total * y + c
    return total * x


def column(row):
    return jnp.broadcast_to(row, (HDIM, HDIM)).T[:, :1]


def ends_of(lengths_ref):
    ends = [lengths_ref[0]]
    for d in range(1, lengths_ref.shape[0]):
        ends.append(ends[-1] + lengths_ref[d])
    return ends


def start_of(ends, positions):
    start = jnp.zeros_like(positions)
    for end in ends:
        start = jnp.where(positions >= end, end, start)
    return start


def fetch(pairs, sems):
    copies = [pltpu.make_async_copy(f, t, sems.at[i]) for i, (f, t) in enumerate(pairs)]
    for copy in copies:
        copy.start()
    return copies


def send_kernel(
    place_ref,
    steps_ref,
    time_ref,
    noised_ref,
    pre_ref,
    post_ref,
    out_ref,
    sent_ref,
    noised,
    pre,
    post_part,
    out_part,
    sems,
):
    rows, features = noised.shape
    share = pre.shape[1]
    slot = place_ref[2] * place_ref[3] + place_ref[1]
    lanes = pl.ds(pl.multiple_of(slot // (HDIM // FOLD_POST) * HDIM, HDIM), HDIM)
    lines = pl.ds(pl.multiple_of(slot // 2 * (2 * FOLD_OUT), 2 * FOLD_OUT), 2 * FOLD_OUT)
    half = features // 2
    copies = fetch(
        (
            (noised_ref, noised),
            (pre_ref.at[:half], pre.at[:half]),
            (pre_ref.at[half:], pre.at[half:]),
            (post_ref.at[:, lanes], post_part),
            (out_ref.at[lines], out_part),
        ),
        sems,
    )
    angle = (0.5 * math.pi / TSTEPS) * steps_ref[...].astype(F32)
    noise = column(sine(angle)) * time_ref[...]
    copies[3].wait()
    post = post_part[...].astype(F32).T
    quarter = lax.rem(slot, HDIM // FOLD_POST)
    post_rows = post[:FOLD_POST]
    for k in range(1, HDIM // FOLD_POST):
        post_rows = jnp.where(quarter == k, post[FOLD_POST * k : FOLD_POST * (k + 1)], post_rows)
    copies[4].wait()
    out_rows = out_part[...].astype(F32)
    out_rows = jnp.where(lax.rem(slot, 2) == 0, out_rows[:FOLD_OUT], out_rows[FOLD_OUT:])
    parts = out_rows.shape[1] // share
    out_rows = [out_rows[:, share * k : share * (k + 1)] for k in range(parts)]
    sent_ref[rows:, :] = jnp.concatenate([post_rows] + out_rows, axis=0).astype(BF16)
    for k in range(3):
        copies[k].wait()
    sent_ref[:rows, :] = (dot(noised[...], pre[...]) + noise).astype(BF16)


def project_kernel(
    place_ref, context_ref, key_ref, value_ref, mine_ref, theirs_ref, context, weight, sems
):
    parts = 4
    share = context.shape[1] // parts
    pairs = []
    for k in range(parts):
        at = pl.ds(share * k, share)
        pairs.append((context_ref.at[:, at], context.at[:, at]))
        pairs.append((key_ref.at[at], weight.at[0, at]))
        pairs.append((value_ref.at[at], weight.at[1, at]))
    copies = fetch(pairs, sems)
    keys = jnp.zeros((context.shape[0], 2 * HDIM), F32)
    values = keys
    for k in range(parts):
        at = slice(share * k, share * (k + 1))
        for copy in copies[3 * k : 3 * k + 3]:
            copy.wait()
        keys = keys + dot(context[:, at], weight[0, at])
        values = values + dot(context[:, at], weight[1, at])
    left = jnp.concatenate((keys[:, :HDIM], values[:, :HDIM]), axis=1)
    right = jnp.concatenate((keys[:, HDIM:], values[:, HDIM:]), axis=1)
    first = place_ref[2] == 0
    mine_ref[...] = jnp.where(first, left, right).astype(BF16)
    theirs_ref[...] = jnp.where(first, right, left).astype(BF16)


def fold_kernel(place_ref, w_out_ref, *refs):
    *block_refs, out_ref, weight, sems = refs
    heads, width = weight.shape
    blocks = gathered_blocks(block_refs)
    parts = len(blocks)
    share = blocks[0].shape[1]
    half = heads // 2
    copies = fetch(
        [(w_out_ref.at[pl.ds(half * k, half)], weight.at[pl.ds(half * k, half)]) for k in range(2)],
        sems,
    )
    span = FOLD_OUT * parts
    rest = blocks[0].shape[0] - span
    top = rest - FOLD_POST
    for copy in copies:
        copy.wait()
    direct = jnp.zeros((FOLD_POST, heads), F32)
    for distance, block in enumerate(blocks):
        owner = owner_of(place_ref, distance, parts)
        at = pl.ds(pl.multiple_of(owner * share, share), share)
        direct = direct + dot(block[top:rest], weight[:, at], ((1,), (1,)))
    rows = jnp.concatenate([block[rest:] for block in blocks], axis=0)
    gram = [jnp.zeros((FOLD_OUT, heads), F32)] * parts
    for k in range(parts):
        product = dot(rows, weight[:, share * k : share * (k + 1)], ((1,), (1,)))
        for b in range(parts):
            at = span * b + FOLD_OUT * k
            gram[b] = gram[b] + product[at : at + FOLD_OUT]
    folded = jnp.concatenate([direct] + gram, axis=0).astype(BF16)
    for k in range(out_ref.shape[0]):
        out_ref[k] = folded


def query_kernel(place_ref, w_query_ref, hold_ref, wait_ref, *refs):
    *block_refs, mine_ref, theirs_ref, weight, sems = refs
    rows = mine_ref.shape[0]
    parts, share, _ = weight.shape
    copies = []
    for distance in range(parts):
        owner = owner_of(place_ref, distance, parts)
        at = pl.ds(pl.multiple_of(owner * share, share), share)
        copies.append(
            pltpu.make_async_copy(w_query_ref.at[at], weight.at[distance], sems.at[distance])
        )
        copies[-1].start()
    blocks = gathered_blocks(block_refs)
    query = jnp.zeros((rows, weight.shape[2]), F32)
    squares = jnp.zeros((rows, 1), F32)
    for distance, block in enumerate(blocks):
        wide = block[:rows].astype(F32)
        squares = squares + jnp.sum(wide * wide, axis=1, keepdims=True)
    for distance, block in enumerate(blocks):
        copies[distance].wait()
        query = query + dot(block[:rows], weight[distance])
    query = (query * lax.rsqrt(squares / (share * parts) + EPSILON)).astype(BF16)
    first = place_ref[2] == 0
    mine_ref[...] = jnp.where(first, query[:, :HDIM], query[:, HDIM:])
    theirs_ref[...] = jnp.where(first, query[:, HDIM:], query[:, :HDIM])


def cross_kernel(place_ref, w_out_ref, *refs):
    *block_refs, out_ref = refs
    blocks = gathered_blocks(block_refs)
    parts = len(blocks)
    share = blocks[0].shape[1]
    rows, heads = out_ref.shape
    cross = jnp.zeros((rows, heads), F32)
    for distance, block in enumerate(blocks):
        owner = owner_of(place_ref, distance, parts)
        at = pl.ds(pl.multiple_of(owner * share, share), share)
        cross = cross + dot(block[:rows], w_out_ref[:, at], ((1,), (1,)))
    out_ref[...] = cross


def line_positions(place_ref):
    row = place_ref[1] // GROUP
    here = lax.rem(place_ref[1], GROUP)
    chips = [row * GROUP + lax.rem(here + (GROUP - k), GROUP) for k in range(GROUP)]
    lanes = lax.broadcasted_iota(jnp.int32, (1, PAIR), 1)
    return jnp.concatenate([chip * PAIR + lanes for chip in chips], axis=1)


def key_steps(place_ref, ends):
    row = place_ref[1] // GROUP
    here = lax.rem(place_ref[1], GROUP)
    floor = start_of(ends, row * (GROUP * PAIR))
    past = jnp.maximum(floor - (here * PAIR + PAIR - 1), 0)
    lowest = (past + GROUP * PAIR - 1) // (GROUP * PAIR)
    return row - lowest + 1


def allowed_pairs(place_ref, step, query_start, query_pos):
    base = (place_ref[1] - step * GROUP) * PAIR
    key_pos = base + lax.broadcasted_iota(jnp.int32, (PAIR, query_pos.shape[1]), 0)
    return (key_pos >= query_start) & (key_pos <= query_pos)


def forward_kernel(lengths_ref, place_ref, q_ref, kv_ref, out_ref):
    ends = ends_of(lengths_ref)
    width = GROUP * PAIR
    query_pos = line_positions(place_ref)
    query_start = start_of(ends, query_pos)
    q = q_ref[...].reshape(width, HDIM)

    def body(step, carry):
        row_max, row_total, weighted = carry
        scores = dot(kv_ref[step, :, :HDIM], q, ((1,), (1,))) * SCALE
        scores = jnp.where(allowed_pairs(place_ref, step, query_start, query_pos), scores, MASKED)
        new_max = jnp.maximum(row_max, jnp.max(scores, axis=0, keepdims=True))
        probs = jnp.exp(scores - new_max)
        fading = jnp.exp(row_max - new_max)
        row_total = row_total * fading + jnp.sum(probs, axis=0, keepdims=True)
        weighted = weighted * fading + dot(kv_ref[step, :, HDIM:], probs.astype(BF16), ((0,), (0,)))
        return new_max, row_total, weighted

    row_max, row_total, weighted = lax.fori_loop(
        0,
        key_steps(place_ref, ends),
        body,
        (
            jnp.full((1, width), MASKED, F32),
            jnp.zeros((1, width), F32),
            jnp.zeros((HDIM, width), F32),
        ),
    )
    out = (weighted / row_total).T.astype(BF16)
    log_total = row_max + jnp.log(row_total)
    for k in range(GROUP):
        at = slice(PAIR * k, PAIR * (k + 1))
        out_ref[k, :PAIR, :] = out[at]
        out_ref[k, PAIR:, :] = stat_rows(log_total[:, at])


def merge_kernel(*refs):
    *part_refs, out_ref, total_ref = refs
    logs = [stat_row(ref[PAIR:, :].astype(F32), 0) for ref in part_refs]
    top = functools.reduce(jnp.maximum, logs)
    log_total = top + jnp.log(functools.reduce(jnp.add, [jnp.exp(x - top) for x in logs]))
    out = jnp.zeros((PAIR, HDIM), F32)
    for x, ref in zip(logs, part_refs):
        weight = jnp.broadcast_to(jnp.exp(x - log_total), (HDIM, PAIR)).T
        out = out + weight * ref[:PAIR, :].astype(F32)
    out_ref[...] = out.astype(BF16)
    total_ref[...] = log_total


def both_cores(place_ref, own_ref, other_ref, count):
    own = own_ref[:, :count, :].reshape(-1, own_ref.shape[2])
    other = other_ref[:, :count, :].reshape(-1, other_ref.shape[2])
    first = place_ref[2] == 0
    return jnp.where(first, own, other), jnp.where(first, other, own)


def raw_kernel(place_ref, attended_ref, own_ref, other_ref, input_ref, out_ref):
    parts, own, _ = out_ref.shape
    attended = attended_ref[...]
    low, high = both_cores(place_ref, own_ref, other_ref, FOLD_POST)
    half = low.shape[0]
    raw_low = (dot(attended, low, ((1,), (1,))) + input_ref[:, :half]).astype(BF16)
    raw_high = (dot(attended, high, ((1,), (1,))) + input_ref[:, half:]).astype(BF16)
    packed = jnp.concatenate([attended[own * k : own * (k + 1)] for k in range(parts)], axis=1)
    for k in range(parts):
        out_ref[k, :, :half] = raw_low[own * k : own * (k + 1)]
        out_ref[k, :, half : 2 * half] = raw_high[own * k : own * (k + 1)]
        out_ref[k, :, 2 * half :] = packed


def norm_kernel(
    place_ref, arrived_ref, gram_ref, attended_ref, cross_ref, input_ref, back_ref, out_ref
):
    parts, own, _ = arrived_ref.shape
    features = out_ref.shape[2] - HDIM
    wide = attended_ref.shape[1]
    total = arrived_ref[0, :, :features].astype(F32)
    for k in range(1, parts):
        total = total + arrived_ref[k, :, :features].astype(F32)
    cross = cross_ref[...]
    back = jnp.zeros_like(cross)
    for k in range(parts):
        theirs = jnp.concatenate(
            [
                arrived_ref[k, :, features + wide * j : features + wide * (j + 1)]
                for j in range(parts)
            ],
            axis=0,
        )
        back = back + dot(theirs, gram_ref[owner_of(place_ref, k, parts)])
    back_ref[...] = cross + back
    attended = attended_ref[...].astype(F32)
    features_in = input_ref[...].astype(F32)
    squares = jnp.sum((attended * (2.0 * cross + back)).T, axis=0, keepdims=True) + jnp.sum(
        (features_in * features_in).T, axis=0, keepdims=True
    )
    side = jnp.concatenate(pieces(squares) + (jnp.zeros((own - 3, HDIM), BF16),), axis=0)
    summed = total.astype(BF16)
    for k in range(parts):
        out_ref[k, :, :features] = summed
        out_ref[k, :, features:] = side


def loss_kernel(
    width,
    lengths_ref,
    place_ref,
    steps_ref,
    arrived_ref,
    target_ref,
    own_ref,
    other_ref,
    back_ref,
    mine_ref,
    theirs_ref,
    loss_ref,
):
    parts, own, _ = arrived_ref.shape
    rows, features = target_ref.shape
    position = (place_ref[1] * 2 + place_ref[2]) * rows
    position = position + lax.broadcasted_iota(jnp.int32, (1, rows), 1)
    angle = (0.5 * math.pi / TSTEPS) * steps_ref[...].astype(F32)
    keep_level = sine(0.5 * math.pi - angle)
    weight = 1.0 + keep_level * keep_level
    for end in ends_of(lengths_ref):
        weight = jnp.where(position + 1 == end, 0.0, weight)
    side = arrived_ref[:, :, features:].astype(F32)
    squares = jnp.sum(jnp.sum(side, axis=0), axis=0, keepdims=True)
    inverse = column(lax.rsqrt(jnp.maximum(squares / width, 0.0) + EPSILON))
    prediction = arrived_ref[:, :, :features].reshape(rows, features).astype(F32) * inverse
    missed = prediction - target_ref[...].astype(F32)
    weighted_missed = column(weight) * missed
    loss = jnp.sum(weighted_missed * missed, axis=1, keepdims=True)
    loss_ref[...] = jnp.broadcast_to(jnp.sum(loss, axis=0, keepdims=True), (1, HDIM))
    pred_grad = weighted_missed.astype(BF16)
    along = jnp.sum(pred_grad.astype(F32) * prediction, axis=1, keepdims=True) / width
    low, high = both_cores(place_ref, own_ref, other_ref, FOLD_POST)
    half = low.shape[0]
    direct = dot(pred_grad[:, :half], low) + dot(pred_grad[:, half:], high)
    grad = (inverse * (direct - along * inverse * back_ref[...])).astype(BF16)
    first = place_ref[2] == 0
    mine_ref[...] = jnp.where(first, grad[:, :HDIM], grad[:, HDIM:])
    theirs_ref[...] = jnp.where(first, grad[:, HDIM:], grad[:, :HDIM])


def sent_kernel(grad_ref, attended_ref, total_ref, loss_ref, out_ref):
    grad = grad_ref[...]
    product = grad.astype(F32) * attended_ref[...].astype(F32)
    output_dot = jnp.sum(product.T, axis=0, keepdims=True)
    stats = stat_rows(total_ref[...], output_dot).astype(F32)
    loss_rows = [p.astype(F32) for p in pieces(loss_ref[...])]
    stats = jnp.concatenate([stats[:12]] + loss_rows + [stats[15:]], axis=0)
    out_ref[:PAIR, :] = grad
    out_ref[PAIR:, :] = stats.astype(BF16)


def backward_kernel(lengths_ref, place_ref, kv_ref, q_ref, *refs):
    *sent_refs, out_ref = refs
    ends = ends_of(lengths_ref)
    width = GROUP * PAIR
    query_pos = line_positions(place_ref)
    query_start = start_of(ends, query_pos)
    q = q_ref[...].reshape(width, HDIM)
    grad = jnp.concatenate([ref[:PAIR, :] for ref in sent_refs], axis=0)
    stats = [ref[PAIR:, :].astype(F32) for ref in sent_refs]
    log_total = jnp.concatenate([stat_row(x, 0) for x in stats], axis=1)
    output_dot = jnp.concatenate([stat_row(x, 6) for x in stats], axis=1)
    loss = functools.reduce(jnp.add, [x[12:13] + x[13:14] + x[14:15] for x in stats])
    tail = jnp.concatenate(
        [p.astype(F32) for p in pieces(loss)] + [jnp.zeros((STATS - 3, HDIM), F32)], axis=0
    )
    tail = jnp.concatenate((tail, tail), axis=1).astype(BF16)
    steps = key_steps(place_ref, ends)
    for step in range(out_ref.shape[0]):
        out_ref[step, PAIR:, :] = tail

        @pl.when(step < steps)
        def _():
            allowed = allowed_pairs(place_ref, step, query_start, query_pos)
            scores = dot(kv_ref[step, :, :HDIM], q, ((1,), (1,))) * SCALE
            probs = jnp.where(allowed, jnp.exp(scores - log_total), 0.0)
            out_ref[step, :PAIR, HDIM:] = dot(probs.astype(BF16), grad).astype(BF16)
            prob_grad = dot(kv_ref[step, :, HDIM:], grad, ((1,), (1,)))
            score_grad = (probs * (prob_grad - output_dot) * SCALE).astype(BF16)
            out_ref[step, :PAIR, :HDIM] = dot(score_grad, q).astype(BF16)

        @pl.when(step >= steps)
        def _():
            out_ref[step, :PAIR, :] = jnp.zeros((PAIR, 2 * HDIM), BF16)


def collect_kernel(*refs):
    *part_refs, out_ref, loss_ref = refs
    total = functools.reduce(jnp.add, [ref[...].astype(F32) for ref in part_refs])
    out_ref[...] = total[:PAIR].astype(BF16)
    rows = total[PAIR : PAIR + 3, :HDIM]
    loss_ref[...] = jnp.sum(rows, axis=0, keepdims=True)


def context_kernel(grad_ref, key_ref, value_ref, out_ref):
    key_grad = jnp.concatenate((grad_ref[:, :HDIM], grad_ref[:, 2 * HDIM : 3 * HDIM]), axis=1)
    value_grad = jnp.concatenate((grad_ref[:, HDIM : 2 * HDIM], grad_ref[:, 3 * HDIM :]), axis=1)
    total = dot(key_grad, key_ref[...], ((1,), (1,))) + dot(value_grad, value_ref[...], ((1,), (1,)))
    out_ref[0] = total.astype(BF16)


SMEM = pl.BlockSpec(memory_space=pltpu.SMEM)
HBM = pl.BlockSpec(memory_space=pltpu.HBM)
ANY = pl.BlockSpec(memory_space=pl.ANY)
VMEM = pl.BlockSpec(memory_space=pltpu.VMEM)
PARAMS = pltpu.CompilerParams(vmem_limit_bytes=32 * 1024 * 1024)


def local(
    concepts,
    noised,
    step_ids,
    doc_lengths,
    context,
    time_vec,
    w_pre,
    w_query,
    w_key,
    w_value,
    w_out,
    w_post,
):
    rows, features = concepts.shape
    parts = lax.axis_size("tp")
    chips = lax.axis_size(CHIPS)
    core = lax.axis_index("core")
    part = lax.axis_index("tp")
    seq_total = rows * lax.axis_size(ROWS)
    share = w_post.shape[0]
    own = rows // parts
    chip = lax.axis_index(CHIPS)
    place = jnp.stack((part, chip, core, chips)).astype(jnp.int32)
    width = share * parts
    head_width = w_out.shape[0]
    fold_rows = FOLD_POST + FOLD_OUT * parts
    steps = step_ids.reshape(1, rows)

    with jax.named_scope("inputs"):
        sent = pl.pallas_call(
            send_kernel,
            out_shape=jax.ShapeDtypeStruct((rows + fold_rows, share), BF16),
            in_specs=[SMEM, VMEM, VMEM, HBM, HBM, HBM, HBM],
            out_specs=VMEM,
            scratch_shapes=[
                pltpu.VMEM((rows, features), BF16),
                pltpu.VMEM((features, share), BF16),
                pltpu.VMEM((share, HDIM), BF16),
                pltpu.VMEM((2 * FOLD_OUT, width), BF16),
                pltpu.SemaphoreType.DMA((5,)),
            ],
            compiler_params=PARAMS,
        )(place, steps, time_vec.reshape(1, share), noised, w_pre, w_post, w_out)
        blocks = around(sent, "tp")
        input_part = sent[:rows]
        input_post = dot(input_part, w_post)
    with jax.named_scope("keys_values"):
        kv_shape = jax.ShapeDtypeStruct((rows, 2 * HDIM), BF16)
        mine, theirs = pl.pallas_call(
            project_kernel,
            out_shape=(kv_shape, kv_shape),
            in_specs=[SMEM, HBM, HBM, HBM],
            out_specs=(VMEM, VMEM),
            scratch_shapes=[
                pltpu.VMEM(context.shape, BF16),
                pltpu.VMEM((2,) + w_key.shape, BF16),
                pltpu.SemaphoreType.DMA((12,)),
            ],
            compiler_params=PARAMS,
        )(place, context, w_key, w_value)
        own_kv = to_head(mine, theirs, core)
        all_kv = jnp.stack(shifted(own_kv, "y"))
    with jax.named_scope("fold"):
        folded = pl.pallas_call(
            fold_kernel,
            out_shape=jax.ShapeDtypeStruct((chips, fold_rows, head_width), BF16),
            in_specs=[SMEM, HBM] + [VMEM] * len(blocks),
            out_specs=VMEM,
            scratch_shapes=[pltpu.VMEM(w_out.shape, BF16), pltpu.SemaphoreType.DMA((2,))],
            compiler_params=PARAMS,
        )(place, w_out, *blocks)
        own_fold = lax.all_to_all(folded, CHIPS, 0, 0, tiled=True)
        other_fold = swap(own_fold)
        gram = [f[:, FOLD_POST:].reshape(chips, parts, FOLD_OUT, -1) for f in (own_fold, other_fold)]
        first = core == 0
        gram = jnp.stack((jnp.where(first, gram[0], gram[1]), jnp.where(first, gram[1], gram[0])))
        gram = gram.transpose(2, 0, 1, 3, 4).reshape(parts, 2 * chips * FOLD_OUT, -1)
    with jax.named_scope("targets"):
        count = lax.axis_size(ROWS)
        following = lax.ppermute(concepts[:1], ROWS, [(i + 1, i) for i in range(count - 1)])
        targets = jnp.concatenate((concepts[1:], following), axis=0)
    with jax.named_scope("queries"):
        query_shape = jax.ShapeDtypeStruct((rows, HDIM), BF16)
        mine, theirs = pl.pallas_call(
            query_kernel,
            out_shape=(query_shape, query_shape),
            in_specs=[SMEM, HBM, ANY, ANY] + [VMEM] * len(blocks),
            out_specs=(VMEM, VMEM),
            scratch_shapes=[
                pltpu.VMEM((parts, share, head_width), BF16),
                pltpu.SemaphoreType.DMA((parts,)),
            ],
            compiler_params=PARAMS,
        )(place, w_query, folded, all_kv, *blocks)
        query_head = to_head(mine, theirs, core)
        cross = pl.pallas_call(
            cross_kernel,
            out_shape=jax.ShapeDtypeStruct((rows, head_width), F32),
            in_specs=[SMEM] + [VMEM] * (1 + len(blocks)),
            out_specs=VMEM,
            compiler_params=PARAMS,
        )(place, w_out, *blocks)
        line_queries = jnp.stack(shifted(query_head, "x"))
    with jax.named_scope("attention"):
        sent = pl.pallas_call(
            forward_kernel,
            out_shape=jax.ShapeDtypeStruct((GROUP, PAIR + STATS, HDIM), BF16),
            in_specs=[SMEM, SMEM, VMEM, VMEM],
            out_specs=VMEM,
            compiler_params=PARAMS,
        )(doc_lengths, place, line_queries, all_kv)
        attended_head, log_total = pl.pallas_call(
            merge_kernel,
            out_shape=(
                jax.ShapeDtypeStruct((PAIR, HDIM), BF16),
                jax.ShapeDtypeStruct((1, PAIR), F32),
            ),
            in_specs=[VMEM] * GROUP,
            out_specs=(VMEM, VMEM),
            compiler_params=PARAMS,
        )(*returned(sent, "x"))
        attended = to_rows(attended_head, core)
    with jax.named_scope("raw"):
        sent = pl.pallas_call(
            raw_kernel,
            out_shape=jax.ShapeDtypeStruct((parts, own, features + head_width * parts), BF16),
            in_specs=[SMEM, VMEM, VMEM, VMEM, VMEM],
            out_specs=VMEM,
            compiler_params=PARAMS,
        )(place, attended, own_fold, other_fold, input_post)
        arrived = lax.all_to_all(sent, "tp", 0, 0, tiled=True)
    with jax.named_scope("norm"):
        back, sent = pl.pallas_call(
            norm_kernel,
            out_shape=(
                jax.ShapeDtypeStruct((rows, head_width), F32),
                jax.ShapeDtypeStruct((parts, own, features + HDIM), BF16),
            ),
            in_specs=[SMEM] + [VMEM] * 5,
            out_specs=(VMEM, VMEM),
            compiler_params=PARAMS,
        )(place, arrived, gram, attended, cross, input_part)
        arrived = lax.all_to_all(sent, "tp", 0, 0, tiled=True)
    with jax.named_scope("loss"):
        mine, theirs, loss_part = pl.pallas_call(
            functools.partial(loss_kernel, width),
            out_shape=(
                query_shape,
                query_shape,
                jax.ShapeDtypeStruct((1, HDIM), F32),
            ),
            in_specs=[SMEM, SMEM] + [VMEM] * 6,
            out_specs=(VMEM, VMEM, VMEM),
            compiler_params=PARAMS,
        )(doc_lengths, place, steps, arrived, targets, own_fold, other_fold, back)
    with jax.named_scope("sent_grads"):
        grad_head = to_head(mine, theirs, core)
        sent = pl.pallas_call(
            sent_kernel,
            out_shape=jax.ShapeDtypeStruct((PAIR + STATS, HDIM), BF16),
            in_specs=[VMEM] * 4,
            out_specs=VMEM,
            compiler_params=PARAMS,
        )(grad_head, attended_head, log_total, loss_part)
        line_grads = shifted(sent, "x")
    with jax.named_scope("attention_grad"):
        sent = pl.pallas_call(
            backward_kernel,
            out_shape=jax.ShapeDtypeStruct((chips // GROUP, PAIR + STATS, 2 * HDIM), BF16),
            in_specs=[SMEM, SMEM] + [VMEM] * (2 + GROUP),
            out_specs=VMEM,
            compiler_params=PARAMS,
        )(doc_lengths, place, all_kv, line_queries, *line_grads)
        kv_grad, loss_part = pl.pallas_call(
            collect_kernel,
            out_shape=(
                jax.ShapeDtypeStruct((PAIR, 2 * HDIM), BF16),
                jax.ShapeDtypeStruct((1, HDIM), F32),
            ),
            in_specs=[VMEM] * (chips // GROUP),
            out_specs=(VMEM, VMEM),
            compiler_params=PARAMS,
        )(*returned(sent, "y"))
        kv_grad = to_rows(kv_grad, core)
        loss_part = loss_part[0, 0]
        loss = (loss_part + swap(loss_part)) / (seq_total * features)
    with jax.named_scope("d_context"):
        terms = pl.pallas_call(
            context_kernel,
            grid=(parts,),
            out_shape=jax.ShapeDtypeStruct((parts, rows, share), BF16),
            in_specs=[
                pl.BlockSpec((rows, 4 * HDIM), lambda t: (0, 0)),
                pl.BlockSpec((share, 2 * HDIM), lambda t: (t, 0)),
                pl.BlockSpec((share, 2 * HDIM), lambda t: (t, 0)),
            ],
            out_specs=pl.BlockSpec((1, rows, share), lambda t: (t, 0, 0)),
            compiler_params=PARAMS,
        )(kv_grad, w_key, w_value)
        arrived = lax.all_to_all(terms, "tp", 0, 0, tiled=True)
        d_context = jnp.sum(arrived.astype(F32), axis=0).astype(BF16)
    return d_context, loss


def solution(mesh):
    cores = 2
    count, parts = mesh.devices.shape
    side = math.isqrt(count // cores)
    split = Mesh(mesh.devices.reshape(side, side, cores, parts), ("y", "x", "core", "tp"))
    by_rows = P(ROWS, None)
    by_columns = P(None, "tp")
    return jax.shard_map(
        local,
        mesh=split,
        in_specs=(
            by_rows,
            by_rows,
            P(ROWS),
            P(),
            by_rows,
            P("tp"),
            by_columns,
            by_columns,
            by_columns,
            by_columns,
            P("tp", None),
            P("tp", None),
        ),
        out_specs=(P(ROWS, "tp"), P()),
        check_vma=False,
    )
```

```python
import functools
import math

import jax
import jax.numpy as jnp
from jax import lax
from jax.experimental import pallas as pl
from jax.experimental.pallas import tpu as pltpu
from jax.sharding import Mesh
from jax.sharding import PartitionSpec as P

HDIM = 128
TSTEPS = 100
MASKED = -1e30
EPSILON = 1e-06
ROWS = ("y", "x", "core")
CHIPS = ("y", "x")
SCALE = 1.0 / math.sqrt(HDIM)
PAIR = 256
GROUP = 4
FOLD_POST = 32
FOLD_OUT = 8
STATS = 16
F32 = jnp.float32
BF16 = jnp.bfloat16


def dot(a, b, contract=((1,), (0,))):
    return lax.dot_general(a, b, (contract, ((), ())), preferred_element_type=F32)


def shifted(block, axis):
    count = lax.axis_size(axis)
    routes = [[(i, (i + s) % count) for i in range(count)] for s in range(1, count)]
    return [block] + [lax.ppermute(block, axis, route) for route in routes]


def returned(blocks, axis):
    count = lax.axis_size(axis)
    routes = [[(i, (i - s) % count) for i in range(count)] for s in range(count)]
    return [blocks[0]] + [lax.ppermute(blocks[s], axis, routes[s]) for s in range(1, count)]


def around(block, axis):
    count = lax.axis_size(axis)
    up = [(i, (i + 1) % count) for i in range(count)]
    down = [(i, (i - 1) % count) for i in range(count)]
    behind, ahead = [block], [block]
    for _ in range(count // 2 - 1):
        behind.append(lax.ppermute(behind[-1], axis, up))
        ahead.append(lax.ppermute(ahead[-1], axis, down))
    half = block.shape[0] // 2
    far = [lax.ppermute(behind[-1][:half], axis, up), lax.ppermute(ahead[-1][half:], axis, down)]
    return behind + far + ahead[:0:-1]


def gathered_blocks(refs):
    half = (len(refs) - 1) // 2
    far = jnp.concatenate((refs[half][...], refs[half + 1][...]), axis=0)
    return [r[...] for r in refs[:half]] + [far] + [r[...] for r in refs[half + 2 :]]


def owner_of(place_ref, distance, parts):
    return lax.rem(place_ref[0] + (parts - distance), parts)


def swap(block):
    return lax.ppermute(block, "core", [(0, 1), (1, 0)])


def to_head(mine, theirs, core):
    first = core == 0
    got = swap(theirs)
    return jnp.concatenate((jnp.where(first, mine, got), jnp.where(first, got, mine)), axis=0)


def to_rows(block, core):
    first = core == 0
    half = block.shape[0] // 2
    top, bottom = block[:half], block[half:]
    mine = jnp.where(first, top, bottom)
    got = swap(jnp.where(first, bottom, top))
    return jnp.concatenate((jnp.where(first, mine, got), jnp.where(first, got, mine)), axis=1)


def pieces(values):
    high = values.astype(BF16)
    rest = values - high.astype(F32)
    middle = rest.astype(BF16)
    return high, middle, (rest - middle.astype(F32)).astype(BF16)


def stat_rows(*rows):
    out = []
    for row in rows:
        for piece in pieces(row):
            out += [piece[:, :HDIM].astype(F32), piece[:, HDIM:].astype(F32)]
    out.append(jnp.zeros((STATS - len(out), HDIM), F32))
    return jnp.concatenate(out, axis=0).astype(BF16)


def stat_row(block, at):
    total = block[at : at + 2] + block[at + 2 : at + 4] + block[at + 4 : at + 6]
    return jnp.concatenate((total[:1], total[1:]), axis=1)


def sine(x):
    y = x * x
    total = jnp.full_like(x, 1.0 / 6227020800.0)
    for c in (-1.0 / 39916800.0, 1.0 / 362880.0, -1.0 / 5040.0, 1.0 / 120.0, -1.0 / 6.0, 1.0):
        total = total * y + c
    return total * x


def column(row):
    return jnp.broadcast_to(row, (HDIM, HDIM)).T[:, :1]


def ends_of(lengths_ref):
    ends = [lengths_ref[0]]
    for d in range(1, lengths_ref.shape[0]):
        ends.append(ends[-1] + lengths_ref[d])
    return ends


def start_of(ends, positions):
    start = jnp.zeros_like(positions)
    for end in ends:
        start = jnp.where(positions >= end, end, start)
    return start


def fetch(pairs, sems):
    copies = [pltpu.make_async_copy(f, t, sems.at[i]) for i, (f, t) in enumerate(pairs)]
    for copy in copies:
        copy.start()
    return copies


def send_kernel(
    place_ref,
    steps_ref,
    time_ref,
    noised_ref,
    pre_ref,
    post_ref,
    out_ref,
    sent_ref,
    noised,
    pre,
    post_part,
    out_part,
    sems,
):
    rows, features = noised.shape
    share = pre.shape[1]
    slot = place_ref[2] * place_ref[3] + place_ref[1]
    lanes = pl.ds(pl.multiple_of(slot // (HDIM // FOLD_POST) * HDIM, HDIM), HDIM)
    lines = pl.ds(pl.multiple_of(slot // 2 * (2 * FOLD_OUT), 2 * FOLD_OUT), 2 * FOLD_OUT)
    half = features // 2
    copies = fetch(
        (
            (noised_ref, noised),
            (pre_ref.at[:half], pre.at[:half]),
            (pre_ref.at[half:], pre.at[half:]),
            (post_ref.at[:, lanes], post_part),
            (out_ref.at[lines], out_part),
        ),
        sems,
    )
    angle = (0.5 * math.pi / TSTEPS) * steps_ref[...].astype(F32)
    noise = column(sine(angle)) * time_ref[...]
    copies[3].wait()
    post = post_part[...].astype(F32).T
    quarter = lax.rem(slot, HDIM // FOLD_POST)
    post_rows = post[:FOLD_POST]
    for k in range(1, HDIM // FOLD_POST):
        post_rows = jnp.where(quarter == k, post[FOLD_POST * k : FOLD_POST * (k + 1)], post_rows)
    copies[4].wait()
    out_rows = out_part[...].astype(F32)
    out_rows = jnp.where(lax.rem(slot, 2) == 0, out_rows[:FOLD_OUT], out_rows[FOLD_OUT:])
    parts = out_rows.shape[1] // share
    out_rows = [out_rows[:, share * k : share * (k + 1)] for k in range(parts)]
    sent_ref[rows:, :] = jnp.concatenate([post_rows] + out_rows, axis=0).astype(BF16)
    for k in range(3):
        copies[k].wait()
    sent_ref[:rows, :] = (dot(noised[...], pre[...]) + noise).astype(BF16)


def project_kernel(
    place_ref, context_ref, key_ref, value_ref, mine_ref, theirs_ref, context, weight, sems
):
    parts = 4
    share = context.shape[1] // parts
    pairs = []
    for k in range(parts):
        at = pl.ds(share * k, share)
        pairs.append((context_ref.at[:, at], context.at[:, at]))
        pairs.append((key_ref.at[at], weight.at[0, at]))
        pairs.append((value_ref.at[at], weight.at[1, at]))
    copies = fetch(pairs, sems)
    keys = jnp.zeros((context.shape[0], 2 * HDIM), F32)
    values = keys
    for k in range(parts):
        at = slice(share * k, share * (k + 1))
        for copy in copies[3 * k : 3 * k + 3]:
            copy.wait()
        keys = keys + dot(context[:, at], weight[0, at])
        values = values + dot(context[:, at], weight[1, at])
    left = jnp.concatenate((keys[:, :HDIM], values[:, :HDIM]), axis=1)
    right = jnp.concatenate((keys[:, HDIM:], values[:, HDIM:]), axis=1)
    first = place_ref[2] == 0
    mine_ref[...] = jnp.where(first, left, right).astype(BF16)
    theirs_ref[...] = jnp.where(first, right, left).astype(BF16)


def gathered_kernel(place_ref, w_query_ref, w_out_ref, post_ref, hold_ref, *refs):
    block_refs, refs = refs[:-6], refs[-6:]
    mine_ref, theirs_ref, cross_ref, post_out_ref, input_ref, folded_ref = refs
    rows = mine_ref.shape[0]
    heads, width = w_out_ref.shape
    blocks = gathered_blocks(block_refs)
    squares = jnp.zeros((rows, 1), F32)
    for block in blocks:
        wide = block[:rows].astype(F32)
        squares = squares + jnp.sum(wide * wide, axis=1, keepdims=True)
    query = jnp.zeros((rows, heads), F32)
    parts = len(blocks)
    share = blocks[0].shape[1]
    for distance, block in enumerate(blocks):
        owner = owner_of(place_ref, distance, parts)
        at = pl.ds(pl.multiple_of(owner * share, share), share)
        query = query + dot(block[:rows], w_query_ref[at, :])
    query = (query * lax.rsqrt(squares / width + EPSILON)).astype(BF16)
    first = place_ref[2] == 0
    mine_ref[...] = jnp.where(first, query[:, :HDIM], query[:, HDIM:])
    theirs_ref[...] = jnp.where(first, query[:, HDIM:], query[:, :HDIM])

    top = rows + FOLD_POST
    both = jnp.zeros((top, heads), F32)
    for distance, block in enumerate(blocks):
        owner = owner_of(place_ref, distance, parts)
        at = pl.ds(pl.multiple_of(owner * share, share), share)
        both = both + dot(block[:top], w_out_ref[:, at], ((1,), (1,)))
    cross_ref[...] = both[:rows]
    span = FOLD_OUT * parts
    slices = jnp.concatenate([block[top:] for block in blocks], axis=0)
    gram = [jnp.zeros((FOLD_OUT, heads), F32)] * parts
    for k in range(parts):
        product = dot(slices, w_out_ref[:, share * k : share * (k + 1)], ((1,), (1,)))
        for b in range(parts):
            at = span * b + FOLD_OUT * k
            gram[b] = gram[b] + product[at : at + FOLD_OUT]
    folded = jnp.concatenate([both[rows:]] + gram, axis=0).astype(BF16)
    for k in range(folded_ref.shape[0]):
        folded_ref[k] = folded
    post_out_ref[...] = dot(blocks[0][:rows], post_ref[...])
    input_ref[...] = blocks[0][:rows]


def line_positions(place_ref):
    row = place_ref[1] // GROUP
    here = lax.rem(place_ref[1], GROUP)
    chips = [row * GROUP + lax.rem(here + (GROUP - k), GROUP) for k in range(GROUP)]
    lanes = lax.broadcasted_iota(jnp.int32, (1, PAIR), 1)
    return jnp.concatenate([chip * PAIR + lanes for chip in chips], axis=1)


def key_steps(place_ref, ends):
    row = place_ref[1] // GROUP
    here = lax.rem(place_ref[1], GROUP)
    floor = start_of(ends, row * (GROUP * PAIR))
    past = jnp.maximum(floor - (here * PAIR + PAIR - 1), 0)
    lowest = (past + GROUP * PAIR - 1) // (GROUP * PAIR)
    return row - lowest + 1


def allowed_pairs(place_ref, step, query_start, query_pos):
    base = (place_ref[1] - step * GROUP) * PAIR
    key_pos = base + lax.broadcasted_iota(jnp.int32, (PAIR, query_pos.shape[1]), 0)
    return (key_pos >= query_start) & (key_pos <= query_pos)


def forward_kernel(lengths_ref, place_ref, q_ref, kv_ref, out_ref):
    ends = ends_of(lengths_ref)
    width = GROUP * PAIR
    query_pos = line_positions(place_ref)
    query_start = start_of(ends, query_pos)
    q = q_ref[...].reshape(width, HDIM)

    def body(step, carry):
        row_max, row_total, weighted = carry
        scores = dot(kv_ref[step, :, :HDIM], q, ((1,), (1,))) * SCALE
        scores = jnp.where(allowed_pairs(place_ref, step, query_start, query_pos), scores, MASKED)
        new_max = jnp.maximum(row_max, jnp.max(scores, axis=0, keepdims=True))
        probs = jnp.exp(scores - new_max)
        fading = jnp.exp(row_max - new_max)
        row_total = row_total * fading + jnp.sum(probs, axis=0, keepdims=True)
        weighted = weighted * fading + dot(kv_ref[step, :, HDIM:], probs.astype(BF16), ((0,), (0,)))
        return new_max, row_total, weighted

    row_max, row_total, weighted = lax.fori_loop(
        0,
        key_steps(place_ref, ends),
        body,
        (
            jnp.full((1, width), MASKED, F32),
            jnp.zeros((1, width), F32),
            jnp.zeros((HDIM, width), F32),
        ),
    )
    out = (weighted / row_total).T.astype(BF16)
    log_total = row_max + jnp.log(row_total)
    for k in range(GROUP):
        at = slice(PAIR * k, PAIR * (k + 1))
        out_ref[k, :PAIR, :] = out[at]
        out_ref[k, PAIR:, :] = stat_rows(log_total[:, at])


def merge_kernel(*refs):
    *part_refs, out_ref, total_ref = refs
    logs = [stat_row(ref[PAIR:, :].astype(F32), 0) for ref in part_refs]
    top = functools.reduce(jnp.maximum, logs)
    log_total = top + jnp.log(functools.reduce(jnp.add, [jnp.exp(x - top) for x in logs]))
    out = jnp.zeros((PAIR, HDIM), F32)
    for x, ref in zip(logs, part_refs):
        weight = jnp.broadcast_to(jnp.exp(x - log_total), (HDIM, PAIR)).T
        out = out + weight * ref[:PAIR, :].astype(F32)
    out_ref[...] = out.astype(BF16)
    total_ref[...] = log_total


def both_cores(place_ref, own_ref, other_ref, count):
    own = own_ref[:, :count, :].reshape(-1, own_ref.shape[2])
    other = other_ref[:, :count, :].reshape(-1, other_ref.shape[2])
    first = place_ref[2] == 0
    return jnp.where(first, own, other), jnp.where(first, other, own)


def raw_kernel(place_ref, attended_ref, own_ref, other_ref, input_ref, hold_ref, out_ref):
    parts, own, _ = out_ref.shape
    attended = attended_ref[...]
    low, high = both_cores(place_ref, own_ref, other_ref, FOLD_POST)
    half = low.shape[0]
    raw_low = (dot(attended, low, ((1,), (1,))) + input_ref[:, :half]).astype(BF16)
    raw_high = (dot(attended, high, ((1,), (1,))) + input_ref[:, half:]).astype(BF16)
    packed = jnp.concatenate([attended[own * k : own * (k + 1)] for k in range(parts)], axis=1)
    for k in range(parts):
        out_ref[k, :, :half] = raw_low[own * k : own * (k + 1)]
        out_ref[k, :, half : 2 * half] = raw_high[own * k : own * (k + 1)]
        out_ref[k, :, 2 * half :] = packed


def norm_kernel(
    place_ref,
    arrived_ref,
    own_ref,
    other_ref,
    attended_ref,
    cross_ref,
    input_ref,
    back_ref,
    out_ref,
):
    parts, own, _ = arrived_ref.shape
    features = out_ref.shape[2] - HDIM
    rows, share = input_ref.shape
    wide = attended_ref.shape[1]
    total = arrived_ref[0, :, :features].astype(F32)
    for k in range(1, parts):
        total = total + arrived_ref[k, :, :features].astype(F32)
    cross = cross_ref[...]
    back = jnp.zeros_like(cross)
    first = place_ref[2] == 0
    chips = own_ref.shape[0]
    grams = []
    for ref in (own_ref, other_ref):
        gram = ref[:, FOLD_POST:, :].astype(F32)
        grams.append(gram.reshape(chips, parts, FOLD_OUT, wide))
    for distance in range(parts):
        k = owner_of(place_ref, distance, parts)
        theirs = jnp.concatenate(
            [
                arrived_ref[k, :, features + wide * j : features + wide * (j + 1)]
                for j in range(parts)
            ],
            axis=0,
        )
        half = chips * FOLD_OUT
        own_gram, other_gram = (g[:, distance].reshape(half, wide).astype(BF16) for g in grams)
        back = back + dot(theirs[:, :half], jnp.where(first, own_gram, other_gram))
        back = back + dot(theirs[:, half:], jnp.where(first, other_gram, own_gram))
    back_ref[...] = cross + back
    attended = attended_ref[...].astype(F32)
    features_in = input_ref[...].astype(F32)
    squares = jnp.sum((attended * (2.0 * cross + back)).T, axis=0, keepdims=True) + jnp.sum(
        (features_in * features_in).T, axis=0, keepdims=True
    )
    side = jnp.concatenate(pieces(squares) + (jnp.zeros((own - 3, HDIM), BF16),), axis=0)
    summed = total.astype(BF16)
    for k in range(parts):
        out_ref[k, :, :features] = summed
        out_ref[k, :, features:] = side


def loss_kernel(
    width,
    lengths_ref,
    place_ref,
    steps_ref,
    arrived_ref,
    target_ref,
    own_ref,
    other_ref,
    back_ref,
    mine_ref,
    theirs_ref,
    loss_ref,
):
    parts, own, _ = arrived_ref.shape
    rows, features = target_ref.shape
    position = (place_ref[1] * 2 + place_ref[2]) * rows
    position = position + lax.broadcasted_iota(jnp.int32, (1, rows), 1)
    angle = (0.5 * math.pi / TSTEPS) * steps_ref[...].astype(F32)
    keep_level = sine(0.5 * math.pi - angle)
    weight = 1.0 + keep_level * keep_level
    for end in ends_of(lengths_ref):
        weight = jnp.where(position + 1 == end, 0.0, weight)
    side = arrived_ref[:, :, features:].astype(F32)
    squares = jnp.sum(jnp.sum(side, axis=0), axis=0, keepdims=True)
    inverse = column(lax.rsqrt(jnp.maximum(squares / width, 0.0) + EPSILON))
    prediction = arrived_ref[:, :, :features].reshape(rows, features).astype(F32) * inverse
    missed = prediction - target_ref[...].astype(F32)
    weighted_missed = column(weight) * missed
    loss = jnp.sum(weighted_missed * missed, axis=1, keepdims=True)
    loss_ref[...] = jnp.broadcast_to(jnp.sum(loss, axis=0, keepdims=True), (1, HDIM))
    pred_grad = weighted_missed.astype(BF16)
    along = jnp.sum(pred_grad.astype(F32) * prediction, axis=1, keepdims=True) / width
    low, high = both_cores(place_ref, own_ref, other_ref, FOLD_POST)
    half = low.shape[0]
    direct = dot(pred_grad[:, :half], low) + dot(pred_grad[:, half:], high)
    grad = (inverse * (direct - along * inverse * back_ref[...])).astype(BF16)
    first = place_ref[2] == 0
    mine_ref[...] = jnp.where(first, grad[:, :HDIM], grad[:, HDIM:])
    theirs_ref[...] = jnp.where(first, grad[:, HDIM:], grad[:, :HDIM])


def sent_kernel(grad_ref, attended_ref, total_ref, loss_ref, out_ref):
    grad = grad_ref[...]
    product = grad.astype(F32) * attended_ref[...].astype(F32)
    output_dot = jnp.sum(product.T, axis=0, keepdims=True)
    stats = stat_rows(total_ref[...], output_dot).astype(F32)
    loss_rows = [p.astype(F32) for p in pieces(loss_ref[...])]
    stats = jnp.concatenate([stats[:12]] + loss_rows + [stats[15:]], axis=0)
    out_ref[:PAIR, :] = grad
    out_ref[PAIR:, :] = stats.astype(BF16)


def backward_kernel(lengths_ref, place_ref, kv_ref, q_ref, *refs):
    *sent_refs, out_ref = refs
    ends = ends_of(lengths_ref)
    width = GROUP * PAIR
    query_pos = line_positions(place_ref)
    query_start = start_of(ends, query_pos)
    q = q_ref[...].reshape(width, HDIM)
    grad = jnp.concatenate([ref[:PAIR, :] for ref in sent_refs], axis=0)
    stats = [ref[PAIR:, :].astype(F32) for ref in sent_refs]
    log_total = jnp.concatenate([stat_row(x, 0) for x in stats], axis=1)
    output_dot = jnp.concatenate([stat_row(x, 6) for x in stats], axis=1)
    loss = functools.reduce(jnp.add, [x[12:13] + x[13:14] + x[14:15] for x in stats])
    tail = jnp.concatenate(
        [p.astype(F32) for p in pieces(loss)] + [jnp.zeros((STATS - 3, HDIM), F32)], axis=0
    )
    tail = jnp.concatenate((tail, tail), axis=1).astype(BF16)
    steps = key_steps(place_ref, ends)
    for step in range(out_ref.shape[0]):
        row = lax.rem(place_ref[1] // GROUP + (out_ref.shape[0] - step), out_ref.shape[0])
        out_ref[row, PAIR:, :] = tail

        @pl.when(step < steps)
        def _():
            allowed = allowed_pairs(place_ref, step, query_start, query_pos)
            scores = dot(kv_ref[step, :, :HDIM], q, ((1,), (1,))) * SCALE
            probs = jnp.where(allowed, jnp.exp(scores - log_total), 0.0)
            out_ref[row, :PAIR, HDIM:] = dot(probs.astype(BF16), grad).astype(BF16)
            prob_grad = dot(kv_ref[step, :, HDIM:], grad, ((1,), (1,)))
            score_grad = (probs * (prob_grad - output_dot) * SCALE).astype(BF16)
            out_ref[row, :PAIR, :HDIM] = dot(score_grad, q).astype(BF16)

        @pl.when(step >= steps)
        def _():
            out_ref[row, :PAIR, :] = jnp.zeros((PAIR, 2 * HDIM), BF16)


def collect_kernel(*refs):
    arrived_ref, out_ref, loss_ref = refs
    parts = [arrived_ref[k].astype(F32) for k in range(arrived_ref.shape[0])]
    total = functools.reduce(jnp.add, parts)
    out_ref[...] = total[:PAIR].astype(BF16)
    rows = total[PAIR : PAIR + 3, :HDIM]
    loss_ref[...] = jnp.sum(rows, axis=0, keepdims=True)


def context_kernel(grad_ref, hold_ref, key_ref, value_ref, out_ref):
    grad = grad_ref[...].astype(F32).T.astype(BF16)
    key_grad = jnp.concatenate((grad[:HDIM], grad[2 * HDIM : 3 * HDIM]), axis=0)
    value_grad = jnp.concatenate((grad[HDIM : 2 * HDIM], grad[3 * HDIM :]), axis=0)
    parts, share, _ = out_ref.shape
    for k in range(parts):
        at = slice(share * k, share * (k + 1))
        total = dot(key_ref[at], key_grad) + dot(value_ref[at], value_grad)
        out_ref[k] = total.astype(BF16)


def total_kernel(arrived_ref, out_ref):
    parts = [arrived_ref[k].astype(F32) for k in range(arrived_ref.shape[0])]
    out_ref[...] = functools.reduce(jnp.add, parts).T.astype(BF16)


SMEM = pl.BlockSpec(memory_space=pltpu.SMEM)
HBM = pl.BlockSpec(memory_space=pltpu.HBM)
ANY = pl.BlockSpec(memory_space=pl.ANY)
VMEM = pl.BlockSpec(memory_space=pltpu.VMEM)
PARAMS = pltpu.CompilerParams(vmem_limit_bytes=32 * 1024 * 1024)
WHOLE = pltpu.CompilerParams(vmem_limit_bytes=60 * 1024 * 1024)


def local(
    concepts,
    noised,
    step_ids,
    doc_lengths,
    context,
    time_vec,
    w_pre,
    w_query,
    w_key,
    w_value,
    w_out,
    w_post,
):
    rows, features = concepts.shape
    parts = lax.axis_size("tp")
    chips = lax.axis_size(CHIPS)
    core = lax.axis_index("core")
    part = lax.axis_index("tp")
    seq_total = rows * lax.axis_size(ROWS)
    share = w_post.shape[0]
    own = rows // parts
    chip = lax.axis_index(CHIPS)
    place = jnp.stack((part, chip, core, chips)).astype(jnp.int32)
    width = share * parts
    head_width = w_out.shape[0]
    fold_rows = FOLD_POST + FOLD_OUT * parts
    steps = step_ids.reshape(1, rows)

    with jax.named_scope("inputs"):
        sent = pl.pallas_call(
            send_kernel,
            out_shape=jax.ShapeDtypeStruct((rows + fold_rows, share), BF16),
            in_specs=[SMEM, VMEM, VMEM, HBM, HBM, HBM, HBM],
            out_specs=VMEM,
            scratch_shapes=[
                pltpu.VMEM((rows, features), BF16),
                pltpu.VMEM((features, share), BF16),
                pltpu.VMEM((share, HDIM), BF16),
                pltpu.VMEM((2 * FOLD_OUT, width), BF16),
                pltpu.SemaphoreType.DMA((5,)),
            ],
            compiler_params=WHOLE,
        )(place, steps, time_vec.reshape(1, share), noised, w_pre, w_post, w_out)
        blocks = around(sent, "tp")
    with jax.named_scope("keys_values"):
        kv_shape = jax.ShapeDtypeStruct((rows, 2 * HDIM), BF16)
        mine, theirs = pl.pallas_call(
            project_kernel,
            out_shape=(kv_shape, kv_shape),
            in_specs=[SMEM, HBM, HBM, HBM],
            out_specs=(VMEM, VMEM),
            scratch_shapes=[
                pltpu.VMEM(context.shape, BF16),
                pltpu.VMEM((2,) + w_key.shape, BF16),
                pltpu.SemaphoreType.DMA((12,)),
            ],
            compiler_params=PARAMS,
        )(place, context, w_key, w_value)
        own_kv = to_head(mine, theirs, core)
        all_kv = jnp.stack(shifted(own_kv, "y"))
    with jax.named_scope("targets"):
        count = lax.axis_size(ROWS)
        following = lax.ppermute(concepts[:1], ROWS, [(i + 1, i) for i in range(count - 1)])
        targets = jnp.concatenate((concepts[1:], following), axis=0)
    with jax.named_scope("gathered"):
        query_shape = jax.ShapeDtypeStruct((rows, HDIM), BF16)
        mine, theirs, cross, input_post, input_part, folded = pl.pallas_call(
            gathered_kernel,
            out_shape=(
                query_shape,
                query_shape,
                jax.ShapeDtypeStruct((rows, head_width), F32),
                jax.ShapeDtypeStruct((rows, features), F32),
                jax.ShapeDtypeStruct((rows, share), BF16),
                jax.ShapeDtypeStruct((chips, fold_rows, head_width), BF16),
            ),
            in_specs=[SMEM, VMEM, VMEM, VMEM, ANY] + [VMEM] * len(blocks),
            out_specs=(VMEM,) * 6,
            compiler_params=PARAMS,
        )(place, w_query, w_out, w_post, all_kv, *blocks)
        query_head = to_head(mine, theirs, core)
        line_queries = jnp.stack(shifted(query_head, "x"))
        own_fold = lax.all_to_all(folded, CHIPS, 0, 0, tiled=True)
        other_fold = swap(own_fold)
    with jax.named_scope("attention"):
        sent = pl.pallas_call(
            forward_kernel,
            out_shape=jax.ShapeDtypeStruct((GROUP, PAIR + STATS, HDIM), BF16),
            in_specs=[SMEM, SMEM, VMEM, VMEM],
            out_specs=VMEM,
            compiler_params=PARAMS,
        )(doc_lengths, place, line_queries, all_kv)
        attended_head, log_total = pl.pallas_call(
            merge_kernel,
            out_shape=(
                jax.ShapeDtypeStruct((PAIR, HDIM), BF16),
                jax.ShapeDtypeStruct((1, PAIR), F32),
            ),
            in_specs=[VMEM] * GROUP,
            out_specs=(VMEM, VMEM),
            compiler_params=PARAMS,
        )(*returned(sent, "x"))
        attended = to_rows(attended_head, core)
    with jax.named_scope("raw"):
        sent = pl.pallas_call(
            raw_kernel,
            out_shape=jax.ShapeDtypeStruct((parts, own, features + head_width * parts), BF16),
            in_specs=[SMEM, VMEM, VMEM, VMEM, VMEM, ANY],
            out_specs=VMEM,
            compiler_params=PARAMS,
        )(place, attended, own_fold, other_fold, input_post, targets)
        arrived = lax.all_to_all(sent, "tp", 0, 0, tiled=True)
    with jax.named_scope("norm"):
        back, sent = pl.pallas_call(
            norm_kernel,
            out_shape=(
                jax.ShapeDtypeStruct((rows, head_width), F32),
                jax.ShapeDtypeStruct((parts, own, features + HDIM), BF16),
            ),
            in_specs=[SMEM] + [VMEM] * 6,
            out_specs=(VMEM, VMEM),
            compiler_params=PARAMS,
        )(place, arrived, own_fold, other_fold, attended, cross, input_part)
        arrived = lax.all_to_all(sent, "tp", 0, 0, tiled=True)
    with jax.named_scope("loss"):
        mine, theirs, loss_part = pl.pallas_call(
            functools.partial(loss_kernel, width),
            out_shape=(
                query_shape,
                query_shape,
                jax.ShapeDtypeStruct((1, HDIM), F32),
            ),
            in_specs=[SMEM, SMEM] + [VMEM] * 6,
            out_specs=(VMEM, VMEM, VMEM),
            compiler_params=PARAMS,
        )(doc_lengths, place, steps, arrived, targets, own_fold, other_fold, back)
    with jax.named_scope("sent_grads"):
        grad_head = to_head(mine, theirs, core)
        sent = pl.pallas_call(
            sent_kernel,
            out_shape=jax.ShapeDtypeStruct((PAIR + STATS, HDIM), BF16),
            in_specs=[VMEM] * 4,
            out_specs=VMEM,
            compiler_params=PARAMS,
        )(grad_head, attended_head, log_total, loss_part)
        line_grads = shifted(sent, "x")
    with jax.named_scope("attention_grad"):
        sent = pl.pallas_call(
            backward_kernel,
            out_shape=jax.ShapeDtypeStruct((chips // GROUP, PAIR + STATS, 2 * HDIM), BF16),
            in_specs=[SMEM, SMEM] + [VMEM] * (2 + GROUP),
            out_specs=VMEM,
            compiler_params=PARAMS,
        )(doc_lengths, place, all_kv, line_queries, *line_grads)
        kv_grad, loss_part = pl.pallas_call(
            collect_kernel,
            out_shape=(
                jax.ShapeDtypeStruct((PAIR, 2 * HDIM), BF16),
                jax.ShapeDtypeStruct((1, HDIM), F32),
            ),
            in_specs=[VMEM],
            out_specs=(VMEM, VMEM),
            compiler_params=PARAMS,
        )(lax.all_to_all(sent, "y", 0, 0, tiled=True))
        kv_grad = to_rows(kv_grad, core)
        loss_part = loss_part[0, 0]
        loss = (loss_part + swap(loss_part)) / (seq_total * features)
    with jax.named_scope("d_context"):
        terms = pl.pallas_call(
            context_kernel,
            out_shape=jax.ShapeDtypeStruct((parts, share, rows), BF16),
            in_specs=[VMEM, ANY, VMEM, VMEM],
            out_specs=VMEM,
            compiler_params=PARAMS,
        )(kv_grad, loss.reshape(1, 1), w_key, w_value)
        d_context = pl.pallas_call(
            total_kernel,
            out_shape=jax.ShapeDtypeStruct((rows, share), BF16),
            in_specs=[VMEM],
            out_specs=VMEM,
            compiler_params=PARAMS,
        )(lax.all_to_all(terms, "tp", 0, 0, tiled=True))
    return d_context, loss


def solution(mesh):
    cores = 2
    count, parts = mesh.devices.shape
    side = math.isqrt(count // cores)
    split = Mesh(mesh.devices.reshape(side, side, cores, parts), ("y", "x", "core", "tp"))
    by_rows = P(ROWS, None)
    by_columns = P(None, "tp")
    return jax.shard_map(
        local,
        mesh=split,
        in_specs=(
            by_rows,
            by_rows,
            P(ROWS),
            P(),
            by_rows,
            P("tp"),
            by_columns,
            by_columns,
            by_columns,
            by_columns,
            P("tp", None),
            P("tp", None),
        ),
        out_specs=(P(ROWS, "tp"), P()),
        check_vma=False,
    )
```

```python
import functools
import math

import jax
import jax.numpy as jnp
from jax import lax
from jax.experimental import pallas as pl
from jax.experimental.pallas import tpu as pltpu
from jax.sharding import Mesh
from jax.sharding import PartitionSpec as P

HDIM = 128
TSTEPS = 100
MASKED = -1e30
EPSILON = 1e-06
ROWS = ("y", "x", "core")
CHIPS = ("y", "x")
SCALE = 1.0 / math.sqrt(HDIM)
PAIR = 256
GROUP = 4
FOLD_POST = 32
FOLD_OUT = 8
STATS = 16
F32 = jnp.float32
BF16 = jnp.bfloat16


def dot(a, b, contract=((1,), (0,))):
    return lax.dot_general(a, b, (contract, ((), ())), preferred_element_type=F32)


def shifted(block, axis):
    count = lax.axis_size(axis)
    routes = [[(i, (i + s) % count) for i in range(count)] for s in range(1, count)]
    return [block] + [lax.ppermute(block, axis, route) for route in routes]


def returned(blocks, axis):
    count = lax.axis_size(axis)
    routes = [[(i, (i - s) % count) for i in range(count)] for s in range(count)]
    return [blocks[0]] + [lax.ppermute(blocks[s], axis, routes[s]) for s in range(1, count)]


def around(block, axis):
    count = lax.axis_size(axis)
    up = [(i, (i + 1) % count) for i in range(count)]
    down = [(i, (i - 1) % count) for i in range(count)]
    behind, ahead = [block], [block]
    for _ in range(count // 2 - 1):
        behind.append(lax.ppermute(behind[-1], axis, up))
        ahead.append(lax.ppermute(ahead[-1], axis, down))
    half = block.shape[0] // 2
    far = [lax.ppermute(behind[-1][:half], axis, up), lax.ppermute(ahead[-1][half:], axis, down)]
    return behind + far + ahead[:0:-1]


def gathered_blocks(refs):
    half = (len(refs) - 1) // 2
    far = jnp.concatenate((refs[half][...], refs[half + 1][...]), axis=0)
    return [r[...] for r in refs[:half]] + [far] + [r[...] for r in refs[half + 2 :]]


def owner_of(place_ref, distance, parts):
    return lax.rem(place_ref[0] + (parts - distance), parts)


def swap(block):
    return lax.ppermute(block, "core", [(0, 1), (1, 0)])


def to_head(mine, theirs, core):
    first = core == 0
    got = swap(theirs)
    return jnp.concatenate((jnp.where(first, mine, got), jnp.where(first, got, mine)), axis=0)


def to_rows(block, core):
    first = core == 0
    half = block.shape[0] // 2
    top, bottom = block[:half], block[half:]
    mine = jnp.where(first, top, bottom)
    got = swap(jnp.where(first, bottom, top))
    return jnp.concatenate((jnp.where(first, mine, got), jnp.where(first, got, mine)), axis=1)


def pieces(values):
    high = values.astype(BF16)
    rest = values - high.astype(F32)
    middle = rest.astype(BF16)
    return high, middle, (rest - middle.astype(F32)).astype(BF16)


def stat_rows(*rows):
    out = []
    for row in rows:
        for piece in pieces(row):
            out += [piece[:, :HDIM].astype(F32), piece[:, HDIM:].astype(F32)]
    out.append(jnp.zeros((STATS - len(out), HDIM), F32))
    return jnp.concatenate(out, axis=0).astype(BF16)


def stat_row(block, at):
    total = block[at : at + 2] + block[at + 2 : at + 4] + block[at + 4 : at + 6]
    return jnp.concatenate((total[:1], total[1:]), axis=1)


def sine(x):
    y = x * x
    total = jnp.full_like(x, 1.0 / 6227020800.0)
    for c in (-1.0 / 39916800.0, 1.0 / 362880.0, -1.0 / 5040.0, 1.0 / 120.0, -1.0 / 6.0, 1.0):
        total = total * y + c
    return total * x


def column(row):
    return jnp.broadcast_to(row, (HDIM, HDIM)).T[:, :1]


def ends_of(lengths_ref):
    ends = [lengths_ref[0]]
    for d in range(1, lengths_ref.shape[0]):
        ends.append(ends[-1] + lengths_ref[d])
    return ends


def start_of(ends, positions):
    start = jnp.zeros_like(positions)
    for end in ends:
        start = jnp.where(positions >= end, end, start)
    return start


def fetch(pairs, sems):
    copies = [pltpu.make_async_copy(f, t, sems.at[i]) for i, (f, t) in enumerate(pairs)]
    for copy in copies:
        copy.start()
    return copies


def send_kernel(
    steps_ref,
    time_ref,
    noised_ref,
    pre_ref,
    post_ref,
    out_ref,
    sent_ref,
    noised,
    pre,
    post_part,
    out_part,
    sems,
):
    rows, features = noised.shape
    share = pre.shape[1]
    slot = lax.axis_index("core") * lax.axis_size(CHIPS)
    slot = slot + lax.axis_index("y") * lax.axis_size("x") + lax.axis_index("x")
    lanes = pl.ds(pl.multiple_of(slot // (HDIM // FOLD_POST) * HDIM, HDIM), HDIM)
    lines = pl.ds(pl.multiple_of(slot // 2 * (2 * FOLD_OUT), 2 * FOLD_OUT), 2 * FOLD_OUT)
    quarter = features // 4
    pairs = [(post_ref.at[:, lanes], post_part), (out_ref.at[lines], out_part), (noised_ref, noised)]
    pairs += [
        (pre_ref.at[pl.ds(quarter * k, quarter)], pre.at[pl.ds(quarter * k, quarter)])
        for k in range(4)
    ]
    copies = fetch(pairs, sems)
    angle = (0.5 * math.pi / TSTEPS) * steps_ref[...].astype(F32)
    noise = column(sine(angle)) * time_ref[...]
    copies[0].wait()
    post = post_part[...].astype(F32).T
    which = lax.rem(slot, HDIM // FOLD_POST)
    post_rows = post[:FOLD_POST]
    for k in range(1, HDIM // FOLD_POST):
        post_rows = jnp.where(which == k, post[FOLD_POST * k : FOLD_POST * (k + 1)], post_rows)
    copies[1].wait()
    out_rows = out_part[...].astype(F32)
    out_rows = jnp.where(lax.rem(slot, 2) == 0, out_rows[:FOLD_OUT], out_rows[FOLD_OUT:])
    parts = out_rows.shape[1] // share
    out_rows = [out_rows[:, share * k : share * (k + 1)] for k in range(parts)]
    sent_ref[rows:, :] = jnp.concatenate([post_rows] + out_rows, axis=0).astype(BF16)
    copies[2].wait()
    total = noise
    for k in range(4):
        at = slice(quarter * k, quarter * (k + 1))
        copies[3 + k].wait()
        total = total + dot(noised[:, at], pre[at])
    sent_ref[:rows, :] = total.astype(BF16)


def project_kernel(
    place_ref, context_ref, key_ref, value_ref, mine_ref, theirs_ref, context, weight, sems
):
    parts = 4
    share = context.shape[1] // parts
    pairs = []
    for k in range(parts):
        at = pl.ds(share * k, share)
        pairs.append((context_ref.at[:, at], context.at[:, at]))
        pairs.append((key_ref.at[at], weight.at[0, at]))
        pairs.append((value_ref.at[at], weight.at[1, at]))
    copies = fetch(pairs, sems)
    keys = jnp.zeros((context.shape[0], 2 * HDIM), F32)
    values = keys
    for k in range(parts):
        at = slice(share * k, share * (k + 1))
        for copy in copies[3 * k : 3 * k + 3]:
            copy.wait()
        keys = keys + dot(context[:, at], weight[0, at])
        values = values + dot(context[:, at], weight[1, at])
    left = jnp.concatenate((keys[:, :HDIM], values[:, :HDIM]), axis=1)
    right = jnp.concatenate((keys[:, HDIM:], values[:, HDIM:]), axis=1)
    first = place_ref[2] == 0
    mine_ref[...] = jnp.where(first, left, right).astype(BF16)
    theirs_ref[...] = jnp.where(first, right, left).astype(BF16)


def gathered_kernel(place_ref, w_query_ref, w_out_ref, hold_ref, *refs):
    *block_refs, mine_ref, theirs_ref, cross_ref, folded_ref, near, sems = refs
    rows = mine_ref.shape[0]
    heads, width = w_out_ref.shape
    near_refs = (block_refs[1], block_refs[-1])
    near_copies = fetch([(ref, near.at[k]) for k, ref in enumerate(near_refs)], sems)
    half = (len(block_refs) - 1) // 2
    parts = len(block_refs) - 1
    far = jnp.concatenate((block_refs[half][...], block_refs[half + 1][...]), axis=0)
    blocks = {0: block_refs[0][...], half: far}
    for k in range(2, half):
        blocks[k] = block_refs[k][...]
    for k in range(half + 1, parts - 1):
        blocks[k] = block_refs[k + 1][...]
    share = far.shape[1]
    top = rows + FOLD_POST

    def against(total, weight_of, distance, count):
        owner = owner_of(place_ref, distance, parts)
        at = pl.ds(pl.multiple_of(owner * share, share), share)
        return total + weight_of(blocks[distance][:count], at)

    def by_out(block, at):
        return dot(block, w_out_ref[:, at], ((1,), (1,)))

    def by_query(block, at):
        return dot(block, w_query_ref[at, :])

    both = jnp.zeros((top, heads), F32)
    for distance in list(blocks):
        both = against(both, by_out, distance, top)
    for copy in near_copies:
        copy.wait()
    for k, distance in enumerate((1, parts - 1)):
        blocks[distance] = near[k]
        both = against(both, by_out, distance, top)
    cross_ref[...] = both[:rows]
    span = FOLD_OUT * parts
    slices = jnp.concatenate([blocks[k][top:] for k in range(parts)], axis=0)
    gram = [jnp.zeros((FOLD_OUT, heads), F32)] * parts
    for k in range(parts):
        product = by_out(slices, slice(share * k, share * (k + 1)))
        for b in range(parts):
            at = span * b + FOLD_OUT * k
            gram[b] = gram[b] + product[at : at + FOLD_OUT]
    folded = jnp.concatenate([both[rows:]] + gram, axis=0).astype(BF16)
    for k in range(folded_ref.shape[0]):
        folded_ref[k] = folded

    squares = jnp.zeros((rows, 1), F32)
    query = jnp.zeros((rows, heads), F32)
    for distance in range(parts):
        wide = blocks[distance][:rows].astype(F32)
        squares = squares + jnp.sum(wide * wide, axis=1, keepdims=True)
        query = against(query, by_query, distance, rows)
    query = (query * lax.rsqrt(squares / width + EPSILON)).astype(BF16)
    first = place_ref[2] == 0
    mine_ref[...] = jnp.where(first, query[:, :HDIM], query[:, HDIM:])
    theirs_ref[...] = jnp.where(first, query[:, HDIM:], query[:, :HDIM])


def post_kernel(sent_ref, post_ref, hold_ref, input_ref, input_post_ref):
    features = sent_ref[: input_ref.shape[0], :]
    input_ref[...] = features
    input_post_ref[...] = dot(features, post_ref[...])


def line_positions(place_ref):
    row = place_ref[1] // GROUP
    here = lax.rem(place_ref[1], GROUP)
    chips = [row * GROUP + lax.rem(here + (GROUP - k), GROUP) for k in range(GROUP)]
    lanes = lax.broadcasted_iota(jnp.int32, (1, PAIR), 1)
    return jnp.concatenate([chip * PAIR + lanes for chip in chips], axis=1)


def key_steps(place_ref, ends):
    row = place_ref[1] // GROUP
    here = lax.rem(place_ref[1], GROUP)
    floor = start_of(ends, row * (GROUP * PAIR))
    past = jnp.maximum(floor - (here * PAIR + PAIR - 1), 0)
    lowest = (past + GROUP * PAIR - 1) // (GROUP * PAIR)
    return row - lowest + 1


def allowed_pairs(place_ref, step, query_start, query_pos):
    base = (place_ref[1] - step * GROUP) * PAIR
    key_pos = base + lax.broadcasted_iota(jnp.int32, (PAIR, query_pos.shape[1]), 0)
    return (key_pos >= query_start) & (key_pos <= query_pos)


def forward_kernel(lengths_ref, place_ref, q_ref, kv_ref, hold_ref, out_ref):
    ends = ends_of(lengths_ref)
    width = GROUP * PAIR
    query_pos = line_positions(place_ref)
    query_start = start_of(ends, query_pos)
    q = q_ref[...].reshape(width, HDIM)

    def body(step, carry):
        row_max, row_total, weighted = carry
        scores = dot(kv_ref[step, :, :HDIM], q, ((1,), (1,))) * SCALE
        scores = jnp.where(allowed_pairs(place_ref, step, query_start, query_pos), scores, MASKED)
        new_max = jnp.maximum(row_max, jnp.max(scores, axis=0, keepdims=True))
        probs = jnp.exp(scores - new_max)
        fading = jnp.exp(row_max - new_max)
        row_total = row_total * fading + jnp.sum(probs, axis=0, keepdims=True)
        weighted = weighted * fading + dot(kv_ref[step, :, HDIM:], probs.astype(BF16), ((0,), (0,)))
        return new_max, row_total, weighted

    row_max, row_total, weighted = lax.fori_loop(
        0,
        key_steps(place_ref, ends),
        body,
        (
            jnp.full((1, width), MASKED, F32),
            jnp.zeros((1, width), F32),
            jnp.zeros((HDIM, width), F32),
        ),
    )
    out = (weighted / row_total).T.astype(BF16)
    log_total = row_max + jnp.log(row_total)
    for k in range(GROUP):
        at = slice(PAIR * k, PAIR * (k + 1))
        out_ref[k, :PAIR, :] = out[at]
        out_ref[k, PAIR:, :] = stat_rows(log_total[:, at])


def merge_kernel(*refs):
    *part_refs, out_ref, total_ref = refs
    logs = [stat_row(ref[PAIR:, :].astype(F32), 0) for ref in part_refs]
    top = functools.reduce(jnp.maximum, logs)
    log_total = top + jnp.log(functools.reduce(jnp.add, [jnp.exp(x - top) for x in logs]))
    out = jnp.zeros((PAIR, HDIM), F32)
    for x, ref in zip(logs, part_refs):
        weight = jnp.broadcast_to(jnp.exp(x - log_total), (HDIM, PAIR)).T
        out = out + weight * ref[:PAIR, :].astype(F32)
    out_ref[...] = out.astype(BF16)
    total_ref[...] = log_total


def both_cores(place_ref, own_ref, other_ref, count):
    own = own_ref[:, :count, :].reshape(-1, own_ref.shape[2])
    other = other_ref[:, :count, :].reshape(-1, other_ref.shape[2])
    first = place_ref[2] == 0
    return jnp.where(first, own, other), jnp.where(first, other, own)


def raw_kernel(place_ref, attended_ref, own_ref, other_ref, input_ref, hold_ref, out_ref):
    parts, own, _ = out_ref.shape
    attended = attended_ref[...]
    low, high = both_cores(place_ref, own_ref, other_ref, FOLD_POST)
    half = low.shape[0]
    raw_low = (dot(attended, low, ((1,), (1,))) + input_ref[:, :half]).astype(BF16)
    raw_high = (dot(attended, high, ((1,), (1,))) + input_ref[:, half:]).astype(BF16)
    packed = jnp.concatenate([attended[own * k : own * (k + 1)] for k in range(parts)], axis=1)
    for k in range(parts):
        out_ref[k, :, :half] = raw_low[own * k : own * (k + 1)]
        out_ref[k, :, half : 2 * half] = raw_high[own * k : own * (k + 1)]
        out_ref[k, :, 2 * half :] = packed


def norm_kernel(
    place_ref,
    arrived_ref,
    own_ref,
    other_ref,
    attended_ref,
    cross_ref,
    input_ref,
    back_ref,
    out_ref,
):
    parts, own, _ = arrived_ref.shape
    features = out_ref.shape[2] - HDIM
    rows, share = input_ref.shape
    wide = attended_ref.shape[1]
    total = arrived_ref[0, :, :features].astype(F32)
    for k in range(1, parts):
        total = total + arrived_ref[k, :, :features].astype(F32)
    cross = cross_ref[...]
    back = jnp.zeros_like(cross)
    first = place_ref[2] == 0
    chips = own_ref.shape[0]
    grams = []
    for ref in (own_ref, other_ref):
        gram = ref[:, FOLD_POST:, :].astype(F32)
        grams.append(gram.reshape(chips, parts, FOLD_OUT, wide))
    for distance in range(parts):
        k = owner_of(place_ref, distance, parts)
        theirs = jnp.concatenate(
            [
                arrived_ref[k, :, features + wide * j : features + wide * (j + 1)]
                for j in range(parts)
            ],
            axis=0,
        )
        half = chips * FOLD_OUT
        own_gram, other_gram = (g[:, distance].reshape(half, wide).astype(BF16) for g in grams)
        back = back + dot(theirs[:, :half], jnp.where(first, own_gram, other_gram))
        back = back + dot(theirs[:, half:], jnp.where(first, other_gram, own_gram))
    back_ref[...] = cross + back
    attended = attended_ref[...].astype(F32)
    features_in = input_ref[...].astype(F32)
    squares = jnp.sum((attended * (2.0 * cross + back)).T, axis=0, keepdims=True) + jnp.sum(
        (features_in * features_in).T, axis=0, keepdims=True
    )
    side = jnp.concatenate(pieces(squares) + (jnp.zeros((own - 3, HDIM), BF16),), axis=0)
    summed = total.astype(BF16)
    for k in range(parts):
        out_ref[k, :, :features] = summed
        out_ref[k, :, features:] = side


def loss_kernel(
    width,
    lengths_ref,
    place_ref,
    steps_ref,
    arrived_ref,
    target_ref,
    own_ref,
    other_ref,
    back_ref,
    mine_ref,
    theirs_ref,
    loss_ref,
):
    parts, own, _ = arrived_ref.shape
    rows, features = target_ref.shape
    position = (place_ref[1] * 2 + place_ref[2]) * rows
    position = position + lax.broadcasted_iota(jnp.int32, (1, rows), 1)
    angle = (0.5 * math.pi / TSTEPS) * steps_ref[...].astype(F32)
    keep_level = sine(0.5 * math.pi - angle)
    weight = 1.0 + keep_level * keep_level
    for end in ends_of(lengths_ref):
        weight = jnp.where(position + 1 == end, 0.0, weight)
    side = arrived_ref[:, :, features:].astype(F32)
    squares = jnp.sum(jnp.sum(side, axis=0), axis=0, keepdims=True)
    inverse = column(lax.rsqrt(jnp.maximum(squares / width, 0.0) + EPSILON))
    prediction = arrived_ref[:, :, :features].reshape(rows, features).astype(F32) * inverse
    missed = prediction - target_ref[...].astype(F32)
    weighted_missed = column(weight) * missed
    loss = jnp.sum(weighted_missed * missed, axis=1, keepdims=True)
    loss_ref[...] = jnp.broadcast_to(jnp.sum(loss, axis=0, keepdims=True), (1, HDIM))
    pred_grad = weighted_missed.astype(BF16)
    along = jnp.sum(pred_grad.astype(F32) * prediction, axis=1, keepdims=True) / width
    low, high = both_cores(place_ref, own_ref, other_ref, FOLD_POST)
    half = low.shape[0]
    direct = dot(pred_grad[:, :half], low) + dot(pred_grad[:, half:], high)
    grad = (inverse * (direct - along * inverse * back_ref[...])).astype(BF16)
    first = place_ref[2] == 0
    mine_ref[...] = jnp.where(first, grad[:, :HDIM], grad[:, HDIM:])
    theirs_ref[...] = jnp.where(first, grad[:, HDIM:], grad[:, :HDIM])


def sent_kernel(grad_ref, attended_ref, total_ref, loss_ref, out_ref):
    grad = grad_ref[...]
    product = grad.astype(F32) * attended_ref[...].astype(F32)
    output_dot = jnp.sum(product.T, axis=0, keepdims=True)
    stats = stat_rows(total_ref[...], output_dot).astype(F32)
    loss_rows = [p.astype(F32) for p in pieces(loss_ref[...])]
    stats = jnp.concatenate([stats[:12]] + loss_rows + [stats[15:]], axis=0)
    out_ref[:PAIR, :] = grad
    out_ref[PAIR:, :] = stats.astype(BF16)


def backward_kernel(lengths_ref, place_ref, kv_ref, q_ref, *refs):
    *sent_refs, out_ref = refs
    ends = ends_of(lengths_ref)
    width = GROUP * PAIR
    query_pos = line_positions(place_ref)
    query_start = start_of(ends, query_pos)
    q = q_ref[...].reshape(width, HDIM)
    grad = jnp.concatenate([ref[:PAIR, :] for ref in sent_refs], axis=0)
    stats = [ref[PAIR:, :].astype(F32) for ref in sent_refs]
    log_total = jnp.concatenate([stat_row(x, 0) for x in stats], axis=1)
    output_dot = jnp.concatenate([stat_row(x, 6) for x in stats], axis=1)
    loss = functools.reduce(jnp.add, [x[12:13] + x[13:14] + x[14:15] for x in stats])
    tail = jnp.concatenate(
        [p.astype(F32) for p in pieces(loss)] + [jnp.zeros((STATS - 3, HDIM), F32)], axis=0
    )
    tail = jnp.concatenate((tail, tail), axis=1).astype(BF16)
    steps = key_steps(place_ref, ends)
    for step in range(out_ref.shape[0]):
        row = lax.rem(place_ref[1] // GROUP + (out_ref.shape[0] - step), out_ref.shape[0])
        out_ref[row, PAIR:, :] = tail

        @pl.when(step < steps)
        def _():
            allowed = allowed_pairs(place_ref, step, query_start, query_pos)
            scores = dot(kv_ref[step, :, :HDIM], q, ((1,), (1,))) * SCALE
            probs = jnp.where(allowed, jnp.exp(scores - log_total), 0.0)
            out_ref[row, :PAIR, HDIM:] = dot(probs.astype(BF16), grad).astype(BF16)
            prob_grad = dot(kv_ref[step, :, HDIM:], grad, ((1,), (1,)))
            score_grad = (probs * (prob_grad - output_dot) * SCALE).astype(BF16)
            out_ref[row, :PAIR, :HDIM] = dot(score_grad, q).astype(BF16)

        @pl.when(step >= steps)
        def _():
            out_ref[row, :PAIR, :] = jnp.zeros((PAIR, 2 * HDIM), BF16)


def collect_kernel(*refs):
    arrived_ref, out_ref, loss_ref = refs
    parts = [arrived_ref[k].astype(F32) for k in range(arrived_ref.shape[0])]
    total = functools.reduce(jnp.add, parts)
    out_ref[...] = total[:PAIR].astype(BF16)
    rows = total[PAIR : PAIR + 3, :HDIM]
    loss_ref[...] = jnp.sum(rows, axis=0, keepdims=True)


def context_kernel(grad_ref, hold_ref, key_ref, value_ref, out_ref):
    grad = grad_ref[...].astype(F32).T.astype(BF16)
    key_grad = jnp.concatenate((grad[:HDIM], grad[2 * HDIM : 3 * HDIM]), axis=0)
    value_grad = jnp.concatenate((grad[HDIM : 2 * HDIM], grad[3 * HDIM :]), axis=0)
    parts, share, _ = out_ref.shape
    for k in range(parts):
        at = slice(share * k, share * (k + 1))
        total = dot(key_ref[at], key_grad) + dot(value_ref[at], value_grad)
        out_ref[k] = total.astype(BF16)


def total_kernel(arrived_ref, out_ref):
    parts = [arrived_ref[k].astype(F32) for k in range(arrived_ref.shape[0])]
    out_ref[...] = functools.reduce(jnp.add, parts).T.astype(BF16)


SMEM = pl.BlockSpec(memory_space=pltpu.SMEM)
HBM = pl.BlockSpec(memory_space=pltpu.HBM)
ANY = pl.BlockSpec(memory_space=pl.ANY)
VMEM = pl.BlockSpec(memory_space=pltpu.VMEM)
PARAMS = pltpu.CompilerParams(vmem_limit_bytes=32 * 1024 * 1024)
WHOLE = pltpu.CompilerParams(vmem_limit_bytes=60 * 1024 * 1024)


def local(
    concepts,
    noised,
    step_ids,
    doc_lengths,
    context,
    time_vec,
    w_pre,
    w_query,
    w_key,
    w_value,
    w_out,
    w_post,
):
    rows, features = concepts.shape
    parts = lax.axis_size("tp")
    chips = lax.axis_size(CHIPS)
    core = lax.axis_index("core")
    part = lax.axis_index("tp")
    seq_total = rows * lax.axis_size(ROWS)
    share = w_post.shape[0]
    own = rows // parts
    chip = lax.axis_index(CHIPS)
    place = jnp.stack((part, chip, core, chips)).astype(jnp.int32)
    width = share * parts
    head_width = w_out.shape[0]
    fold_rows = FOLD_POST + FOLD_OUT * parts
    steps = step_ids.reshape(1, rows)

    with jax.named_scope("inputs"):
        sent = pl.pallas_call(
            send_kernel,
            out_shape=jax.ShapeDtypeStruct((rows + fold_rows, share), BF16),
            in_specs=[VMEM, VMEM, HBM, HBM, HBM, HBM],
            out_specs=VMEM,
            scratch_shapes=[
                pltpu.VMEM((rows, features), BF16),
                pltpu.VMEM((features, share), BF16),
                pltpu.VMEM((share, HDIM), BF16),
                pltpu.VMEM((2 * FOLD_OUT, width), BF16),
                pltpu.SemaphoreType.DMA((7,)),
            ],
            compiler_params=WHOLE,
        )(steps, time_vec.reshape(1, share), noised, w_pre, w_post, w_out)
        blocks = around(sent, "tp")
    with jax.named_scope("keys_values"):
        kv_shape = jax.ShapeDtypeStruct((rows, 2 * HDIM), BF16)
        mine, theirs = pl.pallas_call(
            project_kernel,
            out_shape=(kv_shape, kv_shape),
            in_specs=[SMEM, HBM, HBM, HBM],
            out_specs=(VMEM, VMEM),
            scratch_shapes=[
                pltpu.VMEM(context.shape, BF16),
                pltpu.VMEM((2,) + w_key.shape, BF16),
                pltpu.SemaphoreType.DMA((12,)),
            ],
            compiler_params=PARAMS,
        )(place, context, w_key, w_value)
        own_kv = to_head(mine, theirs, core)
        all_kv = jnp.stack(shifted(own_kv, "y"))
    with jax.named_scope("targets"):
        count = lax.axis_size(ROWS)
        following = lax.ppermute(concepts[:1], ROWS, [(i + 1, i) for i in range(count - 1)])
        targets = jnp.concatenate((concepts[1:], following), axis=0)
    with jax.named_scope("gathered"):
        query_shape = jax.ShapeDtypeStruct((rows, HDIM), BF16)
        mine, theirs, cross, folded = pl.pallas_call(
            gathered_kernel,
            out_shape=(
                query_shape,
                query_shape,
                jax.ShapeDtypeStruct((rows, head_width), F32),
                jax.ShapeDtypeStruct((chips, fold_rows, head_width), BF16),
            ),
            in_specs=[SMEM, VMEM, VMEM, ANY, VMEM, ANY] + [VMEM] * (len(blocks) - 3) + [ANY],
            out_specs=(VMEM,) * 4,
            scratch_shapes=[
                pltpu.VMEM((2,) + sent.shape, BF16),
                pltpu.SemaphoreType.DMA((2,)),
            ],
            compiler_params=PARAMS,
        )(place, w_query, w_out, all_kv, *blocks)
        query_head = to_head(mine, theirs, core)
        line_queries = jnp.stack(shifted(query_head, "x"))
        input_part, input_post = pl.pallas_call(
            post_kernel,
            out_shape=(
                jax.ShapeDtypeStruct((rows, share), BF16),
                jax.ShapeDtypeStruct((rows, features), F32),
            ),
            in_specs=[VMEM, VMEM, ANY],
            out_specs=(VMEM, VMEM),
            compiler_params=PARAMS,
        )(sent, w_post, query_head)
        own_fold = lax.all_to_all(folded, CHIPS, 0, 0, tiled=True)
        other_fold = swap(own_fold)
    with jax.named_scope("attention"):
        sent = pl.pallas_call(
            forward_kernel,
            out_shape=jax.ShapeDtypeStruct((GROUP, PAIR + STATS, HDIM), BF16),
            in_specs=[SMEM, SMEM, VMEM, VMEM, ANY],
            out_specs=VMEM,
            compiler_params=PARAMS,
        )(doc_lengths, place, line_queries, all_kv, input_post)
        attended_head, log_total = pl.pallas_call(
            merge_kernel,
            out_shape=(
                jax.ShapeDtypeStruct((PAIR, HDIM), BF16),
                jax.ShapeDtypeStruct((1, PAIR), F32),
            ),
            in_specs=[VMEM] * GROUP,
            out_specs=(VMEM, VMEM),
            compiler_params=PARAMS,
        )(*returned(sent, "x"))
        attended = to_rows(attended_head, core)
    with jax.named_scope("raw"):
        sent = pl.pallas_call(
            raw_kernel,
            out_shape=jax.ShapeDtypeStruct((parts, own, features + head_width * parts), BF16),
            in_specs=[SMEM, VMEM, VMEM, VMEM, VMEM, ANY],
            out_specs=VMEM,
            compiler_params=PARAMS,
        )(place, attended, own_fold, other_fold, input_post, targets)
        arrived = lax.all_to_all(sent, "tp", 0, 0, tiled=True)
    with jax.named_scope("norm"):
        back, sent = pl.pallas_call(
            norm_kernel,
            out_shape=(
                jax.ShapeDtypeStruct((rows, head_width), F32),
                jax.ShapeDtypeStruct((parts, own, features + HDIM), BF16),
            ),
            in_specs=[SMEM] + [VMEM] * 6,
            out_specs=(VMEM, VMEM),
            compiler_params=PARAMS,
        )(place, arrived, own_fold, other_fold, attended, cross, input_part)
        arrived = lax.all_to_all(sent, "tp", 0, 0, tiled=True)
    with jax.named_scope("loss"):
        mine, theirs, loss_part = pl.pallas_call(
            functools.partial(loss_kernel, width),
            out_shape=(
                query_shape,
                query_shape,
                jax.ShapeDtypeStruct((1, HDIM), F32),
            ),
            in_specs=[SMEM, SMEM] + [VMEM] * 6,
            out_specs=(VMEM, VMEM, VMEM),
            compiler_params=PARAMS,
        )(doc_lengths, place, steps, arrived, targets, own_fold, other_fold, back)
    with jax.named_scope("sent_grads"):
        grad_head = to_head(mine, theirs, core)
        sent = pl.pallas_call(
            sent_kernel,
            out_shape=jax.ShapeDtypeStruct((PAIR + STATS, HDIM), BF16),
            in_specs=[VMEM] * 4,
            out_specs=VMEM,
            compiler_params=PARAMS,
        )(grad_head, attended_head, log_total, loss_part)
        line_grads = shifted(sent, "x")
    with jax.named_scope("attention_grad"):
        sent = pl.pallas_call(
            backward_kernel,
            out_shape=jax.ShapeDtypeStruct((chips // GROUP, PAIR + STATS, 2 * HDIM), BF16),
            in_specs=[SMEM, SMEM] + [VMEM] * (2 + GROUP),
            out_specs=VMEM,
            compiler_params=PARAMS,
        )(doc_lengths, place, all_kv, line_queries, *line_grads)
        kv_grad, loss_part = pl.pallas_call(
            collect_kernel,
            out_shape=(
                jax.ShapeDtypeStruct((PAIR, 2 * HDIM), BF16),
                jax.ShapeDtypeStruct((1, HDIM), F32),
            ),
            in_specs=[VMEM],
            out_specs=(VMEM, VMEM),
            compiler_params=PARAMS,
        )(lax.all_to_all(sent, "y", 0, 0, tiled=True))
        kv_grad = to_rows(kv_grad, core)
        loss_part = loss_part[0, 0]
        loss = (loss_part + swap(loss_part)) / (seq_total * features)
    with jax.named_scope("d_context"):
        terms = pl.pallas_call(
            context_kernel,
            out_shape=jax.ShapeDtypeStruct((parts, share, rows), BF16),
            in_specs=[VMEM, ANY, VMEM, VMEM],
            out_specs=VMEM,
            compiler_params=PARAMS,
        )(kv_grad, loss.reshape(1, 1), w_key, w_value)
        d_context = pl.pallas_call(
            total_kernel,
            out_shape=jax.ShapeDtypeStruct((rows, share), BF16),
            in_specs=[VMEM],
            out_specs=VMEM,
            compiler_params=PARAMS,
        )(lax.all_to_all(terms, "tp", 0, 0, tiled=True))
    return d_context, loss


def solution(mesh):
    cores = 2
    count, parts = mesh.devices.shape
    side = math.isqrt(count // cores)
    split = Mesh(mesh.devices.reshape(side, side, cores, parts), ("y", "x", "core", "tp"))
    by_rows = P(ROWS, None)
    by_columns = P(None, "tp")
    return jax.shard_map(
        local,
        mesh=split,
        in_specs=(
            by_rows,
            by_rows,
            P(ROWS),
            P(),
            by_rows,
            P("tp"),
            by_columns,
            by_columns,
            by_columns,
            by_columns,
            P("tp", None),
            P("tp", None),
        ),
        out_specs=(P(ROWS, "tp"), P()),
        check_vma=False,
    )
```

```python
import functools
import math

import jax
import jax.numpy as jnp
from jax import lax
from jax.experimental import pallas as pl
from jax.experimental.pallas import tpu as pltpu
from jax.sharding import Mesh
from jax.sharding import PartitionSpec as P

HDIM = 128
TSTEPS = 100
MASKED = -1e30
EPSILON = 1e-06
ROWS = ("y", "x", "core")
CHIPS = ("y", "x")
SCALE = 1.0 / math.sqrt(HDIM)
LOG2E = math.log2(math.e)
PAIR = 256
GROUP = 4
FOLD_POST = 32
FOLD_OUT = 8
STATS = 16
F32 = jnp.float32
BF16 = jnp.bfloat16


def dot(a, b, contract=((1,), (0,))):
    return lax.dot_general(a, b, (contract, ((), ())), preferred_element_type=F32)


def shifted(block, axis):
    count = lax.axis_size(axis)
    routes = [[(i, (i + s) % count) for i in range(count)] for s in range(1, count)]
    return [block] + [lax.ppermute(block, axis, route) for route in routes]


def returned(blocks, axis):
    count = lax.axis_size(axis)
    routes = [[(i, (i - s) % count) for i in range(count)] for s in range(count)]
    return [blocks[0]] + [lax.ppermute(blocks[s], axis, routes[s]) for s in range(1, count)]


def around(block, axis):
    count = lax.axis_size(axis)
    up = [(i, (i + 1) % count) for i in range(count)]
    down = [(i, (i - 1) % count) for i in range(count)]
    behind, ahead = [block], [block]
    for _ in range(count // 2 - 1):
        behind.append(lax.ppermute(behind[-1], axis, up))
        ahead.append(lax.ppermute(ahead[-1], axis, down))
    half = block.shape[0] // 2
    far = [lax.ppermute(behind[-1][:half], axis, up), lax.ppermute(ahead[-1][half:], axis, down)]
    return behind + far + ahead[:0:-1]


def gathered_blocks(refs):
    half = (len(refs) - 1) // 2
    far = jnp.concatenate((refs[half][...], refs[half + 1][...]), axis=0)
    return [r[...] for r in refs[:half]] + [far] + [r[...] for r in refs[half + 2 :]]


def owner_of(place_ref, distance, parts):
    return lax.rem(place_ref[0] + (parts - distance), parts)


def swap(block):
    return lax.ppermute(block, "core", [(0, 1), (1, 0)])


def to_head(mine, theirs, core):
    first = core == 0
    got = swap(theirs)
    return jnp.concatenate((jnp.where(first, mine, got), jnp.where(first, got, mine)), axis=0)


def to_rows(block, core):
    first = core == 0
    half = block.shape[0] // 2
    top, bottom = block[:half], block[half:]
    mine = jnp.where(first, top, bottom)
    got = swap(jnp.where(first, bottom, top))
    return jnp.concatenate((jnp.where(first, mine, got), jnp.where(first, got, mine)), axis=1)


def pieces(values):
    high = values.astype(BF16)
    rest = values - high.astype(F32)
    middle = rest.astype(BF16)
    return high, middle, (rest - middle.astype(F32)).astype(BF16)


def stat_rows(*rows):
    out = []
    for row in rows:
        for piece in pieces(row):
            out += [piece[:, :HDIM].astype(F32), piece[:, HDIM:].astype(F32)]
    out.append(jnp.zeros((STATS - len(out), HDIM), F32))
    return jnp.concatenate(out, axis=0).astype(BF16)


def stat_row(block, at):
    total = block[at : at + 2] + block[at + 2 : at + 4] + block[at + 4 : at + 6]
    return jnp.concatenate((total[:1], total[1:]), axis=1)


def sine(x):
    y = x * x
    total = jnp.full_like(x, 1.0 / 6227020800.0)
    for c in (-1.0 / 39916800.0, 1.0 / 362880.0, -1.0 / 5040.0, 1.0 / 120.0, -1.0 / 6.0, 1.0):
        total = total * y + c
    return total * x


def column(row):
    return jnp.broadcast_to(row, (HDIM, HDIM)).T[:, :1]


def ends_of(lengths_ref):
    ends = [lengths_ref[0]]
    for d in range(1, lengths_ref.shape[0]):
        ends.append(ends[-1] + lengths_ref[d])
    return ends


def start_of(ends, positions):
    start = jnp.zeros_like(positions)
    for end in ends:
        start = jnp.where(positions >= end, end, start)
    return start


def fetch(pairs, sems):
    copies = [pltpu.make_async_copy(f, t, sems.at[i]) for i, (f, t) in enumerate(pairs)]
    for copy in copies:
        copy.start()
    return copies


def send_kernel(
    steps_ref,
    time_ref,
    noised_ref,
    pre_ref,
    post_ref,
    out_ref,
    sent_ref,
    noised,
    pre,
    post_part,
    out_part,
    sems,
):
    rows, features = noised.shape
    share = pre.shape[1]
    slot = lax.axis_index("core") * lax.axis_size(CHIPS)
    slot = slot + lax.axis_index("y") * lax.axis_size("x") + lax.axis_index("x")
    lanes = pl.ds(pl.multiple_of(slot // (HDIM // FOLD_POST) * HDIM, HDIM), HDIM)
    lines = pl.ds(pl.multiple_of(slot // 2 * (2 * FOLD_OUT), 2 * FOLD_OUT), 2 * FOLD_OUT)
    quarter = features // 4
    pairs = [(post_ref.at[:, lanes], post_part), (out_ref.at[lines], out_part), (noised_ref, noised)]
    pairs += [
        (pre_ref.at[pl.ds(quarter * k, quarter)], pre.at[pl.ds(quarter * k, quarter)])
        for k in range(4)
    ]
    copies = fetch(pairs, sems)
    angle = (0.5 * math.pi / TSTEPS) * steps_ref[...].astype(F32)
    noise = column(sine(angle)) * time_ref[...]
    copies[0].wait()
    post = post_part[...].astype(F32).T
    which = lax.rem(slot, HDIM // FOLD_POST)
    post_rows = post[:FOLD_POST]
    for k in range(1, HDIM // FOLD_POST):
        post_rows = jnp.where(which == k, post[FOLD_POST * k : FOLD_POST * (k + 1)], post_rows)
    copies[1].wait()
    out_rows = out_part[...].astype(F32)
    out_rows = jnp.where(lax.rem(slot, 2) == 0, out_rows[:FOLD_OUT], out_rows[FOLD_OUT:])
    parts = out_rows.shape[1] // share
    out_rows = [out_rows[:, share * k : share * (k + 1)] for k in range(parts)]
    sent_ref[rows:, :] = jnp.concatenate([post_rows] + out_rows, axis=0).astype(BF16)
    copies[2].wait()
    total = noise
    for k in range(4):
        at = slice(quarter * k, quarter * (k + 1))
        copies[3 + k].wait()
        total = total + dot(noised[:, at], pre[at])
    sent_ref[:rows, :] = total.astype(BF16)


def project_kernel(
    place_ref, context_ref, key_ref, value_ref, mine_ref, theirs_ref, context, weight, sems
):
    parts = 4
    share = context.shape[1] // parts
    pairs = []
    for k in range(parts):
        at = pl.ds(share * k, share)
        pairs.append((context_ref.at[:, at], context.at[:, at]))
        pairs.append((key_ref.at[at], weight.at[0, at]))
        pairs.append((value_ref.at[at], weight.at[1, at]))
    copies = fetch(pairs, sems)
    keys = jnp.zeros((context.shape[0], 2 * HDIM), F32)
    values = keys
    for k in range(parts):
        at = slice(share * k, share * (k + 1))
        for copy in copies[3 * k : 3 * k + 3]:
            copy.wait()
        keys = keys + dot(context[:, at], weight[0, at])
        values = values + dot(context[:, at], weight[1, at])
    left = jnp.concatenate((keys[:, :HDIM], values[:, :HDIM]), axis=1)
    right = jnp.concatenate((keys[:, HDIM:], values[:, HDIM:]), axis=1)
    first = place_ref[2] == 0
    mine_ref[...] = jnp.where(first, left, right).astype(BF16)
    theirs_ref[...] = jnp.where(first, right, left).astype(BF16)


def gathered_kernel(place_ref, w_query_ref, w_out_ref, hold_ref, *refs):
    *block_refs, mine_ref, theirs_ref, cross_ref, folded_ref, near, sems = refs
    rows = mine_ref.shape[0]
    heads, width = w_out_ref.shape
    near_refs = (block_refs[1], block_refs[-1])
    near_copies = fetch([(ref, near.at[k]) for k, ref in enumerate(near_refs)], sems)
    half = (len(block_refs) - 1) // 2
    parts = len(block_refs) - 1
    far = jnp.concatenate((block_refs[half][...], block_refs[half + 1][...]), axis=0)
    blocks = {0: block_refs[0][...], half: far}
    for k in range(2, half):
        blocks[k] = block_refs[k][...]
    for k in range(half + 1, parts - 1):
        blocks[k] = block_refs[k + 1][...]
    share = far.shape[1]
    top = rows + FOLD_POST

    def against(total, weight_of, distance, count):
        owner = owner_of(place_ref, distance, parts)
        at = pl.ds(pl.multiple_of(owner * share, share), share)
        return total + weight_of(blocks[distance][:count], at)

    def by_out(block, at):
        return dot(block, w_out_ref[:, at], ((1,), (1,)))

    def by_query(block, at):
        return dot(block, w_query_ref[at, :])

    both = jnp.zeros((top, heads), F32)
    squares = jnp.zeros((rows, 1), F32)
    query = jnp.zeros((rows, heads), F32)
    for step, distance in enumerate(list(blocks) + [1, parts - 1]):
        if step >= parts - 2:
            near_copies[step - parts + 2].wait()
            blocks[distance] = near[step - parts + 2]
        wide = blocks[distance][:rows].astype(F32)
        squares = squares + jnp.sum(wide * wide, axis=1, keepdims=True)
        both = against(both, by_out, distance, top)
        query = against(query, by_query, distance, rows)
    cross_ref[...] = both[:rows]
    span = FOLD_OUT * parts
    slices = [blocks[k][top:].astype(F32) for k in range(parts)]
    gram = jnp.zeros((span, heads), F32)
    for k in range(parts):
        at = slice(FOLD_OUT * k, FOLD_OUT * (k + 1))
        chunk = jnp.concatenate([block[at] for block in slices], axis=0).astype(BF16)
        gram = gram + by_out(chunk, slice(share * k, share * (k + 1)))
    folded = jnp.concatenate((both[rows:], gram), axis=0).astype(BF16)
    for k in range(folded_ref.shape[0]):
        folded_ref[k] = folded

    query = (query * lax.rsqrt(squares / width + EPSILON)).astype(BF16)
    first = place_ref[2] == 0
    mine_ref[...] = jnp.where(first, query[:, :HDIM], query[:, HDIM:])
    theirs_ref[...] = jnp.where(first, query[:, HDIM:], query[:, :HDIM])


def post_kernel(sent_ref, post_ref, hold_ref, input_ref, input_post_ref):
    features = sent_ref[: input_ref.shape[0], :]
    input_ref[...] = features
    input_post_ref[...] = dot(features, post_ref[...])


def line_positions(place_ref):
    row = place_ref[1] // GROUP
    here = lax.rem(place_ref[1], GROUP)
    chips = [row * GROUP + lax.rem(here + (GROUP - k), GROUP) for k in range(GROUP)]
    lanes = lax.broadcasted_iota(jnp.int32, (1, PAIR), 1)
    return jnp.concatenate([chip * PAIR + lanes for chip in chips], axis=1)


def key_steps(place_ref, ends):
    row = place_ref[1] // GROUP
    here = lax.rem(place_ref[1], GROUP)
    floor = start_of(ends, row * (GROUP * PAIR))
    past = jnp.maximum(floor - (here * PAIR + PAIR - 1), 0)
    lowest = (past + GROUP * PAIR - 1) // (GROUP * PAIR)
    return row - lowest + 1


def allowed_pairs(place_ref, step, query_start, query_pos):
    base = (place_ref[1] - step * GROUP) * PAIR
    key_pos = base + lax.broadcasted_iota(jnp.int32, (PAIR, query_pos.shape[1]), 0)
    return (key_pos >= query_start) & (key_pos <= query_pos)


def unmasked(place_ref, ends, step):
    row = place_ref[1] // GROUP
    first_key = (place_ref[1] - step * GROUP) * PAIR
    return (step > 0) & (start_of(ends, (row + 1) * (GROUP * PAIR) - 1) <= first_key)


def forward_kernel(lengths_ref, place_ref, q_ref, kv_ref, hold_ref, out_ref, max_ref, sum_ref, acc_ref):
    ends = ends_of(lengths_ref)
    width = GROUP * PAIR
    query_pos = line_positions(place_ref)
    query_start = start_of(ends, query_pos)
    q = q_ref[...].reshape(width, HDIM)
    max_ref[...] = jnp.full((1, width), MASKED, F32)
    sum_ref[...] = jnp.zeros((1, width), F32)
    acc_ref[...] = jnp.zeros((HDIM, width), F32)

    def add(step, scores):
        row_max = max_ref[...]
        new_max = jnp.maximum(row_max, jnp.max(scores, axis=0, keepdims=True))
        probs = jnp.exp2(scores - new_max)
        fading = jnp.exp2(row_max - new_max)
        max_ref[...] = new_max
        sum_ref[...] = sum_ref[...] * fading + jnp.sum(probs, axis=0, keepdims=True)
        acc_ref[...] = acc_ref[...] * fading + dot(
            kv_ref[step, :, HDIM:], probs.astype(BF16), ((0,), (0,))
        )

    steps = key_steps(place_ref, ends)
    for step in range(kv_ref.shape[0]):
        whole = unmasked(place_ref, ends, step)

        def scores_of():
            return dot(kv_ref[step, :, :HDIM], q, ((1,), (1,))) * (SCALE * LOG2E)

        @pl.when((step < steps) & whole)
        def _():
            add(step, scores_of())

        @pl.when((step < steps) & jnp.logical_not(whole))
        def _():
            allowed = allowed_pairs(place_ref, step, query_start, query_pos)
            add(step, jnp.where(allowed, scores_of(), MASKED))

    row_total = sum_ref[...]
    out = (acc_ref[...] / row_total).T.astype(BF16)
    log_total = max_ref[...] * (1.0 / LOG2E) + jnp.log(row_total)
    for k in range(GROUP):
        at = slice(PAIR * k, PAIR * (k + 1))
        out_ref[k, :PAIR, :] = out[at]
        out_ref[k, PAIR:, :] = stat_rows(log_total[:, at])


def merge_kernel(*refs):
    *part_refs, out_ref, total_ref = refs
    logs = [stat_row(ref[PAIR:, :].astype(F32), 0) for ref in part_refs]
    top = functools.reduce(jnp.maximum, logs)
    log_total = top + jnp.log(functools.reduce(jnp.add, [jnp.exp(x - top) for x in logs]))
    out = jnp.zeros((PAIR, HDIM), F32)
    for x, ref in zip(logs, part_refs):
        weight = jnp.broadcast_to(jnp.exp(x - log_total), (HDIM, PAIR)).T
        out = out + weight * ref[:PAIR, :].astype(F32)
    out_ref[...] = out.astype(BF16)
    total_ref[...] = log_total


def both_cores(place_ref, own_ref, other_ref, count):
    own = own_ref[:, :count, :].reshape(-1, own_ref.shape[2])
    other = other_ref[:, :count, :].reshape(-1, other_ref.shape[2])
    first = place_ref[2] == 0
    return jnp.where(first, own, other), jnp.where(first, other, own)


def raw_kernel(place_ref, attended_ref, own_ref, other_ref, input_ref, hold_ref, out_ref):
    parts, own, _ = out_ref.shape
    attended = attended_ref[...]
    low, high = both_cores(place_ref, own_ref, other_ref, FOLD_POST)
    half = low.shape[0]
    raw_low = (dot(attended, low, ((1,), (1,))) + input_ref[:, :half]).astype(BF16)
    raw_high = (dot(attended, high, ((1,), (1,))) + input_ref[:, half:]).astype(BF16)
    packed = jnp.concatenate([attended[own * k : own * (k + 1)] for k in range(parts)], axis=1)
    for k in range(parts):
        out_ref[k, :, :half] = raw_low[own * k : own * (k + 1)]
        out_ref[k, :, half : 2 * half] = raw_high[own * k : own * (k + 1)]
        out_ref[k, :, 2 * half :] = packed


def norm_kernel(
    place_ref,
    arrived_ref,
    own_ref,
    other_ref,
    attended_ref,
    cross_ref,
    input_ref,
    back_ref,
    out_ref,
):
    parts, own, _ = arrived_ref.shape
    features = out_ref.shape[2] - HDIM
    rows, share = input_ref.shape
    wide = attended_ref.shape[1]
    total = arrived_ref[0, :, :features].astype(F32)
    for k in range(1, parts):
        total = total + arrived_ref[k, :, :features].astype(F32)
    cross = cross_ref[...]
    back = jnp.zeros_like(cross)
    first = place_ref[2] == 0
    chips = own_ref.shape[0]
    grams = []
    for ref in (own_ref, other_ref):
        gram = ref[:, FOLD_POST:, :].astype(F32)
        grams.append(gram.reshape(chips, parts, FOLD_OUT, wide))
    for distance in range(parts):
        k = owner_of(place_ref, distance, parts)
        theirs = jnp.concatenate(
            [
                arrived_ref[k, :, features + wide * j : features + wide * (j + 1)]
                for j in range(parts)
            ],
            axis=0,
        )
        half = chips * FOLD_OUT
        own_gram, other_gram = (g[:, distance].reshape(half, wide).astype(BF16) for g in grams)
        back = back + dot(theirs[:, :half], jnp.where(first, own_gram, other_gram))
        back = back + dot(theirs[:, half:], jnp.where(first, other_gram, own_gram))
    back_ref[...] = cross + back
    attended = attended_ref[...].astype(F32)
    features_in = input_ref[...].astype(F32)
    squares = jnp.sum((attended * (2.0 * cross + back)).T, axis=0, keepdims=True) + jnp.sum(
        (features_in * features_in).T, axis=0, keepdims=True
    )
    side = jnp.concatenate(pieces(squares) + (jnp.zeros((own - 3, HDIM), BF16),), axis=0)
    summed = total.astype(BF16)
    for k in range(parts):
        out_ref[k, :, :features] = summed
        out_ref[k, :, features:] = side


def loss_kernel(
    width,
    lengths_ref,
    place_ref,
    steps_ref,
    arrived_ref,
    target_ref,
    own_ref,
    other_ref,
    back_ref,
    mine_ref,
    theirs_ref,
    loss_ref,
):
    parts, own, _ = arrived_ref.shape
    rows, features = target_ref.shape
    position = (place_ref[1] * 2 + place_ref[2]) * rows
    position = position + lax.broadcasted_iota(jnp.int32, (1, rows), 1)
    angle = (0.5 * math.pi / TSTEPS) * steps_ref[...].astype(F32)
    keep_level = sine(0.5 * math.pi - angle)
    weight = 1.0 + keep_level * keep_level
    for end in ends_of(lengths_ref):
        weight = jnp.where(position + 1 == end, 0.0, weight)
    side = arrived_ref[:, :, features:].astype(F32)
    squares = jnp.sum(jnp.sum(side, axis=0), axis=0, keepdims=True)
    inverse = column(lax.rsqrt(jnp.maximum(squares / width, 0.0) + EPSILON))
    prediction = arrived_ref[:, :, :features].reshape(rows, features).astype(F32) * inverse
    missed = prediction - target_ref[...].astype(F32)
    weighted_missed = column(weight) * missed
    loss = jnp.sum(weighted_missed * missed, axis=1, keepdims=True)
    loss_ref[...] = jnp.broadcast_to(jnp.sum(loss, axis=0, keepdims=True), (1, HDIM))
    pred_grad = weighted_missed.astype(BF16)
    along = jnp.sum(pred_grad.astype(F32) * prediction, axis=1, keepdims=True) / width
    low, high = both_cores(place_ref, own_ref, other_ref, FOLD_POST)
    half = low.shape[0]
    direct = dot(pred_grad[:, :half], low) + dot(pred_grad[:, half:], high)
    grad = (inverse * (direct - along * inverse * back_ref[...])).astype(BF16)
    first = place_ref[2] == 0
    mine_ref[...] = jnp.where(first, grad[:, :HDIM], grad[:, HDIM:])
    theirs_ref[...] = jnp.where(first, grad[:, HDIM:], grad[:, :HDIM])


def sent_kernel(grad_ref, attended_ref, total_ref, loss_ref, out_ref):
    grad = grad_ref[...]
    product = grad.astype(F32) * attended_ref[...].astype(F32)
    output_dot = jnp.sum(product.T, axis=0, keepdims=True)
    stats = stat_rows(total_ref[...], output_dot).astype(F32)
    loss_rows = [p.astype(F32) for p in pieces(loss_ref[...])]
    stats = jnp.concatenate([stats[:12]] + loss_rows + [stats[15:]], axis=0)
    out_ref[:PAIR, :] = grad
    out_ref[PAIR:, :] = stats.astype(BF16)


def backward_kernel(lengths_ref, place_ref, kv_ref, q_ref, *refs):
    *sent_refs, out_ref = refs
    ends = ends_of(lengths_ref)
    width = GROUP * PAIR
    query_pos = line_positions(place_ref)
    query_start = start_of(ends, query_pos)
    q = q_ref[...].reshape(width, HDIM)
    grad = jnp.concatenate([ref[:PAIR, :] for ref in sent_refs], axis=0)
    stats = [ref[PAIR:, :].astype(F32) for ref in sent_refs]
    log_total = jnp.concatenate([stat_row(x, 0) for x in stats], axis=1) * LOG2E
    output_dot = jnp.concatenate([stat_row(x, 6) for x in stats], axis=1)
    loss = functools.reduce(jnp.add, [x[12:13] + x[13:14] + x[14:15] for x in stats])
    tail = jnp.concatenate(
        [p.astype(F32) for p in pieces(loss)] + [jnp.zeros((STATS - 3, HDIM), F32)], axis=0
    )
    tail = jnp.concatenate((tail, tail), axis=1).astype(BF16)
    steps = key_steps(place_ref, ends)
    for step in range(out_ref.shape[0]):
        row = lax.rem(place_ref[1] // GROUP + (out_ref.shape[0] - step), out_ref.shape[0])
        out_ref[row, PAIR:, :] = tail

        def grads(masked):
            scores = dot(kv_ref[step, :, :HDIM], q, ((1,), (1,))) * (SCALE * LOG2E)
            probs = jnp.exp2(scores - log_total)
            if masked:
                allowed = allowed_pairs(place_ref, step, query_start, query_pos)
                probs = jnp.where(allowed, probs, 0.0)
            out_ref[row, :PAIR, HDIM:] = dot(probs.astype(BF16), grad).astype(BF16)
            prob_grad = dot(kv_ref[step, :, HDIM:], grad, ((1,), (1,)))
            score_grad = (probs * (prob_grad - output_dot)).astype(BF16)
            out_ref[row, :PAIR, :HDIM] = (dot(score_grad, q) * SCALE).astype(BF16)

        whole = unmasked(place_ref, ends, step)
        pl.when((step < steps) & whole)(functools.partial(grads, False))
        pl.when((step < steps) & jnp.logical_not(whole))(functools.partial(grads, True))

        @pl.when(step >= steps)
        def _():
            out_ref[row, :PAIR, :] = jnp.zeros((PAIR, 2 * HDIM), BF16)


def collect_kernel(*refs):
    arrived_ref, out_ref, loss_ref = refs
    parts = [arrived_ref[k].astype(F32) for k in range(arrived_ref.shape[0])]
    total = functools.reduce(jnp.add, parts)
    out_ref[...] = total[:PAIR].astype(BF16)
    rows = total[PAIR : PAIR + 3, :HDIM]
    loss_ref[...] = jnp.sum(rows, axis=0, keepdims=True)


def context_kernel(lanes, grad_ref, start_ref, weight_ref, out_ref):
    grad = jnp.concatenate([grad_ref[:, HDIM * k : HDIM * (k + 1)] for k in lanes], axis=1)
    grad = grad.astype(F32).T.astype(BF16)
    parts, share, _ = out_ref.shape
    for k in range(parts):
        total = dot(weight_ref[share * k : share * (k + 1)], grad)
        if out_ref.dtype == BF16:
            total = total + start_ref[k]
        out_ref[k] = total.astype(out_ref.dtype)


def total_kernel(arrived_ref, out_ref):
    parts = [arrived_ref[k].astype(F32) for k in range(arrived_ref.shape[0])]
    out_ref[...] = functools.reduce(jnp.add, parts).T.astype(BF16)


SMEM = pl.BlockSpec(memory_space=pltpu.SMEM)
HBM = pl.BlockSpec(memory_space=pltpu.HBM)
ANY = pl.BlockSpec(memory_space=pl.ANY)
VMEM = pl.BlockSpec(memory_space=pltpu.VMEM)
PARAMS = pltpu.CompilerParams(vmem_limit_bytes=32 * 1024 * 1024)
WHOLE = pltpu.CompilerParams(vmem_limit_bytes=60 * 1024 * 1024)


def local(
    concepts,
    noised,
    step_ids,
    doc_lengths,
    context,
    time_vec,
    w_pre,
    w_query,
    w_key,
    w_value,
    w_out,
    w_post,
):
    rows, features = concepts.shape
    parts = lax.axis_size("tp")
    chips = lax.axis_size(CHIPS)
    core = lax.axis_index("core")
    part = lax.axis_index("tp")
    seq_total = rows * lax.axis_size(ROWS)
    share = w_post.shape[0]
    own = rows // parts
    chip = lax.axis_index(CHIPS)
    place = jnp.stack((part, chip, core, chips)).astype(jnp.int32)
    width = share * parts
    head_width = w_out.shape[0]
    fold_rows = FOLD_POST + FOLD_OUT * parts
    steps = step_ids.reshape(1, rows)

    with jax.named_scope("inputs"):
        sent = pl.pallas_call(
            send_kernel,
            out_shape=jax.ShapeDtypeStruct((rows + fold_rows, share), BF16),
            in_specs=[VMEM, VMEM, HBM, HBM, HBM, HBM],
            out_specs=VMEM,
            scratch_shapes=[
                pltpu.VMEM((rows, features), BF16),
                pltpu.VMEM((features, share), BF16),
                pltpu.VMEM((share, HDIM), BF16),
                pltpu.VMEM((2 * FOLD_OUT, width), BF16),
                pltpu.SemaphoreType.DMA((7,)),
            ],
            compiler_params=WHOLE,
        )(steps, time_vec.reshape(1, share), noised, w_pre, w_post, w_out)
        blocks = around(sent, "tp")
    with jax.named_scope("keys_values"):
        kv_shape = jax.ShapeDtypeStruct((rows, 2 * HDIM), BF16)
        mine, theirs = pl.pallas_call(
            project_kernel,
            out_shape=(kv_shape, kv_shape),
            in_specs=[SMEM, HBM, HBM, HBM],
            out_specs=(VMEM, VMEM),
            scratch_shapes=[
                pltpu.VMEM(context.shape, BF16),
                pltpu.VMEM((2,) + w_key.shape, BF16),
                pltpu.SemaphoreType.DMA((12,)),
            ],
            compiler_params=PARAMS,
        )(place, context, w_key, w_value)
        own_kv = to_head(mine, theirs, core)
        all_kv = jnp.stack(shifted(own_kv, "y"))
    with jax.named_scope("targets"):
        count = lax.axis_size(ROWS)
        following = lax.ppermute(concepts[:1], ROWS, [(i + 1, i) for i in range(count - 1)])
        targets = jnp.concatenate((concepts[1:], following), axis=0)
    with jax.named_scope("gathered"):
        query_shape = jax.ShapeDtypeStruct((rows, HDIM), BF16)
        mine, theirs, cross, folded = pl.pallas_call(
            gathered_kernel,
            out_shape=(
                query_shape,
                query_shape,
                jax.ShapeDtypeStruct((rows, head_width), F32),
                jax.ShapeDtypeStruct((chips, fold_rows, head_width), BF16),
            ),
            in_specs=[SMEM, VMEM, VMEM, ANY, VMEM, ANY] + [VMEM] * (len(blocks) - 3) + [ANY],
            out_specs=(VMEM,) * 4,
            scratch_shapes=[
                pltpu.VMEM((2,) + sent.shape, BF16),
                pltpu.SemaphoreType.DMA((2,)),
            ],
            compiler_params=PARAMS,
        )(place, w_query, w_out, all_kv, *blocks)
        query_head = to_head(mine, theirs, core)
        line_queries = jnp.stack(shifted(query_head, "x"))
        input_part, input_post = pl.pallas_call(
            post_kernel,
            out_shape=(
                jax.ShapeDtypeStruct((rows, share), BF16),
                jax.ShapeDtypeStruct((rows, features), F32),
            ),
            in_specs=[VMEM, VMEM, ANY],
            out_specs=(VMEM, VMEM),
            compiler_params=PARAMS,
        )(sent, w_post, query_head)
        own_fold = lax.all_to_all(folded, CHIPS, 0, 0, tiled=True)
        other_fold = swap(own_fold)
    with jax.named_scope("attention"):
        sent = pl.pallas_call(
            forward_kernel,
            out_shape=jax.ShapeDtypeStruct((GROUP, PAIR + STATS, HDIM), BF16),
            in_specs=[SMEM, SMEM, VMEM, VMEM, ANY],
            out_specs=VMEM,
            scratch_shapes=[
                pltpu.VMEM((1, GROUP * PAIR), F32),
                pltpu.VMEM((1, GROUP * PAIR), F32),
                pltpu.VMEM((HDIM, GROUP * PAIR), F32),
            ],
            compiler_params=PARAMS,
        )(doc_lengths, place, line_queries, all_kv, input_post)
        attended_head, log_total = pl.pallas_call(
            merge_kernel,
            out_shape=(
                jax.ShapeDtypeStruct((PAIR, HDIM), BF16),
                jax.ShapeDtypeStruct((1, PAIR), F32),
            ),
            in_specs=[VMEM] * GROUP,
            out_specs=(VMEM, VMEM),
            compiler_params=PARAMS,
        )(*returned(sent, "x"))
        attended = to_rows(attended_head, core)
    with jax.named_scope("raw"):
        sent = pl.pallas_call(
            raw_kernel,
            out_shape=jax.ShapeDtypeStruct((parts, own, features + head_width * parts), BF16),
            in_specs=[SMEM, VMEM, VMEM, VMEM, VMEM, ANY],
            out_specs=VMEM,
            compiler_params=PARAMS,
        )(place, attended, own_fold, other_fold, input_post, targets)
        arrived = lax.all_to_all(sent, "tp", 0, 0, tiled=True)
    with jax.named_scope("norm"):
        back, sent = pl.pallas_call(
            norm_kernel,
            out_shape=(
                jax.ShapeDtypeStruct((rows, head_width), F32),
                jax.ShapeDtypeStruct((parts, own, features + HDIM), BF16),
            ),
            in_specs=[SMEM] + [VMEM] * 6,
            out_specs=(VMEM, VMEM),
            compiler_params=PARAMS,
        )(place, arrived, own_fold, other_fold, attended, cross, input_part)
        arrived = lax.all_to_all(sent, "tp", 0, 0, tiled=True)
    with jax.named_scope("loss"):
        mine, theirs, loss_part = pl.pallas_call(
            functools.partial(loss_kernel, width),
            out_shape=(
                query_shape,
                query_shape,
                jax.ShapeDtypeStruct((1, HDIM), F32),
            ),
            in_specs=[SMEM, SMEM] + [VMEM] * 6,
            out_specs=(VMEM, VMEM, VMEM),
            compiler_params=PARAMS,
        )(doc_lengths, place, steps, arrived, targets, own_fold, other_fold, back)
    with jax.named_scope("sent_grads"):
        grad_head = to_head(mine, theirs, core)
        sent = pl.pallas_call(
            sent_kernel,
            out_shape=jax.ShapeDtypeStruct((PAIR + STATS, HDIM), BF16),
            in_specs=[VMEM] * 4,
            out_specs=VMEM,
            compiler_params=PARAMS,
        )(grad_head, attended_head, log_total, loss_part)
        line_grads = shifted(sent, "x")
    with jax.named_scope("attention_grad"):
        sent = pl.pallas_call(
            backward_kernel,
            out_shape=jax.ShapeDtypeStruct((chips // GROUP, PAIR + STATS, 2 * HDIM), BF16),
            in_specs=[SMEM, SMEM] + [VMEM] * (2 + GROUP),
            out_specs=VMEM,
            compiler_params=PARAMS,
        )(doc_lengths, place, all_kv, line_queries, *line_grads)
        kv_grad, loss_part = pl.pallas_call(
            collect_kernel,
            out_shape=(
                jax.ShapeDtypeStruct((PAIR, 2 * HDIM), BF16),
                jax.ShapeDtypeStruct((1, HDIM), F32),
            ),
            in_specs=[VMEM],
            out_specs=(VMEM, VMEM),
            compiler_params=PARAMS,
        )(lax.all_to_all(sent, "y", 0, 0, tiled=True))
        kv_grad = to_rows(kv_grad, core)
        loss_part = loss_part[0, 0]
        loss = (loss_part + swap(loss_part)) / (seq_total * features)
    with jax.named_scope("d_context"):
        key_terms = pl.pallas_call(
            functools.partial(context_kernel, (0, 2)),
            out_shape=jax.ShapeDtypeStruct((parts, share, rows), F32),
            in_specs=[VMEM, ANY, VMEM],
            out_specs=VMEM,
            compiler_params=PARAMS,
        )(kv_grad, loss.reshape(1, 1), w_key)
        terms = pl.pallas_call(
            functools.partial(context_kernel, (1, 3)),
            out_shape=jax.ShapeDtypeStruct((parts, share, rows), BF16),
            in_specs=[VMEM, VMEM, VMEM],
            out_specs=VMEM,
            compiler_params=PARAMS,
        )(kv_grad, key_terms, w_value)
        d_context = pl.pallas_call(
            total_kernel,
            out_shape=jax.ShapeDtypeStruct((rows, share), BF16),
            in_specs=[VMEM],
            out_specs=VMEM,
            compiler_params=PARAMS,
        )(lax.all_to_all(terms, "tp", 0, 0, tiled=True))
    return d_context, loss


def solution(mesh):
    cores = 2
    count, parts = mesh.devices.shape
    side = math.isqrt(count // cores)
    split = Mesh(mesh.devices.reshape(side, side, cores, parts), ("y", "x", "core", "tp"))
    by_rows = P(ROWS, None)
    by_columns = P(None, "tp")
    return jax.shard_map(
        local,
        mesh=split,
        in_specs=(
            by_rows,
            by_rows,
            P(ROWS),
            P(),
            by_rows,
            P("tp"),
            by_columns,
            by_columns,
            by_columns,
            by_columns,
            P("tp", None),
            P("tp", None),
        ),
        out_specs=(P(ROWS, "tp"), P()),
        check_vma=False,
    )
```

```python
import functools
import math

import jax
import jax.numpy as jnp
from jax import lax
from jax.experimental import pallas as pl
from jax.experimental.pallas import tpu as pltpu
from jax.sharding import Mesh
from jax.sharding import PartitionSpec as P

HDIM = 128
TSTEPS = 100
MASKED = -1e30
EPSILON = 1e-06
ROWS = ("y", "x", "core")
CHIPS = ("y", "x")
SCALE = 1.0 / math.sqrt(HDIM)
LOG2E = math.log2(math.e)
PAIR = 256
GROUP = 4
FOLD_POST = 32
FOLD_OUT = 8
STATS = 16
F32 = jnp.float32
BF16 = jnp.bfloat16


def dot(a, b, contract=((1,), (0,))):
    return lax.dot_general(a, b, (contract, ((), ())), preferred_element_type=F32)


def shifted(block, axis):
    count = lax.axis_size(axis)
    routes = [[(i, (i + s) % count) for i in range(count)] for s in range(1, count)]
    return [block] + [lax.ppermute(block, axis, route) for route in routes]


def returned(blocks, axis):
    count = lax.axis_size(axis)
    routes = [[(i, (i - s) % count) for i in range(count)] for s in range(count)]
    return [blocks[0]] + [lax.ppermute(blocks[s], axis, routes[s]) for s in range(1, count)]


def around(block, axis):
    count = lax.axis_size(axis)
    up = [(i, (i + 1) % count) for i in range(count)]
    down = [(i, (i - 1) % count) for i in range(count)]
    behind, ahead = [block], [block]
    for _ in range(count // 2 - 1):
        behind.append(lax.ppermute(behind[-1], axis, up))
        ahead.append(lax.ppermute(ahead[-1], axis, down))
    half = block.shape[0] // 2
    far = [lax.ppermute(behind[-1][:half], axis, up), lax.ppermute(ahead[-1][half:], axis, down)]
    return behind + far + ahead[:0:-1]


def gathered_blocks(refs):
    half = (len(refs) - 1) // 2
    far = jnp.concatenate((refs[half][...], refs[half + 1][...]), axis=0)
    return [r[...] for r in refs[:half]] + [far] + [r[...] for r in refs[half + 2 :]]


def owner_of(place_ref, distance, parts):
    return lax.rem(place_ref[0] + (parts - distance), parts)


def swap(block):
    return lax.ppermute(block, "core", [(0, 1), (1, 0)])


def to_head(mine, theirs, core):
    first = core == 0
    got = swap(theirs)
    return jnp.concatenate((jnp.where(first, mine, got), jnp.where(first, got, mine)), axis=0)


def to_rows(block, core):
    first = core == 0
    half = block.shape[0] // 2
    top, bottom = block[:half], block[half:]
    mine = jnp.where(first, top, bottom)
    got = swap(jnp.where(first, bottom, top))
    return jnp.concatenate((jnp.where(first, mine, got), jnp.where(first, got, mine)), axis=1)


def pieces(values):
    high = values.astype(BF16)
    rest = values - high.astype(F32)
    middle = rest.astype(BF16)
    return high, middle, (rest - middle.astype(F32)).astype(BF16)


def stat_rows(*rows):
    out = []
    for row in rows:
        for piece in pieces(row):
            out += [piece[:, :HDIM].astype(F32), piece[:, HDIM:].astype(F32)]
    out.append(jnp.zeros((STATS - len(out), HDIM), F32))
    return jnp.concatenate(out, axis=0).astype(BF16)


def stat_row(block, at):
    total = block[at : at + 2] + block[at + 2 : at + 4] + block[at + 4 : at + 6]
    return jnp.concatenate((total[:1], total[1:]), axis=1)


def sine(x):
    y = x * x
    total = jnp.full_like(x, 1.0 / 6227020800.0)
    for c in (-1.0 / 39916800.0, 1.0 / 362880.0, -1.0 / 5040.0, 1.0 / 120.0, -1.0 / 6.0, 1.0):
        total = total * y + c
    return total * x


def column(row):
    return jnp.broadcast_to(row, (HDIM, HDIM)).T[:, :1]


def ends_of(lengths_ref):
    ends = [lengths_ref[0]]
    for d in range(1, lengths_ref.shape[0]):
        ends.append(ends[-1] + lengths_ref[d])
    return ends


def start_of(ends, positions):
    start = jnp.zeros_like(positions)
    for end in ends:
        start = jnp.where(positions >= end, end, start)
    return start


def fetch(pairs, sems):
    copies = [pltpu.make_async_copy(f, t, sems.at[i]) for i, (f, t) in enumerate(pairs)]
    for copy in copies:
        copy.start()
    return copies


def send_kernel(
    steps_ref,
    time_ref,
    noised_ref,
    pre_ref,
    post_ref,
    out_ref,
    sent_ref,
    noised,
    pre,
    post_part,
    out_part,
    sems,
):
    rows, features = noised.shape
    share = pre.shape[1]
    slot = lax.axis_index("core") * lax.axis_size(CHIPS)
    slot = slot + lax.axis_index("y") * lax.axis_size("x") + lax.axis_index("x")
    lanes = pl.ds(pl.multiple_of(slot // (HDIM // FOLD_POST) * HDIM, HDIM), HDIM)
    lines = pl.ds(pl.multiple_of(slot // 2 * (2 * FOLD_OUT), 2 * FOLD_OUT), 2 * FOLD_OUT)
    quarter = features // 4
    pairs = [(post_ref.at[:, lanes], post_part), (out_ref.at[lines], out_part), (noised_ref, noised)]
    pairs += [
        (pre_ref.at[pl.ds(quarter * k, quarter)], pre.at[pl.ds(quarter * k, quarter)])
        for k in range(4)
    ]
    copies = fetch(pairs, sems)
    angle = (0.5 * math.pi / TSTEPS) * steps_ref[...].astype(F32)
    noise = column(sine(angle)) * time_ref[...]
    copies[0].wait()
    post = post_part[...].astype(F32).T
    which = lax.rem(slot, HDIM // FOLD_POST)
    post_rows = post[:FOLD_POST]
    for k in range(1, HDIM // FOLD_POST):
        post_rows = jnp.where(which == k, post[FOLD_POST * k : FOLD_POST * (k + 1)], post_rows)
    copies[1].wait()
    out_rows = out_part[...].astype(F32)
    out_rows = jnp.where(lax.rem(slot, 2) == 0, out_rows[:FOLD_OUT], out_rows[FOLD_OUT:])
    parts = out_rows.shape[1] // share
    out_rows = [out_rows[:, share * k : share * (k + 1)] for k in range(parts)]
    sent_ref[rows:, :] = jnp.concatenate([post_rows] + out_rows, axis=0).astype(BF16)
    copies[2].wait()
    total = noise
    for k in range(4):
        at = slice(quarter * k, quarter * (k + 1))
        copies[3 + k].wait()
        total = total + dot(noised[:, at], pre[at])
    sent_ref[:rows, :] = total.astype(BF16)


def project_kernel(place_ref, context_ref, key_ref, value_ref, mine_ref, theirs_ref):
    keys = dot(context_ref[...], key_ref[...])
    values = dot(context_ref[...], value_ref[...])
    left = jnp.concatenate((keys[:, :HDIM], values[:, :HDIM]), axis=1)
    right = jnp.concatenate((keys[:, HDIM:], values[:, HDIM:]), axis=1)
    first = place_ref[2] == 0
    mine_ref[...] = jnp.where(first, left, right).astype(BF16)
    theirs_ref[...] = jnp.where(first, right, left).astype(BF16)


def gathered_kernel(place_ref, w_query_ref, w_out_ref, hold_ref, *refs):
    *block_refs, mine_ref, theirs_ref, cross_ref, folded_ref, near, sems = refs
    rows = mine_ref.shape[0]
    heads, width = w_out_ref.shape
    near_refs = (block_refs[1], block_refs[-1])
    near_copies = fetch([(ref, near.at[k]) for k, ref in enumerate(near_refs)], sems)
    half = (len(block_refs) - 1) // 2
    parts = len(block_refs) - 1
    far = jnp.concatenate((block_refs[half][...], block_refs[half + 1][...]), axis=0)
    blocks = {0: block_refs[0][...], half: far}
    for k in range(2, half):
        blocks[k] = block_refs[k][...]
    for k in range(half + 1, parts - 1):
        blocks[k] = block_refs[k + 1][...]
    share = far.shape[1]
    top = rows + FOLD_POST

    def against(total, weight_of, distance, count):
        owner = owner_of(place_ref, distance, parts)
        at = pl.ds(pl.multiple_of(owner * share, share), share)
        return total + weight_of(blocks[distance][:count], at)

    def by_out(block, at):
        return dot(block, w_out_ref[:, at], ((1,), (1,)))

    def by_query(block, at):
        return dot(block, w_query_ref[at, :])

    both = jnp.zeros((top, heads), F32)
    squares = jnp.zeros((rows, 1), F32)
    query = jnp.zeros((rows, heads), F32)
    for step, distance in enumerate(list(blocks) + [1, parts - 1]):
        if step >= parts - 2:
            near_copies[step - parts + 2].wait()
            blocks[distance] = near[step - parts + 2]
        wide = blocks[distance][:rows].astype(F32)
        squares = squares + jnp.sum(wide * wide, axis=1, keepdims=True)
        both = against(both, by_out, distance, top)
        query = against(query, by_query, distance, rows)
    cross_ref[...] = both[:rows]
    span = FOLD_OUT * parts
    slices = [blocks[k][top:].astype(F32) for k in range(parts)]
    gram = jnp.zeros((span, heads), F32)
    for k in range(parts):
        at = slice(FOLD_OUT * k, FOLD_OUT * (k + 1))
        chunk = jnp.concatenate([block[at] for block in slices], axis=0).astype(BF16)
        gram = gram + by_out(chunk, slice(share * k, share * (k + 1)))
    folded = jnp.concatenate((both[rows:], gram), axis=0).astype(BF16)
    for k in range(folded_ref.shape[0]):
        folded_ref[k] = folded

    query = (query * lax.rsqrt(squares / width + EPSILON)).astype(BF16)
    first = place_ref[2] == 0
    mine_ref[...] = jnp.where(first, query[:, :HDIM], query[:, HDIM:])
    theirs_ref[...] = jnp.where(first, query[:, HDIM:], query[:, :HDIM])


def post_kernel(sent_ref, post_ref, hold_ref, input_ref, input_post_ref):
    features = sent_ref[: input_ref.shape[0], :]
    input_ref[...] = features
    input_post_ref[...] = dot(features, post_ref[...])


def line_positions(place_ref):
    row = place_ref[1] // GROUP
    here = lax.rem(place_ref[1], GROUP)
    chips = [row * GROUP + lax.rem(here + (GROUP - k), GROUP) for k in range(GROUP)]
    lanes = lax.broadcasted_iota(jnp.int32, (1, PAIR), 1)
    return jnp.concatenate([chip * PAIR + lanes for chip in chips], axis=1)


def key_steps(place_ref, ends):
    row = place_ref[1] // GROUP
    here = lax.rem(place_ref[1], GROUP)
    floor = start_of(ends, row * (GROUP * PAIR))
    past = jnp.maximum(floor - (here * PAIR + PAIR - 1), 0)
    lowest = (past + GROUP * PAIR - 1) // (GROUP * PAIR)
    return row - lowest + 1


def allowed_pairs(place_ref, step, query_start, query_pos):
    base = (place_ref[1] - step * GROUP) * PAIR
    key_pos = base + lax.broadcasted_iota(jnp.int32, (PAIR, query_pos.shape[1]), 0)
    return (key_pos >= query_start) & (key_pos <= query_pos)


def unmasked(place_ref, ends, step):
    row = place_ref[1] // GROUP
    first_key = (place_ref[1] - step * GROUP) * PAIR
    return (step > 0) & (start_of(ends, (row + 1) * (GROUP * PAIR) - 1) <= first_key)


def forward_kernel(lengths_ref, place_ref, q_ref, kv_ref, hold_ref, out_ref, max_ref, sum_ref, acc_ref):
    ends = ends_of(lengths_ref)
    width = GROUP * PAIR
    query_pos = line_positions(place_ref)
    query_start = start_of(ends, query_pos)
    q = q_ref[...].reshape(width, HDIM)
    max_ref[...] = jnp.full((1, width), MASKED, F32)
    sum_ref[...] = jnp.zeros((1, width), F32)
    acc_ref[...] = jnp.zeros((HDIM, width), F32)

    def add(step, scores):
        row_max = max_ref[...]
        new_max = jnp.maximum(row_max, jnp.max(scores, axis=0, keepdims=True))
        probs = jnp.exp2(scores - new_max)
        fading = jnp.exp2(row_max - new_max)
        max_ref[...] = new_max
        sum_ref[...] = sum_ref[...] * fading + jnp.sum(probs, axis=0, keepdims=True)
        acc_ref[...] = acc_ref[...] * fading + dot(
            kv_ref[step, :, HDIM:], probs.astype(BF16), ((0,), (0,))
        )

    steps = key_steps(place_ref, ends)
    for step in range(kv_ref.shape[0]):
        whole = unmasked(place_ref, ends, step)

        def scores_of():
            return dot(kv_ref[step, :, :HDIM], q, ((1,), (1,))) * (SCALE * LOG2E)

        @pl.when((step < steps) & whole)
        def _():
            add(step, scores_of())

        @pl.when((step < steps) & jnp.logical_not(whole))
        def _():
            allowed = allowed_pairs(place_ref, step, query_start, query_pos)
            add(step, jnp.where(allowed, scores_of(), MASKED))

    row_total = sum_ref[...]
    out = (acc_ref[...] / row_total).T.astype(BF16)
    log_total = max_ref[...] * (1.0 / LOG2E) + jnp.log(row_total)
    for k in range(GROUP):
        at = slice(PAIR * k, PAIR * (k + 1))
        out_ref[k, :PAIR, :] = out[at]
        out_ref[k, PAIR:, :] = stat_rows(log_total[:, at])


def merge_kernel(*refs):
    *part_refs, out_ref, total_ref = refs
    logs = [stat_row(ref[PAIR:, :].astype(F32), 0) for ref in part_refs]
    top = functools.reduce(jnp.maximum, logs)
    log_total = top + jnp.log(functools.reduce(jnp.add, [jnp.exp(x - top) for x in logs]))
    out = jnp.zeros((PAIR, HDIM), F32)
    for x, ref in zip(logs, part_refs):
        weight = jnp.broadcast_to(jnp.exp(x - log_total), (HDIM, PAIR)).T
        out = out + weight * ref[:PAIR, :].astype(F32)
    out_ref[...] = out.astype(BF16)
    total_ref[...] = log_total


def both_cores(place_ref, own_ref, other_ref, count):
    own = own_ref[:, :count, :].reshape(-1, own_ref.shape[2])
    other = other_ref[:, :count, :].reshape(-1, other_ref.shape[2])
    first = place_ref[2] == 0
    return jnp.where(first, own, other), jnp.where(first, other, own)


def raw_kernel(place_ref, attended_ref, own_ref, other_ref, input_ref, hold_ref, out_ref):
    parts, own, _ = out_ref.shape
    attended = attended_ref[...]
    low, high = both_cores(place_ref, own_ref, other_ref, FOLD_POST)
    half = low.shape[0]
    raw_low = (dot(attended, low, ((1,), (1,))) + input_ref[:, :half]).astype(BF16)
    raw_high = (dot(attended, high, ((1,), (1,))) + input_ref[:, half:]).astype(BF16)
    packed = jnp.concatenate([attended[own * k : own * (k + 1)] for k in range(parts)], axis=1)
    for k in range(parts):
        out_ref[k, :, :half] = raw_low[own * k : own * (k + 1)]
        out_ref[k, :, half : 2 * half] = raw_high[own * k : own * (k + 1)]
        out_ref[k, :, 2 * half :] = packed


def norm_kernel(
    place_ref,
    arrived_ref,
    own_ref,
    other_ref,
    attended_ref,
    cross_ref,
    input_ref,
    back_ref,
    out_ref,
):
    parts, own, _ = arrived_ref.shape
    features = out_ref.shape[2] - HDIM
    rows, share = input_ref.shape
    wide = attended_ref.shape[1]
    total = arrived_ref[0, :, :features].astype(F32)
    for k in range(1, parts):
        total = total + arrived_ref[k, :, :features].astype(F32)
    cross = cross_ref[...]
    back = jnp.zeros_like(cross)
    first = place_ref[2] == 0
    chips = own_ref.shape[0]
    grams = []
    for ref in (own_ref, other_ref):
        gram = ref[:, FOLD_POST:, :].astype(F32)
        grams.append(gram.reshape(chips, parts, FOLD_OUT, wide))
    for distance in range(parts):
        k = owner_of(place_ref, distance, parts)
        theirs = jnp.concatenate(
            [
                arrived_ref[k, :, features + wide * j : features + wide * (j + 1)]
                for j in range(parts)
            ],
            axis=0,
        )
        half = chips * FOLD_OUT
        own_gram, other_gram = (g[:, distance].reshape(half, wide).astype(BF16) for g in grams)
        back = back + dot(theirs[:, :half], jnp.where(first, own_gram, other_gram))
        back = back + dot(theirs[:, half:], jnp.where(first, other_gram, own_gram))
    back_ref[...] = cross + back
    attended = attended_ref[...].astype(F32)
    features_in = input_ref[...].astype(F32)
    squares = jnp.sum((attended * (2.0 * cross + back)).T, axis=0, keepdims=True) + jnp.sum(
        (features_in * features_in).T, axis=0, keepdims=True
    )
    side = jnp.concatenate(pieces(squares) + (jnp.zeros((own - 3, HDIM), BF16),), axis=0)
    summed = total.astype(BF16)
    for k in range(parts):
        out_ref[k, :, :features] = summed
        out_ref[k, :, features:] = side


def loss_kernel(
    width,
    lengths_ref,
    place_ref,
    steps_ref,
    arrived_ref,
    target_ref,
    own_ref,
    other_ref,
    back_ref,
    mine_ref,
    theirs_ref,
    loss_ref,
):
    parts, own, _ = arrived_ref.shape
    rows, features = target_ref.shape
    position = (place_ref[1] * 2 + place_ref[2]) * rows
    position = position + lax.broadcasted_iota(jnp.int32, (1, rows), 1)
    angle = (0.5 * math.pi / TSTEPS) * steps_ref[...].astype(F32)
    keep_level = sine(0.5 * math.pi - angle)
    weight = 1.0 + keep_level * keep_level
    for end in ends_of(lengths_ref):
        weight = jnp.where(position + 1 == end, 0.0, weight)
    side = arrived_ref[:, :, features:].astype(F32)
    squares = jnp.sum(jnp.sum(side, axis=0), axis=0, keepdims=True)
    inverse = column(lax.rsqrt(jnp.maximum(squares / width, 0.0) + EPSILON))
    prediction = arrived_ref[:, :, :features].reshape(rows, features).astype(F32) * inverse
    missed = prediction - target_ref[...].astype(F32)
    weighted_missed = column(weight) * missed
    loss = jnp.sum(weighted_missed * missed, axis=1, keepdims=True)
    loss_ref[...] = jnp.broadcast_to(jnp.sum(loss, axis=0, keepdims=True), (1, HDIM))
    pred_grad = weighted_missed.astype(BF16)
    along = jnp.sum(pred_grad.astype(F32) * prediction, axis=1, keepdims=True) / width
    low, high = both_cores(place_ref, own_ref, other_ref, FOLD_POST)
    half = low.shape[0]
    direct = dot(pred_grad[:, :half], low) + dot(pred_grad[:, half:], high)
    grad = (inverse * (direct - along * inverse * back_ref[...])).astype(BF16)
    first = place_ref[2] == 0
    mine_ref[...] = jnp.where(first, grad[:, :HDIM], grad[:, HDIM:])
    theirs_ref[...] = jnp.where(first, grad[:, HDIM:], grad[:, :HDIM])


def sent_kernel(grad_ref, attended_ref, total_ref, loss_ref, out_ref):
    grad = grad_ref[...]
    product = grad.astype(F32) * attended_ref[...].astype(F32)
    output_dot = jnp.sum(product.T, axis=0, keepdims=True)
    stats = stat_rows(total_ref[...], output_dot).astype(F32)
    loss_rows = [p.astype(F32) for p in pieces(loss_ref[...])]
    stats = jnp.concatenate([stats[:12]] + loss_rows + [stats[15:]], axis=0)
    out_ref[:PAIR, :] = grad
    out_ref[PAIR:, :] = stats.astype(BF16)


def backward_kernel(lengths_ref, place_ref, kv_ref, q_ref, *refs):
    *sent_refs, out_ref = refs
    ends = ends_of(lengths_ref)
    width = GROUP * PAIR
    query_pos = line_positions(place_ref)
    query_start = start_of(ends, query_pos)
    q = q_ref[...].reshape(width, HDIM)
    grad = jnp.concatenate([ref[:PAIR, :] for ref in sent_refs], axis=0)
    stats = [ref[PAIR:, :].astype(F32) for ref in sent_refs]
    log_total = jnp.concatenate([stat_row(x, 0) for x in stats], axis=1) * LOG2E
    output_dot = jnp.concatenate([stat_row(x, 6) for x in stats], axis=1)
    loss = functools.reduce(jnp.add, [x[12:13] + x[13:14] + x[14:15] for x in stats])
    tail = jnp.concatenate(
        [p.astype(F32) for p in pieces(loss)] + [jnp.zeros((STATS - 3, HDIM), F32)], axis=0
    )
    tail = jnp.concatenate((tail, tail), axis=1).astype(BF16)
    steps = key_steps(place_ref, ends)
    for step in range(out_ref.shape[0]):
        row = lax.rem(place_ref[1] // GROUP + (out_ref.shape[0] - step), out_ref.shape[0])
        out_ref[row, PAIR:, :] = tail

        def grads(masked):
            scores = dot(kv_ref[step, :, :HDIM], q, ((1,), (1,))) * (SCALE * LOG2E)
            probs = jnp.exp2(scores - log_total)
            if masked:
                allowed = allowed_pairs(place_ref, step, query_start, query_pos)
                probs = jnp.where(allowed, probs, 0.0)
            out_ref[row, :PAIR, HDIM:] = dot(probs.astype(BF16), grad).astype(BF16)
            prob_grad = dot(kv_ref[step, :, HDIM:], grad, ((1,), (1,)))
            score_grad = (probs * (prob_grad - output_dot)).astype(BF16)
            out_ref[row, :PAIR, :HDIM] = (dot(score_grad, q) * SCALE).astype(BF16)

        whole = unmasked(place_ref, ends, step)
        pl.when((step < steps) & whole)(functools.partial(grads, False))
        pl.when((step < steps) & jnp.logical_not(whole))(functools.partial(grads, True))

        @pl.when(step >= steps)
        def _():
            out_ref[row, :PAIR, :] = jnp.zeros((PAIR, 2 * HDIM), BF16)


def collect_kernel(*refs):
    arrived_ref, out_ref, loss_ref = refs
    parts = [arrived_ref[k].astype(F32) for k in range(arrived_ref.shape[0])]
    total = functools.reduce(jnp.add, parts)
    out_ref[...] = total[:PAIR].astype(BF16)
    rows = total[PAIR : PAIR + 3, :HDIM]
    loss_ref[...] = jnp.sum(rows, axis=0, keepdims=True)


def context_kernel(lanes, grad_ref, start_ref, weight_ref, out_ref):
    grad = jnp.concatenate([grad_ref[:, HDIM * k : HDIM * (k + 1)] for k in lanes], axis=1)
    grad = grad.astype(F32).T.astype(BF16)
    parts, share, _ = out_ref.shape
    for k in range(parts):
        total = dot(weight_ref[share * k : share * (k + 1)], grad)
        if out_ref.dtype == BF16:
            total = total + start_ref[k]
        out_ref[k] = total.astype(out_ref.dtype)


def total_kernel(arrived_ref, out_ref):
    parts = [arrived_ref[k].astype(F32) for k in range(arrived_ref.shape[0])]
    out_ref[...] = functools.reduce(jnp.add, parts).T.astype(BF16)


SMEM = pl.BlockSpec(memory_space=pltpu.SMEM)
HBM = pl.BlockSpec(memory_space=pltpu.HBM)
ANY = pl.BlockSpec(memory_space=pl.ANY)
VMEM = pl.BlockSpec(memory_space=pltpu.VMEM)
PARAMS = pltpu.CompilerParams(vmem_limit_bytes=32 * 1024 * 1024)
WHOLE = pltpu.CompilerParams(vmem_limit_bytes=60 * 1024 * 1024)


def local(
    concepts,
    noised,
    step_ids,
    doc_lengths,
    context,
    time_vec,
    w_pre,
    w_query,
    w_key,
    w_value,
    w_out,
    w_post,
):
    rows, features = concepts.shape
    parts = lax.axis_size("tp")
    chips = lax.axis_size(CHIPS)
    core = lax.axis_index("core")
    part = lax.axis_index("tp")
    seq_total = rows * lax.axis_size(ROWS)
    share = w_post.shape[0]
    own = rows // parts
    chip = lax.axis_index(CHIPS)
    place = jnp.stack((part, chip, core, chips)).astype(jnp.int32)
    width = share * parts
    head_width = w_out.shape[0]
    fold_rows = FOLD_POST + FOLD_OUT * parts
    steps = step_ids.reshape(1, rows)

    with jax.named_scope("inputs"):
        sent = pl.pallas_call(
            send_kernel,
            out_shape=jax.ShapeDtypeStruct((rows + fold_rows, share), BF16),
            in_specs=[VMEM, VMEM, HBM, HBM, HBM, HBM],
            out_specs=VMEM,
            scratch_shapes=[
                pltpu.VMEM((rows, features), BF16),
                pltpu.VMEM((features, share), BF16),
                pltpu.VMEM((share, HDIM), BF16),
                pltpu.VMEM((2 * FOLD_OUT, width), BF16),
                pltpu.SemaphoreType.DMA((7,)),
            ],
            compiler_params=WHOLE,
        )(steps, time_vec.reshape(1, share), noised, w_pre, w_post, w_out)
        blocks = around(sent, "tp")
    with jax.named_scope("keys_values"):
        kv_shape = jax.ShapeDtypeStruct((rows, 2 * HDIM), BF16)
        mine, theirs = pl.pallas_call(
            project_kernel,
            out_shape=(kv_shape, kv_shape),
            in_specs=[SMEM, VMEM, VMEM, VMEM],
            out_specs=(VMEM, VMEM),
            compiler_params=PARAMS,
        )(place, context, w_key, w_value)
        own_kv = to_head(mine, theirs, core)
        all_kv = jnp.stack(shifted(own_kv, "y"))
    with jax.named_scope("targets"):
        count = lax.axis_size(ROWS)
        following = lax.ppermute(concepts[:1], ROWS, [(i + 1, i) for i in range(count - 1)])
        targets = jnp.concatenate((concepts[1:], following), axis=0)
    with jax.named_scope("gathered"):
        query_shape = jax.ShapeDtypeStruct((rows, HDIM), BF16)
        mine, theirs, cross, folded = pl.pallas_call(
            gathered_kernel,
            out_shape=(
                query_shape,
                query_shape,
                jax.ShapeDtypeStruct((rows, head_width), F32),
                jax.ShapeDtypeStruct((chips, fold_rows, head_width), BF16),
            ),
            in_specs=[SMEM, VMEM, VMEM, ANY, VMEM, ANY] + [VMEM] * (len(blocks) - 3) + [ANY],
            out_specs=(VMEM,) * 4,
            scratch_shapes=[
                pltpu.VMEM((2,) + sent.shape, BF16),
                pltpu.SemaphoreType.DMA((2,)),
            ],
            compiler_params=PARAMS,
        )(place, w_query, w_out, all_kv, *blocks)
        query_head = to_head(mine, theirs, core)
        line_queries = jnp.stack(shifted(query_head, "x"))
        input_part, input_post = pl.pallas_call(
            post_kernel,
            out_shape=(
                jax.ShapeDtypeStruct((rows, share), BF16),
                jax.ShapeDtypeStruct((rows, features), F32),
            ),
            in_specs=[VMEM, VMEM, ANY],
            out_specs=(VMEM, VMEM),
            compiler_params=PARAMS,
        )(sent, w_post, query_head)
        own_fold = lax.all_to_all(folded, CHIPS, 0, 0, tiled=True)
        other_fold = swap(own_fold)
    with jax.named_scope("attention"):
        sent = pl.pallas_call(
            forward_kernel,
            out_shape=jax.ShapeDtypeStruct((GROUP, PAIR + STATS, HDIM), BF16),
            in_specs=[SMEM, SMEM, VMEM, VMEM, ANY],
            out_specs=VMEM,
            scratch_shapes=[
                pltpu.VMEM((1, GROUP * PAIR), F32),
                pltpu.VMEM((1, GROUP * PAIR), F32),
                pltpu.VMEM((HDIM, GROUP * PAIR), F32),
            ],
            compiler_params=PARAMS,
        )(doc_lengths, place, line_queries, all_kv, input_post)
        attended_head, log_total = pl.pallas_call(
            merge_kernel,
            out_shape=(
                jax.ShapeDtypeStruct((PAIR, HDIM), BF16),
                jax.ShapeDtypeStruct((1, PAIR), F32),
            ),
            in_specs=[VMEM] * GROUP,
            out_specs=(VMEM, VMEM),
            compiler_params=PARAMS,
        )(*returned(sent, "x"))
        attended = to_rows(attended_head, core)
    with jax.named_scope("raw"):
        sent = pl.pallas_call(
            raw_kernel,
            out_shape=jax.ShapeDtypeStruct((parts, own, features + head_width * parts), BF16),
            in_specs=[SMEM, VMEM, VMEM, VMEM, VMEM, ANY],
            out_specs=VMEM,
            compiler_params=PARAMS,
        )(place, attended, own_fold, other_fold, input_post, targets)
        arrived = lax.all_to_all(sent, "tp", 0, 0, tiled=True)
    with jax.named_scope("norm"):
        back, sent = pl.pallas_call(
            norm_kernel,
            out_shape=(
                jax.ShapeDtypeStruct((rows, head_width), F32),
                jax.ShapeDtypeStruct((parts, own, features + HDIM), BF16),
            ),
            in_specs=[SMEM] + [VMEM] * 6,
            out_specs=(VMEM, VMEM),
            compiler_params=PARAMS,
        )(place, arrived, own_fold, other_fold, attended, cross, input_part)
        arrived = lax.all_to_all(sent, "tp", 0, 0, tiled=True)
    with jax.named_scope("loss"):
        mine, theirs, loss_part = pl.pallas_call(
            functools.partial(loss_kernel, width),
            out_shape=(
                query_shape,
                query_shape,
                jax.ShapeDtypeStruct((1, HDIM), F32),
            ),
            in_specs=[SMEM, SMEM] + [VMEM] * 6,
            out_specs=(VMEM, VMEM, VMEM),
            compiler_params=PARAMS,
        )(doc_lengths, place, steps, arrived, targets, own_fold, other_fold, back)
    with jax.named_scope("sent_grads"):
        grad_head = to_head(mine, theirs, core)
        sent = pl.pallas_call(
            sent_kernel,
            out_shape=jax.ShapeDtypeStruct((PAIR + STATS, HDIM), BF16),
            in_specs=[VMEM] * 4,
            out_specs=VMEM,
            compiler_params=PARAMS,
        )(grad_head, attended_head, log_total, loss_part)
        line_grads = shifted(sent, "x")
    with jax.named_scope("attention_grad"):
        sent = pl.pallas_call(
            backward_kernel,
            out_shape=jax.ShapeDtypeStruct((chips // GROUP, PAIR + STATS, 2 * HDIM), BF16),
            in_specs=[SMEM, SMEM] + [VMEM] * (2 + GROUP),
            out_specs=VMEM,
            compiler_params=PARAMS,
        )(doc_lengths, place, all_kv, line_queries, *line_grads)
        kv_grad, loss_part = pl.pallas_call(
            collect_kernel,
            out_shape=(
                jax.ShapeDtypeStruct((PAIR, 2 * HDIM), BF16),
                jax.ShapeDtypeStruct((1, HDIM), F32),
            ),
            in_specs=[VMEM],
            out_specs=(VMEM, VMEM),
            compiler_params=PARAMS,
        )(lax.all_to_all(sent, "y", 0, 0, tiled=True))
        kv_grad = to_rows(kv_grad, core)
        loss_part = loss_part[0, 0]
        loss = (loss_part + swap(loss_part)) / (seq_total * features)
    with jax.named_scope("d_context"):
        key_terms = pl.pallas_call(
            functools.partial(context_kernel, (0, 2)),
            out_shape=jax.ShapeDtypeStruct((parts, share, rows), F32),
            in_specs=[VMEM, ANY, VMEM],
            out_specs=VMEM,
            compiler_params=PARAMS,
        )(kv_grad, loss.reshape(1, 1), w_key)
        terms = pl.pallas_call(
            functools.partial(context_kernel, (1, 3)),
            out_shape=jax.ShapeDtypeStruct((parts, share, rows), BF16),
            in_specs=[VMEM, VMEM, VMEM],
            out_specs=VMEM,
            compiler_params=PARAMS,
        )(kv_grad, key_terms, w_value)
        d_context = pl.pallas_call(
            total_kernel,
            out_shape=jax.ShapeDtypeStruct((rows, share), BF16),
            in_specs=[VMEM],
            out_specs=VMEM,
            compiler_params=PARAMS,
        )(lax.all_to_all(terms, "tp", 0, 0, tiled=True))
    return d_context, loss


def solution(mesh):
    cores = 2
    count, parts = mesh.devices.shape
    side = math.isqrt(count // cores)
    split = Mesh(mesh.devices.reshape(side, side, cores, parts), ("y", "x", "core", "tp"))
    by_rows = P(ROWS, None)
    by_columns = P(None, "tp")
    return jax.shard_map(
        local,
        mesh=split,
        in_specs=(
            by_rows,
            by_rows,
            P(ROWS),
            P(),
            by_rows,
            P("tp"),
            by_columns,
            by_columns,
            by_columns,
            by_columns,
            P("tp", None),
            P("tp", None),
        ),
        out_specs=(P(ROWS, "tp"), P()),
        check_vma=False,
    )
```
